32 devices in a mesh: dp: 8 (over z, y), mp: 4 (over x, core).
Axes of the slice: x: 2, y: 2, z: 4, core: 2. Of those that a mesh axis runs over, the one named last changes fastest.
Arguments:
- tokens: bfloat16 [8192, 2048], P(('dp', 'mp')), may hold values from -6 to 6
- layer_vectors: bfloat16 [8192, 256], P(('dp', 'mp')), may hold values from -6 to 6
- segment_ids: int32 [8192], P('dp'), may hold values from 0 to 23, as said below
- cotangent: bfloat16 [8192, 2048], P(('dp', 'mp')), may hold values from -6 to 6
- norm_gains: bfloat16 [6, 2048], P(None, ('dp', 'mp')), may hold values from 0.099609375 to 1.8984375
- head_gains: bfloat16 [512], P(('dp', 'mp')), may hold values from 1 to 2
- w_query: bfloat16 [2048, 2048], P('dp', 'mp'), may hold values from -0.125 to 0.125
- w_key: bfloat16 [2048, 512], P(('dp', 'mp')), may hold values from -0.125 to 0.125
- w_value: bfloat16 [2048, 512], P(('dp', 'mp')), may hold values from -0.125 to 0.125
- w_out: bfloat16 [2048, 2048], P('mp', 'dp'), may hold values from -0.125 to 0.125
- w_left: bfloat16 [2048, 64], P(('dp', 'mp')), may hold values from -0.125 to 0.125
- w_right: bfloat16 [64, 2048], P(None, ('dp', 'mp')), may hold values from -0.75 to 0.75
- w_gate: bfloat16 [2048, 8192], P('dp', 'mp'), may hold values from -0.125 to 0.125
- w_up: bfloat16 [2048, 8192], P('dp', 'mp'), may hold values from -0.125 to 0.125
- w_down: bfloat16 [8192, 2048], P('mp', 'dp'), may hold values from -0.0625 to 0.0625
- w_layer_gate: bfloat16 [2048, 256], P(('dp', 'mp')), may hold values from -0.125 to 0.125
- w_layer_proj: bfloat16 [256, 2048], P(None, ('dp', 'mp')), may hold values from -0.375 to 0.375
Outputs:
- output: bfloat16 [8192, 2048], P(('dp', 'mp'))
- grad_tokens: bfloat16 [8192, 2048], P(('dp', 'mp'))
- grad_layer_vectors: bfloat16 [8192, 256], P(('dp', 'mp'))
- grad_norm_gains: float32 [6, 2048], P(None, ('dp', 'mp'))
- grad_head_gains: float32 [512], P(('dp', 'mp'))
- grad_w_query: float32 [2048, 2048], P('dp', 'mp')
- grad_w_key: float32 [2048, 512], P(('dp', 'mp'))
- grad_w_value: float32 [2048, 512], P(('dp', 'mp'))
- grad_w_out: float32 [2048, 2048], P('mp', 'dp')
- grad_w_left: float32 [2048, 64], P(('dp', 'mp'))
- grad_w_right: float32 [64, 2048], P(None, ('dp', 'mp'))
- grad_w_gate: float32 [2048, 8192], P('dp', 'mp')
- grad_w_up: float32 [2048, 8192], P('dp', 'mp')
- grad_w_down: float32 [8192, 2048], P('mp', 'dp')
- grad_w_layer_gate: float32 [2048, 256], P(('dp', 'mp'))
- grad_w_layer_proj: float32 [256, 2048], P(None, ('dp', 'mp'))
The draws below stay inside these ranges and needn't reach their ends.
Inputs may be any that keep to these rules, and one draw needn't show every extreme that they name: `segment_ids`: Sorted; the 1024 tokens of sequence s hold documents 3 s, 3 s + 1 and 3 s + 2 in that order; the first and the last document have 256 - 256 // 4 to 255 tokens each.
All inputs are finite; a program needn't handle non-finite values.
Results may differ from the reference program's by a relative error of at most 0.024.
Values may be sent and summed in bfloat16 or wider, within the bound.
No kernel may reach another device: no remote copies, remote signals or barrier semaphores. Data moves between devices by JAX's collectives and lax.ppermute only.
A program may use at most 192 MiB of HBM per device.

```python
import math
import jax
import jax.numpy as jnp
from jax import lax

D = 2048
FF = 8192
HEADS = 8
KV_HEADS = 2
HEAD_DIM = 256
RANK = 64
LAYER_DIM = 256
WINDOW = 512
TOK_DEV = 256
SEQ = 1024
TOKENS = 8192


def draw_segment_ids(key, part):
    sequences = TOKENS // SEQ
    first_key, second_key = jax.random.split(jax.random.fold_in(key, 11))
    first_cut = jax.random.randint(first_key, (sequences, 1), TOK_DEV - TOK_DEV // 4, TOK_DEV)
    second_cut = jax.random.randint(second_key, (sequences, 1), SEQ - TOK_DEV + 1, SEQ - TOK_DEV + TOK_DEV // 4 + 1)
    places = jnp.arange(SEQ, dtype=jnp.int32)[None, :]
    document = (places >= first_cut).astype(jnp.int32) + (places >= second_cut).astype(jnp.int32)
    offset = 3 * jnp.arange(sequences, dtype=jnp.int32)[:, None]
    return (document + offset).reshape(TOKENS)


def shard_levels(stream_key, dims, shards, low, top_value):
    gain, own = 1.0, jax.random.fold_in(stream_key, 6)
    for dim, blocks in shards:
        heights = jnp.exp(jax.random.uniform(jax.random.fold_in(own, dim), (blocks,), jnp.float32, low / len(shards), top_value / len(shards)))
        gain = gain * jnp.repeat(heights, dims[dim] // blocks).reshape([-1 if axis == dim else 1 for axis in range(len(dims))])
    return gain


def normal_values(own_key, extent, spread, bound, cuts=(), held_as=jnp.bfloat16):
    drawn = jax.random.normal(own_key, extent, jnp.float32) * spread
    if len(cuts) > 0:
        drawn = shard_levels(own_key, extent, cuts, -0.22, 0.18) * drawn
    return jnp.clip(drawn, min=-bound, max=bound).astype(held_as)


def setup_inputs(seed: int = 0) -> dict:
    streams_of = jax.random.split(jax.random.key(seed), 18)
    tokens = normal_values(streams_of[0], (TOKENS, D), 1.0, 6.0, ((0, 32),))
    layer_vectors = normal_values(streams_of[1], (TOKENS, LAYER_DIM), 1.0, 6.0, ((0, 32),))
    segment_ids = draw_segment_ids(jax.random.fold_in(streams_of[17], 71), 0)
    cotangent = normal_values(streams_of[3], (TOKENS, D), 1.0, 6.0, ((0, 32),))
    norm_gains = jnp.clip(1.0 + 0.18 * jax.random.normal(streams_of[4], (6, D), jnp.float32), 0.099609375, 1.8984375).astype(jnp.bfloat16)
    head_gains = jnp.clip(1.0 + 1.0 * jax.random.uniform(streams_of[5], (2 * HEAD_DIM,), jnp.float32) ** shard_levels(streams_of[5], (2 * HEAD_DIM,), ((0, 32),), -0.2, 0.2), 1.0, 2.0).astype(jnp.bfloat16)
    w_query = normal_values(streams_of[6], (D, HEADS * HEAD_DIM), D ** -0.5, 0.125, ((0, 8), (1, 4)))
    w_key = normal_values(streams_of[7], (D, KV_HEADS * HEAD_DIM), D ** -0.5, 0.125, ((0, 32),))
    w_value = normal_values(streams_of[8], (D, KV_HEADS * HEAD_DIM), D ** -0.5, 0.125, ((0, 32),))
    w_out = normal_values(streams_of[9], (HEADS * HEAD_DIM, D), (HEADS * HEAD_DIM) ** -0.5, 0.125, ((0, 4), (1, 8)))
    w_left = normal_values(streams_of[10], (D, RANK), D ** -0.5, 0.125, ((0, 32),))
    w_right = normal_values(streams_of[11], (RANK, D), RANK ** -0.5, 0.75, ((1, 32),))
    w_gate = normal_values(streams_of[12], (D, FF), D ** -0.5, 0.125, ((0, 8), (1, 4)))
    w_up = normal_values(streams_of[13], (D, FF), D ** -0.5, 0.125, ((0, 8), (1, 4)))
    w_down = normal_values(streams_of[14], (FF, D), FF ** -0.5, 0.0625, ((0, 4), (1, 8)))
    w_layer_gate = normal_values(streams_of[15], (D, LAYER_DIM), D ** -0.5, 0.125, ((0, 32),))
    w_layer_proj = normal_values(streams_of[16], (LAYER_DIM, D), LAYER_DIM ** -0.5, 0.375, ((1, 32),))
    return dict(tokens=tokens, layer_vectors=layer_vectors, segment_ids=segment_ids, cotangent=cotangent, norm_gains=norm_gains, head_gains=head_gains, w_query=w_query, w_key=w_key, w_value=w_value, w_out=w_out, w_left=w_left, w_right=w_right, w_gate=w_gate, w_up=w_up, w_down=w_down, w_layer_gate=w_layer_gate, w_layer_proj=w_layer_proj)


@jax.custom_vjp
def low(v):
    return lax.optimization_barrier(v.astype(jnp.bfloat16)).astype(jnp.float32)

@jax.custom_vjp
def low_back(v):
    return v

def low_keep(v):
    return (low(v), None)

def low_pass(kept, grad):
    return (grad,)

def back_keep(v):
    return (v, None)

def back_low(kept, grad):
    return (low(grad),)
low.defvjp(low_keep, low_pass)
low_back.defvjp(back_keep, back_low)
epsilon = 1e-06
highest = lax.Precision.HIGHEST
masked_score = -1e+30

def rms_norm(values, scales):
    return values * lax.rsqrt(lax.optimization_barrier(jnp.mean(values * values, axis=-1, keepdims=True)) + epsilon) * scales

def plain_norm(values):
    return values * lax.rsqrt(lax.optimization_barrier(jnp.mean(values * values, axis=-1, keepdims=True)) + epsilon)

def matmul(left, right):
    return jnp.dot(left, right, precision=highest, preferred_element_type=jnp.float32)

def positions_of(segments):
    length = segments.shape[0]
    places = jnp.arange(length, dtype=jnp.int32)
    fresh = jnp.concatenate([jnp.ones((1,), dtype=bool), segments[1:] != segments[:-1]])
    starts = lax.cummax(jnp.where(fresh, places, 0), axis=0)
    return places - starts

def rotary_tables(positions, head_size):
    half = head_size // 2
    frequency = jnp.exp(jnp.arange(half, dtype=jnp.float32) * (-2.0 * math.log(10000.0) / head_size))
    angle = positions.astype(jnp.float32)[:, None] * frequency[None, :]
    return (jnp.cos(angle)[:, None, :], jnp.sin(angle)[:, None, :])

def rotate(values, cosine, sine):
    half = values.shape[-1] // 2
    first = values[..., :half]
    second = values[..., half:]
    return jnp.concatenate([first * cosine - second * sine, second * cosine + first * sine], axis=-1)

def attend_block(pieces):
    query, key, values, row_segments, col_segments = pieces
    scale = HEAD_DIM ** (-0.5)
    scores = low_back(scale * jnp.einsum('rkgd,ckd->kgrc', query, key, precision=highest))
    row_place = jnp.arange(WINDOW)[:, None]
    col_place = jnp.arange(2 * WINDOW)[None, :]
    allowed = (col_place > row_place) & (col_place <= row_place + WINDOW) & (row_segments[:, None] == col_segments[None, :])
    scores = jnp.where(allowed[None, None], scores, masked_score)
    weights = low(jax.nn.softmax(scores, axis=-1))
    return jnp.einsum('kgrc,ckd->rkgd', weights, values, precision=highest)

def pair_blocks(padded, blocks):
    shaped = padded.reshape((blocks + 1, WINDOW) + padded.shape[1:])
    return jnp.concatenate([shaped[:-1], shaped[1:]], axis=1)

def layer(inputs, vectors, params, segments):
    norm_gains, head_gains, w_query, w_key, w_value, w_out, w_left, w_right, w_gate, w_up, w_down, w_layer_gate, w_layer_proj = params
    length = inputs.shape[0]
    group = HEADS // KV_HEADS
    blocks = length // WINDOW
    normed = rms_norm(inputs, norm_gains[0])
    normed_low = low(normed)
    query_raw = low_back(matmul(normed_low, w_query)).reshape(length, HEADS, HEAD_DIM)
    key_raw = low_back(matmul(normed_low, w_key)).reshape(length, KV_HEADS, HEAD_DIM)
    value_raw = low_back(matmul(normed_low, w_value)).reshape(length, KV_HEADS, HEAD_DIM)
    cosine, sine = rotary_tables(positions_of(segments), HEAD_DIM)
    query = low(rotate(rms_norm(query_raw, head_gains[:HEAD_DIM]), cosine, sine))
    key = low(rotate(rms_norm(key_raw, head_gains[HEAD_DIM:]), cosine, sine))
    values = low(plain_norm(value_raw))
    query_blocks = query.reshape(blocks, WINDOW, KV_HEADS, group, HEAD_DIM)
    zero_rows = jnp.zeros((WINDOW, KV_HEADS, HEAD_DIM), jnp.float32)
    key_blocks = pair_blocks(jnp.concatenate([zero_rows, key]), blocks)
    value_blocks = pair_blocks(jnp.concatenate([zero_rows, values]), blocks)
    segment_pad = jnp.concatenate([jnp.full((WINDOW,), -1, jnp.int32), segments.astype(jnp.int32)])
    col_segments = pair_blocks(segment_pad, blocks)
    row_segments = segments.astype(jnp.int32).reshape(blocks, WINDOW)
    attended = lax.map(jax.checkpoint(attend_block), (query_blocks, key_blocks, value_blocks, row_segments, col_segments))
    attended = low(low_back(attended.reshape(length, HEADS * HEAD_DIM)))
    attn = low_back(matmul(attended, w_out))
    after_attn = inputs + rms_norm(attn, norm_gains[1])
    left_low = low(low_back(matmul(normed_low, w_left)))
    laurel_pre = low_back(matmul(left_low, w_right))
    mixed = (after_attn + normed + rms_norm(laurel_pre, norm_gains[2])) * (1.0 / math.sqrt(2.0))
    ff_in = low(rms_norm(mixed, norm_gains[3]))
    gate_pre = low_back(matmul(ff_in, w_gate))
    up_pre = low_back(matmul(ff_in, w_up))
    hidden = low(jax.nn.gelu(gate_pre, approximate=True) * up_pre)
    ff_out = low_back(matmul(hidden, w_down))
    after_ff = mixed + rms_norm(ff_out, norm_gains[4])
    layer_pre = low_back(matmul(low(after_ff), w_layer_gate))
    layer_mix = low(jax.nn.gelu(layer_pre, approximate=True) * vectors)
    layer_out = low_back(matmul(layer_mix, w_layer_proj))
    return after_ff + rms_norm(layer_out, norm_gains[5])

def reference(tokens, layer_vectors, segment_ids, cotangent, norm_gains, head_gains, w_query, w_key, w_value, w_out, w_left, w_right, w_gate, w_up, w_down, w_layer_gate, w_layer_proj):
    params = tuple((weight.astype(jnp.float32) for weight in (norm_gains, head_gains, w_query, w_key, w_value, w_out, w_left, w_right, w_gate, w_up, w_down, w_layer_gate, w_layer_proj)))
    sequences = TOKENS // SEQ
    token_rows = tokens.astype(jnp.float32).reshape(sequences, SEQ, D)
    vector_rows = layer_vectors.astype(jnp.float32).reshape(sequences, SEQ, LAYER_DIM)
    segment_rows = segment_ids.reshape(sequences, SEQ)
    cotangent_rows = cotangent.astype(jnp.float32).reshape(sequences, SEQ, D)

    def one_sequence(totals, pieces):
        token_row, vector_row, segment_row, cotangent_row = pieces

        def forward(token_in, vector_in, weights):
            return layer(token_in, vector_in, weights, segment_row)
        result, pullback = jax.vjp(forward, token_row, vector_row, params)
        grad_row, grad_vector, grad_params = pullback(cotangent_row)
        totals = jax.tree.map(jnp.add, totals, grad_params)
        return (totals, (result.astype(jnp.bfloat16), grad_row.astype(jnp.bfloat16), grad_vector.astype(jnp.bfloat16)))
    zeros = jax.tree.map(jnp.zeros_like, params)
    totals, (results, grad_rows, grad_vectors) = lax.scan(one_sequence, zeros, (token_rows, vector_rows, segment_rows, cotangent_rows))
    return (results.reshape(TOKENS, D), grad_rows.reshape(TOKENS, D), grad_vectors.reshape(TOKENS, LAYER_DIM), totals[0], totals[1], totals[2], totals[3], totals[4], totals[5], totals[6], totals[7], totals[8], totals[9], totals[10], totals[11], totals[12])
```

```python
import math

import jax
import jax.numpy as jnp
from jax import lax
from jax.experimental import pallas as pl
from jax.experimental.pallas import tpu as pltpu
from jax.sharding import PartitionSpec as P

HEAD_DIM = 256
WINDOW = 512

epsilon = 1e-06
root_half = 1.0 / math.sqrt(2.0)
masked_score = -1e30
bf16 = jnp.bfloat16
f32 = jnp.float32


def rms_norm(values, scales):
    return values * lax.rsqrt(jnp.mean(values * values, axis=-1, keepdims=True) + epsilon) * scales


def norm_back(values, scales, upstream):
    _, pullback = jax.vjp(rms_norm, values, scales)
    return pullback(upstream)


def geglu(gate_pre, other):
    return jax.nn.gelu(gate_pre, approximate=True) * other


def product(left, right):
    return jnp.dot(left, right, preferred_element_type=f32)


def product_left(left, right):
    return lax.dot_general(left, right, (((0,), (0,)), ((), ())), preferred_element_type=f32)


def product_right(left, right):
    return lax.dot_general(left, right, (((1,), (1,)), ((), ())), preferred_element_type=f32)


def rotary_tables(segments):
    length = segments.shape[0]
    half = HEAD_DIM // 2
    places = jnp.arange(length, dtype=jnp.int32)
    starts = jnp.sum((segments[None, :] < segments[:, None]).astype(jnp.int32), axis=1)
    frequency = jnp.exp(jnp.arange(half, dtype=f32) * (-2.0 * math.log(10000.0) / HEAD_DIM))
    angle = (places - starts).astype(f32)[:, None] * frequency[None, :]
    return jnp.cos(angle), jnp.sin(angle)


def after(value, *others):
    return lax.optimization_barrier((value, *others))[0]


def core_swap(value):
    return lax.ppermute(value, "mp", [(0, 1), (1, 0), (2, 3), (3, 2)])


def chip_swap(value):
    return lax.ppermute(value, "mp", [(0, 2), (2, 0), (1, 3), (3, 1)])


class Ring:
    def __init__(self):
        self.count = count = lax.axis_size("dp")
        order = [*range(0, count, 2), *reversed(range(1, count, 2))]
        self.ahead = [(order[i], order[(i + 1) % count]) for i in range(count)]
        self.behind = [(b, a) for a, b in self.ahead]
        me = lax.axis_index("dp")
        self.place = jnp.where(me % 2 == 0, me // 2, count - 1 - me // 2)
        self.unrolled = count <= 8

    def member(self, offset):
        place = (self.place + offset) % self.count
        return jnp.where(place < self.count // 2, 2 * place, 2 * (self.count - 1 - place) + 1)

    def up(self, value):
        return lax.ppermute(value, "dp", self.ahead)

    def down(self, value):
        return lax.ppermute(value, "dp", self.behind)

    def gather(self, block, wait=()):
        size, width = block.shape
        if wait:
            block = after(block, *wait)
        if not self.unrolled:
            return lax.all_gather(block, "dp", axis=0, tiled=True), [()] * self.count
        whole = jnp.zeros((size * self.count, width), block.dtype)

        def put(whole, piece, offset, inner=0):
            return lax.dynamic_update_slice(whole, piece, (self.member(offset) * size + inner, 0))

        whole = put(whole, block, 0)
        left = right = block
        hops = []
        for hop in range(1, self.count // 2):
            left, right = self.up(left), self.down(right)
            whole = put(whole, left, -hop)
            whole = put(whole, right, hop)
            hops.append((left, right))
        half = size // 32 * 16
        far = self.count // 2
        left, right = self.up(left[:half]), self.down(right[half:])
        whole = put(whole, left, -far)
        whole = put(whole, right, far, half)
        hops.append((left, right))
        return whole, hops

    def reduce(self, whole, wait=()):
        size = whole.shape[0] // self.count
        if wait:
            whole = after(whole, *wait)
        if not self.unrolled:
            own = lax.psum_scatter(whole, "dp", scatter_dimension=0, tiled=True)
            return own.astype(f32), [()] * self.count

        def take(offset, start=0, stop=size):
            return lax.dynamic_slice_in_dim(
                whole, self.member(offset) * size + start, stop - start, 0
            )

        half = size // 32 * 16
        far = self.count // 2
        left, right = self.up(take(far, 0, half)), self.down(take(far, half, size))
        left = jnp.pad(left, [(0, size - half), (0, 0)])
        right = jnp.pad(right, [(half, 0), (0, 0)])
        hops = [(left, right)]
        for hop in reversed(range(1, far)):
            left = self.up((take(hop).astype(f32) + left).astype(bf16))
            right = self.down((take(-hop).astype(f32) + right).astype(bf16))
            hops.append((left, right))
        return take(0).astype(f32) + left + right, hops


def join(mine, other, swapped, axis):
    return jnp.where(
        swapped,
        jnp.concatenate([other, mine], axis=axis),
        jnp.concatenate([mine, other], axis=axis),
    )


def gather_small(piece, axis):
    me = lax.axis_index("mp")
    piece = join(piece, core_swap(piece), me % 2 == 1, axis)
    piece = join(piece, chip_swap(piece), me // 2 == 1, axis)
    count = lax.axis_size("dp")
    me = lax.axis_index("dp")
    step = 1
    while step < count:
        other = lax.ppermute(piece, "dp", [(i, i ^ step) for i in range(count)])
        piece = join(piece, other, (me // step) % 2 == 1, axis)
        step *= 2
    return piece


def sum_small(value):
    value = value + core_swap(value)
    value = value + chip_swap(value)
    count = lax.axis_size("dp")
    step = 1
    while step < count:
        value = value + lax.ppermute(value, "dp", [(i, i ^ step) for i in range(count)])
        step *= 2
    return value


def gather_slots(piece):
    near = core_swap(piece)
    across = chip_swap(piece)
    return piece, near, across, core_swap(across)


def reduce_slots(partial, pieces=2):
    parts = []
    for i in range(pieces):
        inner = core_swap(partial(3, i, pieces).astype(bf16))
        outer = chip_swap((partial(2, i, pieces) + inner).astype(bf16))
        near = core_swap(partial(1, i, pieces).astype(bf16))
        parts.append((i, near, outer))
    return jnp.concatenate(
        [partial(0, i, pieces) + near + outer for i, near, outer in parts], axis=1
    )


def columns(value, i, pieces):
    width = value.shape[1] // pieces
    return value[:, i * width : (i + 1) * width]


def rows_of(value, i, pieces):
    width = value.shape[0] // pieces
    return value[i * width : (i + 1) * width]


def normalize(raw):
    return raw * lax.rsqrt(jnp.mean(raw * raw, axis=-1, keepdims=True) + epsilon)


def turn(values, cosine, sine):
    half = HEAD_DIM // 2
    first, second = values[:, :half], values[:, half:]
    return jnp.concatenate(
        [first * cosine - second * sine, second * cosine + first * sine], axis=1
    )


def dot(left, right, dims):
    return lax.dot_general(left, right, ((dims[:1], dims[1:]), ((), ())), preferred_element_type=f32)


TILE = 256


def tiles(length):
    return [(i, max(0, i - WINDOW)) for i in range(0, length, TILE)]


def tile_probs(query, key, start, first, rows_ref, cols_ref):
    stop = start + TILE
    scores = dot(query, key, (1, 1)) * HEAD_DIM**-0.5
    row = start + lax.broadcasted_iota(jnp.int32, scores.shape, 0)
    col = first + lax.broadcasted_iota(jnp.int32, scores.shape, 1)
    kept = (col <= row) & (row - col < WINDOW)
    kept &= rows_ref[start:stop, :] == cols_ref[:, first:stop]
    scores = jnp.where(kept, scores, masked_score)
    expo = jnp.exp(scores - jnp.max(scores, axis=-1, keepdims=True))
    return expo / jnp.sum(expo, axis=-1, keepdims=True)


def forward_kernel(raw_ref, cos_ref, sin_ref, rows_ref, cols_ref, gain_ref, out_ref, low_ref):
    length, across = raw_ref.shape
    heads = across // HEAD_DIM - 2
    key_at, value_at = heads * HEAD_DIM, (heads + 1) * HEAD_DIM
    for start in range(0, length, TILE):
        at = slice(start, start + TILE)
        for head in range(heads + 1):
            cols = slice(head * HEAD_DIM, (head + 1) * HEAD_DIM)
            gain = gain_ref[int(head == heads) : int(head == heads) + 1, :]
            turned = turn(normalize(raw_ref[at, cols]) * gain, cos_ref[at, :], sin_ref[at, :])
            low_ref[at, cols] = turned.astype(bf16)
        low_ref[at, value_at:] = normalize(raw_ref[at, value_at:]).astype(bf16)
    for start, first in tiles(length):
        stop = start + TILE
        key = low_ref[first:stop, key_at:value_at]
        value = low_ref[first:stop, value_at:]
        for head in range(heads):
            cols = slice(head * HEAD_DIM, (head + 1) * HEAD_DIM)
            probs = tile_probs(low_ref[start:stop, cols], key, start, first, rows_ref, cols_ref)
            out_ref[start:stop, cols] = dot(probs.astype(bf16), value, (1, 0)).astype(bf16)


def norm_grad(raw, gain, upstream):
    scale = lax.rsqrt(jnp.mean(raw * raw, axis=-1, keepdims=True) + epsilon)
    unit = raw * scale
    inner = upstream * gain
    grad = scale * (inner - unit * jnp.mean(inner * unit, axis=-1, keepdims=True))
    return grad, jnp.sum(upstream * unit, axis=0, keepdims=True)


def backward_kernel(
    raw_ref, low_ref, up_ref, cos_ref, sin_ref, rows_ref, cols_ref, gain_ref, out_ref, gain_out_ref,
    key_sum, value_sum,
):
    length, across = raw_ref.shape
    heads = across // HEAD_DIM - 2
    key_at, value_at = heads * HEAD_DIM, (heads + 1) * HEAD_DIM
    scale = HEAD_DIM**-0.5
    key_sum[...] = jnp.zeros_like(key_sum)
    value_sum[...] = jnp.zeros_like(value_sum)
    query_gain = jnp.zeros((1, HEAD_DIM), f32)
    key_gain = jnp.zeros((1, HEAD_DIM), f32)
    for start, first in tiles(length):
        stop = start + TILE
        at = slice(start, stop)
        key = low_ref[first:stop, key_at:value_at]
        value = low_ref[first:stop, value_at:]
        for head in range(heads):
            cols = slice(head * HEAD_DIM, (head + 1) * HEAD_DIM)
            query = low_ref[at, cols]
            upstream = up_ref[at, cols]
            probs = tile_probs(query, key, start, first, rows_ref, cols_ref)
            grad_probs = dot(upstream, value, (1, 1))
            inner = jnp.sum(probs * grad_probs, axis=-1, keepdims=True)
            grad_scores = (probs * (grad_probs - inner)).astype(bf16)
            value_sum[first:stop, :] += dot(probs.astype(bf16), upstream, (0, 0))
            key_sum[first:stop, :] += dot(grad_scores, query, (0, 0)) * scale
            grad_query = dot(grad_scores, key, (1, 0)) * scale
            grad_query = turn(grad_query, cos_ref[at, :], -sin_ref[at, :])
            grad, gain = norm_grad(raw_ref[at, cols], gain_ref[0:1, :], grad_query)
            out_ref[at, cols] = grad.astype(bf16)
            query_gain += gain
    for start in range(0, length, TILE):
        at = slice(start, start + TILE)
        grad_key = turn(key_sum[at, :], cos_ref[at, :], -sin_ref[at, :])
        grad, gain = norm_grad(raw_ref[at, key_at:value_at], gain_ref[1:2, :], grad_key)
        out_ref[at, key_at:value_at] = grad.astype(bf16)
        key_gain += gain
        grad, _ = norm_grad(raw_ref[at, value_at:], 1.0, value_sum[at, :])
        out_ref[at, value_at:] = grad.astype(bf16)
    gain_out_ref[...] = jnp.concatenate([query_gain, key_gain])


def local_call(kernel, out_shape, flops, inputs, scratch=()):
    size = sum(math.prod(v.shape) * v.dtype.itemsize for v in [*inputs, *jax.tree.leaves(out_shape)])
    vmem = pl.BlockSpec(memory_space=pltpu.VMEM)
    return pl.pallas_call(
        kernel,
        out_shape=out_shape,
        in_specs=[vmem] * len(inputs),
        out_specs=[vmem] * len(out_shape),
        scratch_shapes=list(scratch),
        compiler_params=pltpu.CompilerParams(vmem_limit_bytes=40 * 2**20),
        cost_estimate=pl.CostEstimate(flops=flops, bytes_accessed=size, transcendentals=0),
    )(*inputs)


def attention(raw, cosine, sine, segments, head_scales):
    length, across = raw.shape
    tables = (cosine, sine, segments[:, None], segments[None, :], head_scales)
    heads = across // HEAD_DIM - 2
    return local_call(
        forward_kernel,
        [
            jax.ShapeDtypeStruct((length, heads * HEAD_DIM), bf16),
            jax.ShapeDtypeStruct((length, across), bf16),
        ],
        4 * heads * length * 2 * WINDOW * HEAD_DIM,
        (raw, *tables),
    )


def attention_back(raw, low, upstream, cosine, sine, segments, head_scales):
    length, across = raw.shape
    tables = (cosine, sine, segments[:, None], segments[None, :], head_scales)
    return local_call(
        backward_kernel,
        [jax.ShapeDtypeStruct((length, across), bf16), jax.ShapeDtypeStruct((2, HEAD_DIM), f32)],
        10 * upstream.shape[1] * length * 2 * WINDOW,
        (raw, low, upstream, *tables),
        [pltpu.VMEM((length, HEAD_DIM), f32)] * 2,
    )


def shards(
    tokens,
    layer_vectors,
    segment_ids,
    cotangent,
    norm_gains,
    head_gains,
    w_query,
    w_key,
    w_value,
    w_out,
    w_left,
    w_right,
    w_gate,
    w_up,
    w_down,
    w_layer_gate,
    w_layer_proj,
):
    ring = Ring()
    count = ring.count
    mine = lax.axis_index("mp")
    chip, core = mine // 2, mine % 2
    rows, width = tokens.shape
    length = segment_ids.shape[0]
    share = w_key.shape[0]
    rank = w_left.shape[1]
    layer_dim = w_layer_gate.shape[1]

    heads_part = head_gains.shape[0]
    packed = jnp.concatenate(
        [norm_gains, jnp.pad(head_gains, (0, norm_gains.shape[1] - heads_part))[None]]
    )
    packed = gather_small(packed, 1).astype(f32)
    gains = packed[:6]
    head_scales = packed[6].reshape(-1, norm_gains.shape[1])[:, :heads_part].reshape(2, HEAD_DIM)

    def in_order(slots):
        whole = jnp.zeros((4 * slots[0].shape[0], *slots[0].shape[1:]), slots[0].dtype)
        for slot, piece in enumerate(slots):
            whole = lax.dynamic_update_slice(whole, piece, ((mine ^ slot) * piece.shape[0], 0))
        return whole

    side = HEAD_DIM
    line = w_query.shape[1]
    fold = 2 * rank * share // line
    parts = [
        w_query,
        w_out.T,
        w_key,
        w_value,
        jnp.concatenate([w_layer_gate, w_layer_proj.T], axis=1),
        jnp.concatenate([w_left, w_right.T], axis=1).reshape(fold, line),
    ]
    first, hops = ring.gather(jnp.concatenate(parts))
    gate_up, hops = ring.gather(jnp.concatenate([w_gate, w_up], axis=1), hops[-3])
    down_t, _ = ring.gather(w_down.T, hops[-2])
    first = first.reshape(count, -1, line)
    starts = [sum(p.shape[0] for p in parts[:i]) for i in range(len(parts) + 1)]
    query_weight, out_t, key_part, value_part, layer_part, rank_part = (
        first[:, a:b] for a, b in zip(starts[:-1], starts[1:])
    )
    out_t = out_t.reshape(-1, line)

    def head_columns(value, head):
        return lax.dynamic_slice_in_dim(value, head * side, side, 2)

    def kv_of(head):
        return jnp.concatenate(
            [head_columns(key_part, head), head_columns(value_part, head)], axis=2
        )

    small_part = jnp.concatenate(
        [layer_part, rank_part.reshape(count, share, 2 * rank)], axis=2
    )

    def interleave(own, across):
        both = join(own[:, None], across[:, None], chip == 1, 1)[:, :, None]
        other = core_swap(both)
        return join(both, other, core == 1, 2).reshape(count * 4 * share, -1)

    mixture = interleave(
        jnp.concatenate([kv_of(chip), small_part], axis=2),
        chip_swap(jnp.concatenate([kv_of(1 - chip), small_part], axis=2)),
    )
    qkv_weight = jnp.concatenate(
        [query_weight.reshape(-1, line), mixture[:, : 2 * side]], axis=1
    )
    layer_gate_weight, layer_proj_weight, left_weight, right_weight = jnp.split(
        mixture[:, 2 * side :],
        [layer_dim, 2 * layer_dim, 2 * layer_dim + rank],
        axis=1,
    )

    token_all = in_order(gather_slots(tokens))
    inputs = tokens.astype(f32)
    vectors = layer_vectors.astype(f32)
    normed = rms_norm(inputs, gains[0])
    normed_low = normed.astype(bf16)
    normed_all = rms_norm(token_all.astype(f32), gains[0]).astype(bf16)
    qkv_raw = product(normed_all, qkv_weight)
    cosine, sine = rotary_tables(segment_ids)
    attended_low, qkv_low = attention(qkv_raw, cosine, sine, segment_ids, head_scales)

    def slot_rows(value, slot):
        return lax.dynamic_slice_in_dim(value, (mine ^ slot) * rows, rows, 0)

    attn = reduce_slots(
        lambda slot, i, pieces: product_right(
            slot_rows(attended_low, slot), rows_of(out_t, i, pieces)
        )
    )
    after_attn = inputs + rms_norm(attn, gains[1])
    left_low = product(normed_low, left_weight).astype(bf16)
    laurel_pre = product_right(left_low, right_weight)
    mixed = (after_attn + normed + rms_norm(laurel_pre, gains[2])) * root_half
    ff_in_all = jnp.concatenate(gather_slots(rms_norm(mixed, gains[3]).astype(bf16)))
    hidden_units = w_gate.shape[1]
    gate_pre = product(ff_in_all, gate_up[:, :hidden_units])
    up_pre = product(ff_in_all, gate_up[:, hidden_units:])
    hidden_low = geglu(gate_pre, up_pre).astype(bf16)
    ff_out = reduce_slots(
        lambda slot, i, pieces: product_right(
            rows_of(hidden_low, slot, 4), rows_of(down_t, i, pieces)
        )
    )
    after_ff = mixed + rms_norm(ff_out, gains[4])
    after_ff_low = after_ff.astype(bf16)
    layer_pre = product(after_ff_low, layer_gate_weight)
    layer_mix_low = geglu(layer_pre, vectors).astype(bf16)
    layer_out = product_right(layer_mix_low, layer_proj_weight)
    result = after_ff + rms_norm(layer_out, gains[5])

    upstream = cotangent.astype(f32)
    grad_layer_out, grad_gain_five = norm_back(layer_out, gains[5], upstream)
    grad_layer_out_low = grad_layer_out.astype(bf16)
    grad_layer_proj = product_left(grad_layer_out_low, layer_mix_low)
    grad_mix = product(grad_layer_out_low, layer_proj_weight)
    _, layer_pull = jax.vjp(geglu, layer_pre, vectors)
    grad_layer_pre, grad_vectors = layer_pull(grad_mix)
    grad_layer_pre_low = grad_layer_pre.astype(bf16)
    grad_layer_gate = product_left(after_ff_low, grad_layer_pre_low)
    grad_after_ff = upstream + product_right(grad_layer_pre_low, layer_gate_weight)
    grad_ff_out, grad_gain_four = norm_back(ff_out, gains[4], grad_after_ff)
    grad_ff_all = jnp.concatenate(gather_slots(grad_ff_out.astype(bf16)))
    grad_down_t, hops = ring.reduce(product_left(grad_ff_all, hidden_low).astype(bf16))
    grad_hidden = product(grad_ff_all, down_t)
    _, ff_pull = jax.vjp(geglu, gate_pre, up_pre)
    grad_gate, grad_up = ff_pull(grad_hidden)
    grad_gate_low = grad_gate.astype(bf16)
    grad_up_low = grad_up.astype(bf16)
    grad_gate_weight, gate_hops = ring.reduce(
        product_left(ff_in_all, grad_gate_low).astype(bf16), hops[-2]
    )
    grad_up_weight, up_hops = ring.reduce(
        product_left(ff_in_all, grad_up_low).astype(bf16), hops[-2]
    )
    grad_ff_in = reduce_slots(
        lambda slot, i, pieces: product_right(
            rows_of(grad_gate_low, slot, 4), rows_of(gate_up, i, pieces)[:, :hidden_units]
        )
        + product_right(
            rows_of(grad_up_low, slot, 4), rows_of(gate_up, i, pieces)[:, hidden_units:]
        )
    )
    grad_mixed_norm, grad_gain_three = norm_back(mixed, gains[3], grad_ff_in)
    grad_branch = (grad_after_ff + grad_mixed_norm) * root_half
    grad_laurel, grad_gain_two = norm_back(laurel_pre, gains[2], grad_branch)
    grad_laurel_low = grad_laurel.astype(bf16)
    grad_right = product_left(grad_laurel_low, left_low)
    grad_left_low = product(grad_laurel_low, right_weight).astype(bf16)
    grad_left = product_left(normed_low, grad_left_low)
    grad_attn, grad_gain_one = norm_back(attn, gains[1], grad_branch)
    grad_attn_all = in_order(gather_slots(grad_attn.astype(bf16)))
    grad_attended_low = product(grad_attn_all, out_t).astype(bf16)
    grad_qkv_low, head_grads = attention_back(
        qkv_raw, qkv_low, grad_attended_low, cosine, sine, segment_ids, head_scales
    )

    def pick(value, index, axis):
        return lax.dynamic_index_in_dim(value, index, axis, keepdims=False)

    small_partial = jnp.concatenate(
        [grad_layer_gate, grad_layer_proj, grad_left, grad_right], axis=1
    ).astype(bf16)
    small_partial = small_partial.reshape(count, 2, 2, share, -1)
    small_sum = pick(small_partial, core, 2).astype(f32) + core_swap(
        pick(small_partial, 1 - core, 2)
    )
    small_sum = pick(small_sum, chip, 1) + chip_swap(pick(small_sum, 1 - chip, 1).astype(bf16))
    small_sum = small_sum.astype(bf16)
    out_grad = product_left(grad_attn_all, attended_low).astype(bf16)
    second = jnp.concatenate(
        [
            out_grad.reshape(count, -1, line),
            small_sum[:, :, : 2 * layer_dim],
            small_sum[:, :, 2 * layer_dim :].reshape(count, fold, line),
        ],
        axis=1,
    )
    second, hops = ring.reduce(second.reshape(-1, line), gate_hops[-2] + up_hops[-2])
    out_rows = width // count
    grad_out = second[:out_rows].T
    grad_layer_gate_weight = second[out_rows : out_rows + share, :layer_dim]
    grad_layer_proj_weight = second[out_rows : out_rows + share, layer_dim:].T
    grad_rank = second[out_rows + share :].reshape(share, 2 * rank)
    grad_left_weight = grad_rank[:, :rank]
    grad_right_weight = grad_rank[:, rank:].T

    qkv_grad = product_left(normed_all, grad_qkv_low).astype(bf16)
    kv_partial = qkv_grad[:, line:].reshape(count, 2, 2, share, 2 * side)
    kv_sum = pick(kv_partial, core, 2).astype(f32) + core_swap(pick(kv_partial, 1 - core, 2))
    third = jnp.concatenate(
        [
            qkv_grad[:, :line].reshape(count, -1, line),
            kv_sum.astype(bf16).reshape(count, 2 * share, 2 * side),
        ],
        axis=1,
    )
    third, _ = ring.reduce(third.reshape(-1, line), hops[-2])
    grad_query_weight = third[:out_rows]
    kv_sum = third[out_rows:].reshape(2, share, 2 * side)
    kv_mine = pick(kv_sum, chip, 0)
    kv_other = chip_swap(pick(kv_sum, 1 - chip, 0).astype(bf16)).astype(f32)
    grad_key_weight = join(kv_mine[:, :side], kv_other[:, :side], chip == 1, 1)
    grad_value_weight = join(kv_mine[:, side:], kv_other[:, side:], chip == 1, 1)

    grad_normed_heads = reduce_slots(
        lambda slot, i, pieces: product_right(
            slot_rows(grad_qkv_low, slot), rows_of(qkv_weight, i, pieces)
        )
    )
    grad_normed = grad_branch + product_right(grad_left_low, left_weight) + grad_normed_heads
    grad_inputs_norm, grad_gain_zero = norm_back(inputs, gains[0], grad_normed)
    grad_inputs = grad_branch + grad_inputs_norm
    head_grads = head_grads.reshape(-1)
    gain_grads = jnp.stack(
        [
            grad_gain_zero,
            grad_gain_one,
            grad_gain_two,
            grad_gain_three,
            grad_gain_four,
            grad_gain_five,
            jnp.pad(head_grads, (0, width - head_grads.shape[0])),
        ]
    )
    gain_grads = sum_small(gain_grads)
    device = lax.axis_index("dp") * 4 + mine
    part = norm_gains.shape[1]
    grad_norm_gains = lax.dynamic_slice_in_dim(gain_grads[:6], device * part, part, 1)
    grad_head_gains = lax.dynamic_slice_in_dim(gain_grads[6], device * heads_part, heads_part, 0)
    return (
        result.astype(bf16),
        grad_inputs.astype(bf16),
        grad_vectors.astype(bf16),
        grad_norm_gains,
        grad_head_gains,
        grad_query_weight,
        grad_key_weight,
        grad_value_weight,
        grad_out,
        grad_left_weight,
        grad_right_weight,
        grad_gate_weight,
        grad_up_weight,
        grad_down_t.T,
        grad_layer_gate_weight,
        grad_layer_proj_weight,
    )


def solution(mesh):
    both = ("dp", "mp")
    in_specs = (
        P(both, None),
        P(both, None),
        P("dp"),
        P(both, None),
        P(None, both),
        P(both),
        P("dp", "mp"),
        P(both, None),
        P(both, None),
        P("mp", "dp"),
        P(both, None),
        P(None, both),
        P("dp", "mp"),
        P("dp", "mp"),
        P("mp", "dp"),
        P(both, None),
        P(None, both),
    )
    out_specs = (
        P(both, None),
        P(both, None),
        P(both, None),
        P(None, both),
        P(both),
        P("dp", "mp"),
        P(both, None),
        P(both, None),
        P("mp", "dp"),
        P(both, None),
        P(None, both),
        P("dp", "mp"),
        P("dp", "mp"),
        P("mp", "dp"),
        P(both, None),
        P(None, both),
    )
    return jax.shard_map(shards, mesh=mesh, in_specs=in_specs, out_specs=out_specs, check_vma=False)
```

```python
import math

import jax
import jax.numpy as jnp
from jax import lax
from jax.experimental import pallas as pl
from jax.experimental.pallas import tpu as pltpu
from jax.sharding import PartitionSpec as P

HEAD_DIM = 256
WINDOW = 512

epsilon = 1e-06
root_half = 1.0 / math.sqrt(2.0)
masked_score = -1e30
bf16 = jnp.bfloat16
f32 = jnp.float32


light = pl.CostEstimate(flops=1, bytes_accessed=1, transcendentals=0)


def rms_norm(values, scales):
    return values * lax.rsqrt(jnp.mean(values * values, axis=-1, keepdims=True) + epsilon) * scales


def norm_back(values, scales, upstream):
    _, pullback = jax.vjp(rms_norm, values, scales)
    return pullback(upstream)


def geglu(gate_pre, other):
    return jax.nn.gelu(gate_pre, approximate=True) * other


def product(left, right):
    return jnp.dot(left, right, preferred_element_type=f32)


def product_left(left, right):
    return lax.dot_general(left, right, (((0,), (0,)), ((), ())), preferred_element_type=f32)


def product_right(left, right):
    return lax.dot_general(left, right, (((1,), (1,)), ((), ())), preferred_element_type=f32)


def rotary_tables(segments):
    length = segments.shape[0]
    half = HEAD_DIM // 2
    places = jnp.arange(length, dtype=jnp.int32)
    starts = jnp.sum((segments[None, :] < segments[:, None]).astype(jnp.int32), axis=1)
    frequency = jnp.exp(jnp.arange(half, dtype=f32) * (-2.0 * math.log(10000.0) / HEAD_DIM))
    angle = (places - starts).astype(f32)[:, None] * frequency[None, :]
    return jnp.cos(angle), jnp.sin(angle)


def sync(value):
    return lax.optimization_barrier(value)


def core_swap(value):
    return lax.ppermute(value, "mp", [(0, 1), (1, 0), (2, 3), (3, 2)])


def chip_swap(value):
    return lax.ppermute(value, "mp", [(0, 2), (2, 0), (1, 3), (3, 1)])


class Ring:
    def __init__(self):
        self.count = count = lax.axis_size("dp")
        order = [*range(0, count, 2), *reversed(range(1, count, 2))]
        self.ahead = [(order[i], order[(i + 1) % count]) for i in range(count)]
        self.behind = [(b, a) for a, b in self.ahead]
        me = lax.axis_index("dp")
        self.place = jnp.where(me % 2 == 0, me // 2, count - 1 - me // 2)
        self.unrolled = count <= 8

    def member(self, offset):
        place = (self.place + offset) % self.count
        return jnp.where(place < self.count // 2, 2 * place, 2 * (self.count - 1 - place) + 1)

    def up(self, value):
        return lax.ppermute(value, "dp", self.ahead)

    def down(self, value):
        return lax.ppermute(value, "dp", self.behind)

    def gather(self, block):
        return Gather(self, block)

    def reduce(self, whole=None, far=None):
        return Reduce(self, whole, far)


class Gather:
    def __init__(self, ring, block):
        self.ring, self.size, self.hop = ring, block.shape[0], 0
        self.left = self.right = block
        self.came = [(block,)]
        self.hops = ring.count // 2 if ring.unrolled else 1
        if ring.unrolled:
            whole = jnp.zeros((self.size * ring.count, block.shape[1]), block.dtype)
            self.whole = self.put(whole, block, 0)

    def put(self, whole, piece, offset, inner=0):
        start = self.ring.member(offset) * self.size + inner
        return lax.dynamic_update_slice(whole, piece, (start, 0))

    def ended(self):
        return self.hop == self.hops

    def step(self):
        if not self.ring.unrolled:
            self.hop += 1
            return lax.all_gather(self.left, "dp", axis=0, tiled=True)
        self.hop += 1
        left, right = self.left, self.right
        if self.hop == self.hops:
            half = self.size // 32 * 16
            left, right = left[:half], right[half:]
        return self.ring.up(left), self.ring.down(right)

    def upcoming(self):
        return ()

    def accept(self, pieces, later=()):
        if not self.ring.unrolled:
            self.whole = pieces
            return
        self.left, self.right = pieces
        self.came.append(pieces)
        inner = self.left.shape[0] if self.hop == self.hops else 0
        self.whole = self.put(self.whole, self.left, -self.hop)
        self.whole = self.put(self.whole, self.right, self.hop, inner)


def hop_kernel(ahead_ref, behind_ref, left_ref, right_ref, up_ref, down_ref):
    size, some = ahead_ref.shape[0], left_ref.shape[0]
    up_ref[:some] = (ahead_ref[:some].astype(f32) + left_ref[...].astype(f32)).astype(bf16)
    if some < size:
        up_ref[some:] = ahead_ref[some:]
    rest = size - right_ref.shape[0]
    down_ref[rest:] = (behind_ref[rest:].astype(f32) + right_ref[...].astype(f32)).astype(bf16)
    if rest:
        down_ref[:rest] = behind_ref[:rest]


class Reduce:
    def __init__(self, ring, whole=None, far=None):
        self.ring, self.next, self.far = ring, (), far
        self.hop = self.hops = ring.count // 2 if ring.unrolled else 1
        if whole is not None:
            self.give(sync(whole))

    def give(self, whole):
        self.whole, self.size = whole, whole.shape[0] // self.ring.count
        if not self.ring.unrolled:
            return
        if self.far is None:
            self.far = self.share(self.hops)
        elif self.hop < self.hops:
            self.next = (self.share(self.hop), self.share(-self.hop))

    def share(self, offset):
        at = self.ring.member(offset) * self.size
        return lax.dynamic_slice_in_dim(self.whole, at, self.size, 0)

    def ended(self):
        return self.hop == 0

    def step(self):
        if not self.ring.unrolled:
            return lax.psum_scatter(self.whole, "dp", scatter_dimension=0, tiled=True)
        if self.hop == self.hops:
            half = self.far.shape[0] // 32 * 16
            left, right = self.far[:half], self.far[half:]
        else:
            block = jax.ShapeDtypeStruct(self.next[0].shape, bf16)
            left, right = tiled_call(
                hop_kernel,
                [block] * 2,
                (*self.next, self.left, self.right),
                [pl.BlockSpec(p.shape, lambda i: (0, 0)) for p in (*self.next, self.left, self.right)],
                [pl.BlockSpec(block.shape, lambda i: (0, 0))] * 2,
                1,
            )
        return self.ring.up(left), self.ring.down(right)

    def upcoming(self):
        if not self.ring.unrolled or self.hop - 1 < 0 or not hasattr(self, "whole"):
            return ()
        later = self.hop - 1
        return tuple(self.share(o) for o in ((later, -later) if later else (0,)))

    def accept(self, pieces, later=()):
        self.hop -= 1
        self.next = later
        if not self.ring.unrolled:
            self.left = pieces
        else:
            self.left, self.right = pieces

    def total(self):
        while self.hop > 0:
            pieces = self.step()
            self.accept(pieces, self.upcoming())
        if not self.ring.unrolled:
            return self.left.astype(f32)
        return self.next[0].astype(f32) + self.left.astype(f32) + self.right.astype(f32)


def phase(rings, *values):
    rings = [r for r in rings if not r.ended()]
    pieces, later, values = sync(([r.step() for r in rings], [r.upcoming() for r in rings], values))
    for r, p, n in zip(rings, pieces, later):
        r.accept(p, n)
    return values[0] if len(values) == 1 else values


def join(mine, other, swapped, axis):
    return jnp.where(
        swapped,
        jnp.concatenate([other, mine], axis=axis),
        jnp.concatenate([mine, other], axis=axis),
    )


def gather_chip(piece, axis):
    me = lax.axis_index("mp")
    piece = join(piece, core_swap(piece), me % 2 == 1, axis)
    return join(piece, chip_swap(piece), me // 2 == 1, axis)


def gather_small(piece, axis):
    count = lax.axis_size("dp")
    me = lax.axis_index("dp")
    step = 1
    while step < count:
        other = lax.ppermute(piece, "dp", [(i, i ^ step) for i in range(count)])
        piece = join(piece, other, (me // step) % 2 == 1, axis)
        step *= 2
    return piece


def sum_chip(value):
    value = value + core_swap(value)
    return value + chip_swap(value)


def sum_step(value, step):
    count = lax.axis_size("dp")
    if step >= count:
        return value
    return value + lax.ppermute(value, "dp", [(i, i ^ step) for i in range(count)])


def stack_kernel(*refs):
    *pieces, out_ref = refs
    rows = pieces[0].shape[0]
    for i, piece in enumerate(pieces):
        out_ref[i * rows : (i + 1) * rows] = piece[...]


def stack(*pieces):
    rows, width = pieces[0].shape
    step = width // 4
    return pl.pallas_call(
        stack_kernel,
        out_shape=jax.ShapeDtypeStruct((rows * len(pieces), width), pieces[0].dtype),
        grid=(4,),
        in_specs=[pl.BlockSpec((rows, step), lambda i: (0, i))] * len(pieces),
        out_specs=pl.BlockSpec((rows * len(pieces), step), lambda i: (0, i)),
        compiler_params=pltpu.CompilerParams(vmem_limit_bytes=24 * 2**20),
        cost_estimate=light,
    )(*pieces)


def gather_slots(piece):
    near = core_swap(piece)
    across = chip_swap(piece)
    return stack(piece, near, across, core_swap(across))


def top(value):
    return value[: value.shape[0] // 2]


def bottom(value):
    return value[value.shape[0] // 2 :]


def add_core(value):
    return top(value) + core_swap(bottom(value).astype(bf16))


def cross(far):
    return chip_swap(add_core(far).astype(bf16))


def rows_of(value, i, pieces):
    width = value.shape[0] // pieces
    return value[i * width : (i + 1) * width]


def normalize(raw):
    return raw * lax.rsqrt(jnp.mean(raw * raw, axis=-1, keepdims=True) + epsilon)


def turn(values, cosine, sine):
    half = HEAD_DIM // 2
    first, second = values[:, :half], values[:, half:]
    return jnp.concatenate(
        [first * cosine - second * sine, second * cosine + first * sine], axis=1
    )


def dot(left, right, dims):
    return lax.dot_general(left, right, ((dims[:1], dims[1:]), ((), ())), preferred_element_type=f32)


TILE = 256


def tiles(length):
    return [(i, max(0, i - WINDOW)) for i in range(0, length, TILE)]


def tile_probs(query, key, start, first, rows_ref, cols_ref):
    stop = start + TILE
    scores = dot(query, key, (1, 1)) * HEAD_DIM**-0.5
    row = start + lax.broadcasted_iota(jnp.int32, scores.shape, 0)
    col = first + lax.broadcasted_iota(jnp.int32, scores.shape, 1)
    kept = (col <= row) & (row - col < WINDOW)
    kept &= rows_ref[start:stop, :] == cols_ref[:, first:stop]
    scores = jnp.where(kept, scores, masked_score)
    expo = jnp.exp(scores - jnp.max(scores, axis=-1, keepdims=True))
    return expo / jnp.sum(expo, axis=-1, keepdims=True)


def slot_at(mine_ref, start):
    return pl.ds(pl.multiple_of((mine_ref[0] ^ (start // TILE)) * TILE, TILE), TILE)


def forward_kernel(
    mine_ref, raw_ref, cos_ref, sin_ref, rows_ref, cols_ref, gain_ref, out_ref, low_ref
):
    length, across = raw_ref.shape
    heads = across // HEAD_DIM - 2
    key_at, value_at = heads * HEAD_DIM, (heads + 1) * HEAD_DIM
    for start in range(0, length, TILE):
        at, here = slice(start, start + TILE), slot_at(mine_ref, start)
        for head in range(heads + 1):
            cols = slice(head * HEAD_DIM, (head + 1) * HEAD_DIM)
            gain = gain_ref[int(head == heads) : int(head == heads) + 1, :]
            turned = turn(normalize(raw_ref[here, cols]) * gain, cos_ref[at, :], sin_ref[at, :])
            low_ref[at, cols] = turned.astype(bf16)
        low_ref[at, value_at:] = normalize(raw_ref[here, value_at:]).astype(bf16)
    for start, first in tiles(length):
        stop = start + TILE
        key = low_ref[first:stop, key_at:value_at]
        value = low_ref[first:stop, value_at:]
        for head in range(heads):
            cols = slice(head * HEAD_DIM, (head + 1) * HEAD_DIM)
            probs = tile_probs(low_ref[start:stop, cols], key, start, first, rows_ref, cols_ref)
            attended = dot(probs.astype(bf16), value, (1, 0))
            out_ref[slot_at(mine_ref, start), cols] = attended.astype(bf16)


def norm_grad(raw, gain, upstream):
    scale = lax.rsqrt(jnp.mean(raw * raw, axis=-1, keepdims=True) + epsilon)
    unit = raw * scale
    inner = upstream * gain
    grad = scale * (inner - unit * jnp.mean(inner * unit, axis=-1, keepdims=True))
    return grad, jnp.sum(upstream * unit, axis=0, keepdims=True)


def backward_kernel(
    mine_ref, raw_ref, low_ref, up_ref, cos_ref, sin_ref, rows_ref, cols_ref, gain_ref, out_ref,
    gain_out_ref, key_sum, value_sum,
):
    length, across = raw_ref.shape
    heads = across // HEAD_DIM - 2
    key_at, value_at = heads * HEAD_DIM, (heads + 1) * HEAD_DIM
    scale = HEAD_DIM**-0.5
    key_sum[...] = jnp.zeros_like(key_sum)
    value_sum[...] = jnp.zeros_like(value_sum)
    query_gain = jnp.zeros((1, HEAD_DIM), f32)
    key_gain = jnp.zeros((1, HEAD_DIM), f32)
    for start, first in tiles(length):
        stop = start + TILE
        at, here = slice(start, stop), slot_at(mine_ref, start)
        key = low_ref[first:stop, key_at:value_at]
        value = low_ref[first:stop, value_at:]
        for head in range(heads):
            cols = slice(head * HEAD_DIM, (head + 1) * HEAD_DIM)
            query = low_ref[at, cols]
            upstream = up_ref[here, cols]
            probs = tile_probs(query, key, start, first, rows_ref, cols_ref)
            grad_probs = dot(upstream, value, (1, 1))
            inner = jnp.sum(probs * grad_probs, axis=-1, keepdims=True)
            grad_scores = (probs * (grad_probs - inner)).astype(bf16)
            value_sum[first:stop, :] += dot(probs.astype(bf16), upstream, (0, 0))
            key_sum[first:stop, :] += dot(grad_scores, query, (0, 0)) * scale
            grad_query = dot(grad_scores, key, (1, 0)) * scale
            grad_query = turn(grad_query, cos_ref[at, :], -sin_ref[at, :])
            grad, gain = norm_grad(raw_ref[here, cols], gain_ref[0:1, :], grad_query)
            out_ref[here, cols] = grad.astype(bf16)
            query_gain += gain
    for start in range(0, length, TILE):
        at, here = slice(start, start + TILE), slot_at(mine_ref, start)
        grad_key = turn(key_sum[at, :], cos_ref[at, :], -sin_ref[at, :])
        grad, gain = norm_grad(raw_ref[here, key_at:value_at], gain_ref[1:2, :], grad_key)
        out_ref[here, key_at:value_at] = grad.astype(bf16)
        key_gain += gain
        grad, _ = norm_grad(raw_ref[here, value_at:], 1.0, value_sum[at, :])
        out_ref[here, value_at:] = grad.astype(bf16)
    gain_out_ref[...] = jnp.concatenate([query_gain, key_gain])


def local_call(kernel, out_shape, inputs, scratch=()):
    vmem = pl.BlockSpec(memory_space=pltpu.VMEM)
    return pl.pallas_call(
        kernel,
        out_shape=out_shape,
        in_specs=[pl.BlockSpec(memory_space=pltpu.SMEM)] + [vmem] * (len(inputs) - 1),
        out_specs=[vmem] * len(out_shape),
        scratch_shapes=list(scratch),
        compiler_params=pltpu.CompilerParams(vmem_limit_bytes=40 * 2**20),
        cost_estimate=light,
    )(*inputs)


def attention(mine, raw, cosine, sine, segments, head_scales):
    length, across = raw.shape
    tables = (cosine, sine, segments[:, None], segments[None, :], head_scales)
    heads = across // HEAD_DIM - 2
    return local_call(
        forward_kernel,
        [
            jax.ShapeDtypeStruct((length, heads * HEAD_DIM), bf16),
            jax.ShapeDtypeStruct((length, across), bf16),
        ],
        (mine, raw, *tables),
    )


def attention_back(mine, raw, low, upstream, cosine, sine, segments, head_scales):
    length, across = raw.shape
    tables = (cosine, sine, segments[:, None], segments[None, :], head_scales)
    return local_call(
        backward_kernel,
        [jax.ShapeDtypeStruct((length, across), bf16), jax.ShapeDtypeStruct((2, HEAD_DIM), f32)],
        (mine, raw, low, upstream, *tables),
        [pltpu.VMEM((length, HEAD_DIM), f32)] * 2,
    )


gelu_scale = math.sqrt(2.0 / math.pi)


def feed_forward_kernel(x_ref, gate_ref, up_ref, gate_pre_ref, up_pre_ref, hidden_ref):
    gate_pre = dot(x_ref[...], gate_ref[...], (1, 0))
    up_pre = dot(x_ref[...], up_ref[...], (1, 0))
    gate_pre_ref[...] = gate_pre
    up_pre_ref[...] = up_pre
    bend = jnp.tanh(gelu_scale * (gate_pre + 0.044715 * gate_pre**3))
    hidden_ref[...] = (0.5 * gate_pre * (1.0 + bend) * up_pre).astype(bf16)


def feed_forward_back_kernel(grad_ref, down_ref, gate_ref, up_ref, grad_gate_ref, grad_up_ref):
    grad = dot(grad_ref[...], down_ref[...], (1, 0))
    gate = gate_ref[...]
    bend = jnp.tanh(gelu_scale * (gate + 0.044715 * gate**3))
    slope = gelu_scale * (1.0 + 3.0 * 0.044715 * gate * gate)
    grad_up_ref[...] = (grad * (0.5 * gate * (1.0 + bend))).astype(bf16)
    slope = 0.5 * (1.0 + bend) + 0.5 * gate * (1.0 - bend * bend) * slope
    grad_gate_ref[...] = (grad * up_ref[...] * slope).astype(bf16)


def grad_in_kernel(grad_gate_ref, grad_up_ref, gate_ref, up_ref, out_ref):
    out_ref[...] = dot(grad_gate_ref[...], gate_ref[...], (1, 1)) + dot(
        grad_up_ref[...], up_ref[...], (1, 1)
    )


def tiled_call(kernel, outs, inputs, specs, out_specs, steps):
    return pl.pallas_call(
        kernel,
        out_shape=outs,
        grid=(steps,),
        in_specs=specs,
        out_specs=out_specs,
        compiler_params=pltpu.CompilerParams(vmem_limit_bytes=48 * 2**20),
        cost_estimate=light,
    )(*inputs)


def column_tile(rows):
    return pl.BlockSpec((rows, TILE), lambda i: (0, i))


def feed_forward(x, gate, up, part, before=()):
    tokens, width = x.shape
    units = gate.shape[1]
    steps = units // TILE // 2
    wide = jax.ShapeDtypeStruct((tokens, units), f32)

    def tile(rows):
        return pl.BlockSpec((rows, TILE), lambda i: (0, i + part * steps))

    def kernel(*refs):
        feed_forward_kernel(*refs[:3], *refs[-3:])

    return pl.pallas_call(
        kernel,
        out_shape=[wide, wide, jax.ShapeDtypeStruct((tokens, units), bf16)],
        grid=(steps,),
        in_specs=[
            pl.BlockSpec((tokens, width), lambda i: (0, 0)),
            tile(width),
            tile(width),
            *[pl.BlockSpec(memory_space=pl.ANY)] * len(before),
        ],
        out_specs=[tile(tokens)] * 3,
        input_output_aliases={3 + i: i for i in range(len(before))},
        compiler_params=pltpu.CompilerParams(vmem_limit_bytes=48 * 2**20),
        cost_estimate=light,
    )(x, gate, up, *before)


def pair_grad_kernel(left_ref, gate_ref, up_ref, out_ref):
    left = left_ref[...]
    rows = left.shape[1]
    out_ref[:rows] = dot(left, gate_ref[...], (0, 0)).astype(bf16)
    out_ref[rows:] = dot(left, up_ref[...], (0, 0)).astype(bf16)


def pair_grad(left, grad_gate, grad_up):
    tokens, width = left.shape
    units = grad_gate.shape[1]
    size = width // lax.axis_size("dp")
    tile = max(size, 128)
    whole = pl.BlockSpec((tokens, units), lambda i: (0, 0))
    out = tiled_call(
        pair_grad_kernel,
        [jax.ShapeDtypeStruct((2 * width, units), bf16)],
        (left, grad_gate, grad_up),
        [pl.BlockSpec((tokens, tile), lambda i: (0, i)), whole, whole],
        [pl.BlockSpec((2 * tile, units), lambda i: (i, 0))],
        width // tile,
    )[0]
    if tile == size:
        return out
    out = out.reshape(width // tile, 2, tile // size, size, units)
    return out.transpose(0, 2, 1, 3, 4).reshape(2 * width, units)


def feed_forward_back(grad, down_t, gate_pre, up_pre, far, before=()):
    half, width = grad.shape
    units = down_t.shape[1]

    def kernel(*refs):
        feed_forward_back_kernel(*refs[:4], *refs[-2:])

    return pl.pallas_call(
        kernel,
        out_shape=[jax.ShapeDtypeStruct((2 * half, units), bf16)] * 2,
        grid=(units // TILE,),
        in_specs=[
            pl.BlockSpec((half, width), lambda i: (0, 0)),
            column_tile(width),
            *[pl.BlockSpec((half, TILE), lambda i: (far, i))] * 2,
            *[pl.BlockSpec(memory_space=pl.ANY)] * len(before),
        ],
        out_specs=[pl.BlockSpec((half, TILE), lambda i: (far, i))] * 2,
        input_output_aliases={4 + i: i for i in range(len(before))},
        compiler_params=pltpu.CompilerParams(vmem_limit_bytes=48 * 2**20),
        cost_estimate=light,
    )(grad, down_t, gate_pre, up_pre, *before)


def grad_in(grad_gate, grad_up, gate, up, far):
    tokens, units = grad_gate.shape
    half, width = tokens // 2, gate.shape[0]
    rows = pl.BlockSpec((half, units), lambda i: (far, 0))
    weights = pl.BlockSpec((TILE, units), lambda i: (i, 0))
    return tiled_call(
        grad_in_kernel,
        [jax.ShapeDtypeStruct((half, width), f32)],
        (grad_gate, grad_up, gate, up),
        [rows, rows, weights, weights],
        [column_tile(half)],
        width // TILE,
    )[0]


def place_kernel(members_ref, *refs):
    *inputs, out_ref = refs
    place = 0
    for near, far in zip(inputs[::2], inputs[1::2]):
        for start in range(0, near.shape[1], TILE):
            cols = slice(start, start + TILE)
            at = pl.ds(pl.multiple_of(members_ref[place] * TILE, TILE), TILE)
            out_ref[:, at] = near[:, cols] + far[:, cols].astype(f32)
            place += 1


def place(members, sums, rows, width):
    return local_call(
        place_kernel, [jax.ShapeDtypeStruct((rows, width), f32)], (members, *sums)
    )[0]


def shards(
    tokens,
    layer_vectors,
    segment_ids,
    cotangent,
    norm_gains,
    head_gains,
    w_query,
    w_key,
    w_value,
    w_out,
    w_left,
    w_right,
    w_gate,
    w_up,
    w_down,
    w_layer_gate,
    w_layer_proj,
):
    ring = Ring()
    count = ring.count
    mine = lax.axis_index("mp")
    chip, core = mine // 2, mine % 2
    rows, width = tokens.shape
    length = segment_ids.shape[0]
    share = w_key.shape[0]
    rank = w_left.shape[1]
    layer_dim = w_layer_gate.shape[1]

    heads_part = head_gains.shape[0]
    def pick(value, index, axis):
        return lax.dynamic_index_in_dim(value, index, axis, keepdims=False)

    def small_core(value):
        value = value.reshape(count, 2, 2, share, -1)
        mine_too = core_swap(pick(value, 1 - core, 2))
        return (pick(value, core, 2).astype(f32) + mine_too).astype(bf16)

    def small_chip(value):
        other = chip_swap(pick(value, 1 - chip, 1))
        return (pick(value, chip, 1).astype(f32) + other).astype(bf16)

    side = HEAD_DIM
    line = w_query.shape[1]
    fold = 2 * rank * share // line
    extra = jnp.concatenate(
        [norm_gains, jnp.pad(head_gains, (0, norm_gains.shape[1] - heads_part))[None]]
    )
    extra = gather_chip(jnp.pad(extra, ((0, 8 - extra.shape[0]), (0, 0))), 1)
    gain_columns = extra.shape[1]
    extra = extra.reshape(-1, line)
    gain_rows = extra.shape[0]
    parts = [
        w_query,
        w_out.T,
        w_key,
        w_value,
        jnp.concatenate([w_layer_gate, w_layer_proj.T], axis=1),
        jnp.concatenate([w_left, w_right.T], axis=1).reshape(fold, line),
        jnp.pad(extra, ((0, 16 - gain_rows), (0, 0))),
    ]
    first = ring.gather(jnp.concatenate(parts))
    gate, up, last = (ring.gather(w) for w in (w_gate, w_up, w_down.T))
    inputs = tokens.astype(f32)
    vectors = layer_vectors.astype(f32)
    tokens_near = phase([first], core_swap(tokens))
    tables = phase([first], *rotary_tables(segment_ids))
    cosine, sine = tables
    tokens_far = phase([first], chip_swap(tokens))
    tokens_last = phase([first, gate], core_swap(tokens_far))

    whole = first.whole.reshape(count, -1, line)
    starts = [sum(p.shape[0] for p in parts[:i]) for i in range(len(parts) + 1)]
    query_weight, out_t, key_part, value_part, layer_part, rank_part, extra = (
        whole[:, a:b] for a, b in zip(starts[:-1], starts[1:])
    )
    out_t = out_t.reshape(-1, line)

    def head_columns(value, head):
        return lax.dynamic_slice_in_dim(value, head * side, side, 2)

    def kv_of(head):
        return jnp.concatenate(
            [head_columns(key_part, head), head_columns(value_part, head)], axis=2
        )

    small_part = jnp.concatenate(
        [layer_part, rank_part.reshape(count, share, 2 * rank)], axis=2
    )

    def interleave(own, across):
        both = join(own[:, None], across[:, None], chip == 1, 1)[:, :, None]
        other = core_swap(both)
        return join(both, other, core == 1, 2).reshape(count * 4 * share, -1)

    gains = extra[:, :gain_rows].reshape(count, 8, gain_columns).transpose(1, 0, 2)
    gains = gains.reshape(8, width).astype(f32)
    head_scales = gains[6].reshape(-1, norm_gains.shape[1])[:, :heads_part].reshape(2, HEAD_DIM)
    normed = rms_norm(inputs, gains[0])
    normed_low = normed.astype(bf16)
    normed_all = stack(
        normed_low,
        *(
            rms_norm(t.astype(f32), gains[0]).astype(bf16)
            for t in (tokens_near, tokens_far, tokens_last)
        ),
    )
    normed_all, kv_weight = phase([up], normed_all, chip_swap(kv_of(1 - chip)))
    qkv_weight = jnp.concatenate(
        [query_weight.reshape(-1, line), interleave(kv_of(chip), kv_weight)], axis=1
    )
    qkv_raw = product(normed_all, qkv_weight)
    here = mine.reshape(1)
    attended_low, qkv_low = attention(
        here, qkv_raw, cosine, sine, segment_ids, head_scales
    )
    half = length // 2
    attn_far = product_right(attended_low[half:], out_t)
    attn_far, attended_low, small_part, normed_low, small_all = phase(
        [gate], attn_far, attended_low, small_part, normed_low, chip_swap(small_part)
    )
    attn_near = product_right(attended_low[:half], out_t)
    attn_far, attn_near = phase([up], cross(attn_far), attn_near)
    attn = add_core(attn_near) + attn_far
    small_all = interleave(small_part, small_all)
    layer_gate_weight, layer_proj_weight, left_weight, right_weight = jnp.split(
        small_all, [layer_dim, 2 * layer_dim, 2 * layer_dim + rank], axis=1
    )
    left_low = product(normed_low, left_weight).astype(bf16)
    laurel_pre = product_right(left_low, right_weight)
    after_attn = inputs + rms_norm(attn, gains[1])
    mixed = (after_attn + normed + rms_norm(laurel_pre, gains[2])) * root_half
    ff_in_low = rms_norm(mixed, gains[3]).astype(bf16)
    ff_in_low, mixed, attn, laurel_pre = phase([gate], ff_in_low, mixed, attn, laurel_pre)
    ff_in_near, ff_in_far = phase([up], core_swap(ff_in_low), chip_swap(ff_in_low))
    ff_in_all = stack(ff_in_low, ff_in_near, ff_in_far, core_swap(ff_in_far))
    ff_in_all = phase([gate, up], ff_in_all)
    gate_weight, up_weight = gate.whole, up.whole
    forward, ff_in_all = phase(
        [last], feed_forward(ff_in_all, gate_weight, up_weight, 0), ff_in_all
    )
    forward, ff_in_all = phase(
        [last], feed_forward(ff_in_all, gate_weight, up_weight, 1, forward), ff_in_all
    )
    gate_pre, up_pre, hidden_low = forward
    hidden_near, hidden_far = hidden_low[:half], hidden_low[half:]

    if ring.unrolled:
        early = jnp.concatenate([p for hop in last.came for p in hop])
        early_far, early_near = phase(
            [last], product_right(hidden_far, early), product_right(hidden_near, early)
        )
        early_far, early_near = phase([last], cross(early_far), early_near)
        late = jnp.concatenate([p for hop in last.came[-2:] for p in hop])
        late_far, late_near = sync(
            (cross(product_right(hidden_far, late)), product_right(hidden_near, late))
        )
        offsets = [0]
        for hop in range(1, count // 2):
            offsets += [-hop, hop]
        members = jnp.stack([ring.member(o) for o in [*offsets, count // 2]]).astype(jnp.int32)
        sums = (add_core(early_near), early_far, add_core(late_near), late_far)
        ff_out = place(members, sums, rows, width)
    else:
        late_far = cross(product_right(hidden_far, last.whole))
        ff_out = add_core(product_right(hidden_near, last.whole)) + late_far
    down_t = last.whole
    after_ff = mixed + rms_norm(ff_out, gains[4])
    after_ff_low = after_ff.astype(bf16)
    layer_pre = product(after_ff_low, layer_gate_weight)
    layer_mix_low = geglu(layer_pre, vectors).astype(bf16)
    layer_out = product_right(layer_mix_low, layer_proj_weight)
    result = after_ff + rms_norm(layer_out, gains[5])

    upstream = cotangent.astype(f32)
    grad_layer_out, grad_gain_five = norm_back(layer_out, gains[5], upstream)
    grad_layer_out_low = grad_layer_out.astype(bf16)
    grad_mix = product(grad_layer_out_low, layer_proj_weight)
    _, layer_pull = jax.vjp(geglu, layer_pre, vectors)
    grad_layer_pre, grad_vectors = layer_pull(grad_mix)
    grad_layer_pre_low = grad_layer_pre.astype(bf16)
    grad_after_ff = upstream + product_right(grad_layer_pre_low, layer_gate_weight)
    grad_ff_out, grad_gain_four = norm_back(ff_out, gains[4], grad_after_ff)
    grad_ff_low, layer_mix_low, after_ff_low = sync(
        (grad_ff_out.astype(bf16), layer_mix_low, after_ff_low)
    )
    grad_layer_proj = product_left(grad_layer_out_low, layer_mix_low)
    grad_layer_gate = product_left(after_ff_low, grad_layer_pre_low)
    grad_ff_near = core_swap(grad_ff_low)
    grads_low = feed_forward_back(stack(grad_ff_low, grad_ff_near), down_t, gate_pre, up_pre, 0)
    grad_ff_far, grads_low, grad_ff_near = sync((chip_swap(grad_ff_low), grads_low, grad_ff_near))
    grad_ff_last = core_swap(grad_ff_far)
    grad_ff_all = stack(grad_ff_low, grad_ff_near, grad_ff_far, grad_ff_last)
    block = width // count
    far_columns = lax.dynamic_slice_in_dim(
        grad_ff_all, ring.member(count // 2) * block, block, 1
    )
    far_grad, grad_ff_all = sync(
        (product_left(far_columns, hidden_low).astype(bf16), grad_ff_all)
    )
    down_back = ring.reduce(far=far_grad)
    down_grad = product_left(grad_ff_all, hidden_low).astype(bf16)
    if ring.unrolled:
        down_grad, grad_ff_all = phase([down_back], down_grad, grad_ff_all)
    down_back.give(down_grad)
    grads_low = feed_forward_back(grad_ff_all[half:], down_t, gate_pre, up_pre, 1, grads_low)
    ff_in_far, *grads_low = phase([down_back], grad_in(*grads_low, gate_weight, up_weight, 1), *grads_low)
    ff_in_far, ff_in_near, *grads_low = phase(
        [down_back], cross(ff_in_far), grad_in(*grads_low, gate_weight, up_weight, 0), *grads_low
    )
    grad_ff_in = add_core(ff_in_near) + ff_in_far
    grad_mixed_norm, grad_gain_three = norm_back(mixed, gains[3], grad_ff_in)
    grad_branch = (grad_after_ff + grad_mixed_norm) * root_half
    grad_attn, grad_gain_one = norm_back(attn, gains[1], grad_branch)
    grad_attn_low, grad_branch = sync((grad_attn.astype(bf16), grad_branch))
    grad_attn_far, grad_attn_near, grad_attn_low, grad_branch, both_grad = phase(
        [down_back],
        chip_swap(grad_attn_low),
        core_swap(grad_attn_low),
        grad_attn_low,
        grad_branch,
        pair_grad(ff_in_all, *grads_low),
    )
    both_back = ring.reduce(both_grad)
    grad_attn_all = stack(grad_attn_low, grad_attn_near, grad_attn_far, core_swap(grad_attn_far))
    grad_attended_low = product(grad_attn_all, out_t).astype(bf16)
    grad_qkv_low, head_grads = attention_back(
        here, qkv_raw, qkv_low, grad_attended_low, cosine, sine, segment_ids, head_scales
    )
    normed_far = product_right(grad_qkv_low[half:], qkv_weight)
    normed_far, grad_qkv_low, grad_attn_all, grad_branch = phase(
        [both_back], normed_far, grad_qkv_low, grad_attn_all, grad_branch
    )

    normed_far, grad_qkv_low = sync((add_core(normed_far).astype(bf16), grad_qkv_low))
    normed_far = chip_swap(normed_far)
    qkv_grad = product_left(normed_all, grad_qkv_low).astype(bf16)
    out_grad = product_left(grad_attn_all, attended_low).astype(bf16)
    normed_near = product_right(grad_qkv_low[:half], qkv_weight)
    normed_far, normed_near, qkv_grad, out_grad, kv_grad, grad_branch = phase(
        [both_back],
        normed_far,
        normed_near,
        qkv_grad,
        out_grad,
        small_core(qkv_grad[:, line:]),
        grad_branch,
    )
    grad_laurel, grad_gain_two = norm_back(laurel_pre, gains[2], grad_branch)
    grad_laurel_low = grad_laurel.astype(bf16)
    grad_right = product_left(grad_laurel_low, left_low)
    grad_left_low = product(grad_laurel_low, right_weight).astype(bf16)
    grad_left = product_left(normed_low, grad_left_low)
    small_grad = jnp.concatenate(
        [grad_layer_gate, grad_layer_proj, grad_left, grad_right], axis=1
    ).astype(bf16)
    small_grad = small_chip(small_core(small_grad))
    second = jnp.concatenate(
        [
            qkv_grad[:, :line].reshape(count, -1, line),
            kv_grad.reshape(count, 2 * share, 2 * side),
            out_grad.reshape(count, -1, line),
            small_grad[:, :, : 2 * layer_dim],
            small_grad[:, :, 2 * layer_dim :].reshape(count, fold, line),
        ],
        axis=1,
    )
    second, grad_left_low = phase([both_back], second, grad_left_low)
    second = ring.reduce(second.reshape(-1, line))
    grad_normed_heads = add_core(normed_near) + normed_far
    grad_normed = grad_branch + product_right(grad_left_low, left_weight) + grad_normed_heads
    grad_inputs_norm, grad_gain_zero = norm_back(inputs, gains[0], grad_normed)
    grad_inputs = grad_branch + grad_inputs_norm
    head_grads = head_grads.reshape(-1)
    gain_grads = jnp.stack(
        [
            grad_gain_zero,
            grad_gain_one,
            grad_gain_two,
            grad_gain_three,
            grad_gain_four,
            grad_gain_five,
            jnp.pad(head_grads, (0, width - head_grads.shape[0])),
        ]
    )
    gain_grads, grad_inputs = phase(
        [both_back, second], sum_step(sum_chip(gain_grads), 1), grad_inputs
    )
    both_grad, down_grad, gain_grads = phase(
        [second], both_back.total(), down_back.total().T, sum_step(gain_grads, 2)
    )
    gate_grad, up_grad = jnp.split(both_grad, 2)
    gain_grads = phase([second], sum_step(gain_grads, 4))
    step = 8
    while step < count:
        gain_grads = sum_step(gain_grads, step)
        step *= 2
    device = lax.axis_index("dp") * 4 + mine
    part = norm_gains.shape[1]
    grad_norm_gains = lax.dynamic_slice_in_dim(gain_grads[:6], device * part, part, 1)
    grad_head_gains = lax.dynamic_slice_in_dim(gain_grads[6], device * heads_part, heads_part, 0)

    second = second.total()
    out_rows = width // count
    grad_query_weight, kv_sum, grad_out, grad_layer, grad_rank = jnp.split(
        second,
        [out_rows, out_rows + 2 * share, 2 * out_rows + 2 * share, 2 * out_rows + 3 * share],
    )
    grad_out = grad_out.T
    grad_layer_gate_weight = grad_layer[:, :layer_dim]
    grad_layer_proj_weight = grad_layer[:, layer_dim:].T
    grad_rank = grad_rank.reshape(share, 2 * rank)
    grad_left_weight = grad_rank[:, :rank]
    grad_right_weight = grad_rank[:, rank:].T
    kv_sum = kv_sum.reshape(2, share, 2 * side)
    kv_mine = pick(kv_sum, chip, 0)
    kv_other = chip_swap(pick(kv_sum, 1 - chip, 0).astype(bf16)).astype(f32)
    grad_key_weight = join(kv_mine[:, :side], kv_other[:, :side], chip == 1, 1)
    grad_value_weight = join(kv_mine[:, side:], kv_other[:, side:], chip == 1, 1)
    return (
        result.astype(bf16),
        grad_inputs.astype(bf16),
        grad_vectors.astype(bf16),
        grad_norm_gains,
        grad_head_gains,
        grad_query_weight,
        grad_key_weight,
        grad_value_weight,
        grad_out,
        grad_left_weight,
        grad_right_weight,
        gate_grad,
        up_grad,
        down_grad,
        grad_layer_gate_weight,
        grad_layer_proj_weight,
    )


def solution(mesh):
    both = ("dp", "mp")
    in_specs = (
        P(both, None),
        P(both, None),
        P("dp"),
        P(both, None),
        P(None, both),
        P(both),
        P("dp", "mp"),
        P(both, None),
        P(both, None),
        P("mp", "dp"),
        P(both, None),
        P(None, both),
        P("dp", "mp"),
        P("dp", "mp"),
        P("mp", "dp"),
        P(both, None),
        P(None, both),
    )
    out_specs = (
        P(both, None),
        P(both, None),
        P(both, None),
        P(None, both),
        P(both),
        P("dp", "mp"),
        P(both, None),
        P(both, None),
        P("mp", "dp"),
        P(both, None),
        P(None, both),
        P("dp", "mp"),
        P("dp", "mp"),
        P("mp", "dp"),
        P(both, None),
        P(None, both),
    )
    return jax.shard_map(shards, mesh=mesh, in_specs=in_specs, out_specs=out_specs, check_vma=False)
```

```python
import math

import jax
import jax.numpy as jnp
from jax import lax
from jax.experimental import pallas as pl
from jax.experimental.pallas import tpu as pltpu
from jax.sharding import PartitionSpec as P

HEAD_DIM = 256
WINDOW = 512

epsilon = 1e-06
root_half = 1.0 / math.sqrt(2.0)
masked_score = -1e30
bf16 = jnp.bfloat16
f32 = jnp.float32


light = pl.CostEstimate(flops=1, bytes_accessed=1, transcendentals=0)


def rms_norm(values, scales):
    return values * lax.rsqrt(jnp.mean(values * values, axis=-1, keepdims=True) + epsilon) * scales


def norm_back(values, scales, upstream):
    _, pullback = jax.vjp(rms_norm, values, scales)
    return pullback(upstream)


def geglu(gate_pre, other):
    return jax.nn.gelu(gate_pre, approximate=True) * other


def product(left, right):
    return jnp.dot(left, right, preferred_element_type=f32)


def product_left(left, right):
    return lax.dot_general(left, right, (((0,), (0,)), ((), ())), preferred_element_type=f32)


def product_right(left, right):
    return lax.dot_general(left, right, (((1,), (1,)), ((), ())), preferred_element_type=f32)


def rotary_tables(segments):
    length = segments.shape[0]
    half = HEAD_DIM // 2
    places = jnp.arange(length, dtype=jnp.int32)
    starts = jnp.sum((segments[None, :] < segments[:, None]).astype(jnp.int32), axis=1)
    frequency = jnp.exp(jnp.arange(half, dtype=f32) * (-2.0 * math.log(10000.0) / HEAD_DIM))
    angle = (places - starts).astype(f32)[:, None] * frequency[None, :]
    return jnp.cos(angle), jnp.sin(angle)


def sync(value):
    return lax.optimization_barrier(value)


def core_swap(value):
    return lax.ppermute(value, "mp", [(0, 1), (1, 0), (2, 3), (3, 2)])


def chip_swap(value):
    return lax.ppermute(value, "mp", [(0, 2), (2, 0), (1, 3), (3, 1)])


class Ring:
    def __init__(self):
        self.count = count = lax.axis_size("dp")
        order = [*range(0, count, 2), *reversed(range(1, count, 2))]
        self.ahead = [(order[i], order[(i + 1) % count]) for i in range(count)]
        self.behind = [(b, a) for a, b in self.ahead]
        me = lax.axis_index("dp")
        self.place = jnp.where(me % 2 == 0, me // 2, count - 1 - me // 2)
        self.unrolled = count <= 8

    def member(self, offset):
        place = (self.place + offset) % self.count
        return jnp.where(place < self.count // 2, 2 * place, 2 * (self.count - 1 - place) + 1)

    def up(self, value):
        return lax.ppermute(value, "dp", self.ahead)

    def down(self, value):
        return lax.ppermute(value, "dp", self.behind)

    def gather(self, block):
        return Gather(self, block)

    def reduce(self, whole):
        whole = sync(whole)
        return Reduce(self, slices, (whole,), lambda: whole)


class Gather:
    def __init__(self, ring, block):
        self.ring, self.size, self.hop = ring, block.shape[0], 0
        self.left = self.right = block
        self.came, self.source = [(block,)], ()
        self.hops = ring.count // 2 if ring.unrolled else 1
        if ring.unrolled:
            whole = jnp.zeros((self.size * ring.count, block.shape[1]), block.dtype)
            self.whole = self.put(whole, block, 0)

    def put(self, whole, piece, offset, inner=0):
        start = self.ring.member(offset) * self.size + inner
        return lax.dynamic_update_slice(whole, piece, (start, 0))

    def ended(self):
        return self.hop == self.hops

    def step(self):
        if not self.ring.unrolled:
            self.hop += 1
            return lax.all_gather(self.left, "dp", axis=0, tiled=True)
        self.hop += 1
        left, right = self.left, self.right
        if self.hop == self.hops:
            half = self.size // 32 * 16
            left, right = left[:half], right[half:]
        return self.ring.up(left), self.ring.down(right)

    def upcoming(self):
        return ()

    def accept(self, pieces, later=()):
        if not self.ring.unrolled:
            self.whole = pieces
            return
        self.left, self.right = pieces
        self.came.append(pieces)
        inner = self.left.shape[0] if self.hop == self.hops else 0
        self.whole = self.put(self.whole, self.left, -self.hop)
        self.whole = self.put(self.whole, self.right, self.hop, inner)


def hop_kernel(ahead_ref, behind_ref, left_ref, right_ref, up_ref, down_ref):
    size, some = ahead_ref.shape[0], left_ref.shape[0]
    up_ref[:some] = (ahead_ref[:some].astype(f32) + left_ref[...].astype(f32)).astype(bf16)
    if some < size:
        up_ref[some:] = ahead_ref[some:]
    rest = size - right_ref.shape[0]
    down_ref[rest:] = (behind_ref[rest:].astype(f32) + right_ref[...].astype(f32)).astype(bf16)
    if rest:
        down_ref[:rest] = behind_ref[:rest]


def slices(ring, whole, offsets):
    size = whole.shape[0] // ring.count
    return tuple(
        lax.dynamic_slice_in_dim(whole, ring.member(o) * size, size, 0) for o in offsets
    )


class Reduce:
    def __init__(self, ring, share, source, whole=None, far=None):
        self.ring, self.share, self.source = ring, share, source
        self.hop = self.hops = ring.count // 2 if ring.unrolled else 1
        if not ring.unrolled:
            self.whole, self.far = whole(), ()
        elif far is None:
            (self.far,) = share(ring, *source, (self.hops,))
        else:
            self.far = far

    def ended(self):
        return self.hop == 0

    def step(self):
        if not self.ring.unrolled:
            return lax.psum_scatter(self.whole, "dp", scatter_dimension=0, tiled=True)
        if self.hop == self.hops:
            half = self.far.shape[0] // 32 * 16
            left, right = self.far[:half], self.far[half:]
        else:
            size, width = self.next[0].shape
            step = math.gcd(width, 512)
            inputs = (*self.next, self.left, self.right)
            left, right = tiled_call(
                hop_kernel,
                [jax.ShapeDtypeStruct((size, width), bf16)] * 2,
                inputs,
                [pl.BlockSpec((p.shape[0], step), lambda i: (0, i)) for p in inputs],
                [pl.BlockSpec((size, step), lambda i: (0, i))] * 2,
                width // step,
            )
        return self.ring.up(left), self.ring.down(right)

    def upcoming(self):
        if not self.ring.unrolled:
            return ()
        later = self.hop - 1
        return self.share(self.ring, *self.source, (later, -later) if later else (0,))

    def accept(self, pieces, later=()):
        self.hop -= 1
        self.next = later
        if not self.ring.unrolled:
            self.left = pieces
        else:
            self.left, self.right = pieces

    def total(self):
        while self.hop > 0:
            pieces = self.step()
            self.accept(pieces, self.upcoming())
        if not self.ring.unrolled:
            return self.left.astype(f32)
        return self.next[0].astype(f32) + self.left.astype(f32) + self.right.astype(f32)


def phase(rings, *values):
    rings = [r for r in rings if not r.ended()]
    pieces, later, sources, values = sync(
        ([r.step() for r in rings], [r.upcoming() for r in rings], [r.source for r in rings], values)
    )
    for r, p, n, source in zip(rings, pieces, later, sources):
        r.accept(p, n)
        r.source = source
    return values[0] if len(values) == 1 else values


def join(mine, other, swapped, axis):
    return jnp.where(
        swapped,
        jnp.concatenate([other, mine], axis=axis),
        jnp.concatenate([mine, other], axis=axis),
    )


def gather_chip(piece, axis):
    me = lax.axis_index("mp")
    piece = join(piece, core_swap(piece), me % 2 == 1, axis)
    return join(piece, chip_swap(piece), me // 2 == 1, axis)


def gather_small(piece, axis):
    count = lax.axis_size("dp")
    me = lax.axis_index("dp")
    step = 1
    while step < count:
        other = lax.ppermute(piece, "dp", [(i, i ^ step) for i in range(count)])
        piece = join(piece, other, (me // step) % 2 == 1, axis)
        step *= 2
    return piece


def sum_chip(value):
    value = value + core_swap(value)
    return value + chip_swap(value)


def sum_step(value, step):
    count = lax.axis_size("dp")
    if step >= count:
        return value
    return value + lax.ppermute(value, "dp", [(i, i ^ step) for i in range(count)])


def stack_kernel(*refs):
    *pieces, out_ref = refs
    rows = pieces[0].shape[0]
    for i, piece in enumerate(pieces):
        out_ref[i * rows : (i + 1) * rows] = piece[...]


def stack(*pieces):
    rows, width = pieces[0].shape
    step = width // 4
    return pl.pallas_call(
        stack_kernel,
        out_shape=jax.ShapeDtypeStruct((rows * len(pieces), width), pieces[0].dtype),
        grid=(4,),
        in_specs=[pl.BlockSpec((rows, step), lambda i: (0, i))] * len(pieces),
        out_specs=pl.BlockSpec((rows * len(pieces), step), lambda i: (0, i)),
        compiler_params=pltpu.CompilerParams(vmem_limit_bytes=24 * 2**20),
        cost_estimate=light,
    )(*pieces)


def gather_slots(piece):
    near = core_swap(piece)
    across = chip_swap(piece)
    return stack(piece, near, across, core_swap(across))


def top(value):
    return value[: value.shape[0] // 2]


def bottom(value):
    return value[value.shape[0] // 2 :]


def add_core(value):
    return top(value) + core_swap(bottom(value).astype(bf16))


def cross(far):
    return chip_swap(add_core(far).astype(bf16))


def rows_of(value, i, pieces):
    width = value.shape[0] // pieces
    return value[i * width : (i + 1) * width]


def normalize(raw):
    return raw * lax.rsqrt(jnp.mean(raw * raw, axis=-1, keepdims=True) + epsilon)


def turn(values, cosine, sine):
    half = HEAD_DIM // 2
    first, second = values[:, :half], values[:, half:]
    return jnp.concatenate(
        [first * cosine - second * sine, second * cosine + first * sine], axis=1
    )


def dot(left, right, dims):
    return lax.dot_general(left, right, ((dims[:1], dims[1:]), ((), ())), preferred_element_type=f32)


TILE = 256


def tiles(length):
    return [(i, max(0, i - WINDOW)) for i in range(0, length, TILE)]


def tile_probs(query, key, start, first, rows_ref, cols_ref):
    stop = start + TILE
    scores = dot(query, key, (1, 1)) * HEAD_DIM**-0.5
    row = start + lax.broadcasted_iota(jnp.int32, scores.shape, 0)
    col = first + lax.broadcasted_iota(jnp.int32, scores.shape, 1)
    kept = (col <= row) & (row - col < WINDOW)
    kept &= rows_ref[start:stop, :] == cols_ref[:, first:stop]
    scores = jnp.where(kept, scores, masked_score)
    expo = jnp.exp(scores - jnp.max(scores, axis=-1, keepdims=True))
    return expo / jnp.sum(expo, axis=-1, keepdims=True)


def slot_at(mine_ref, start):
    return pl.ds(pl.multiple_of((mine_ref[0] ^ (start // TILE)) * TILE, TILE), TILE)


def forward_kernel(
    mine_ref, raw_ref, cos_ref, sin_ref, rows_ref, cols_ref, gain_ref, out_ref, low_ref
):
    length, across = raw_ref.shape
    heads = across // HEAD_DIM - 2
    key_at, value_at = heads * HEAD_DIM, (heads + 1) * HEAD_DIM
    for start in range(0, length, TILE):
        at, here = slice(start, start + TILE), slot_at(mine_ref, start)
        for head in range(heads + 1):
            cols = slice(head * HEAD_DIM, (head + 1) * HEAD_DIM)
            gain = gain_ref[int(head == heads) : int(head == heads) + 1, :]
            turned = turn(normalize(raw_ref[here, cols]) * gain, cos_ref[at, :], sin_ref[at, :])
            low_ref[at, cols] = turned.astype(bf16)
        low_ref[at, value_at:] = normalize(raw_ref[here, value_at:]).astype(bf16)
    for start, first in tiles(length):
        stop = start + TILE
        key = low_ref[first:stop, key_at:value_at]
        value = low_ref[first:stop, value_at:]
        for head in range(heads):
            cols = slice(head * HEAD_DIM, (head + 1) * HEAD_DIM)
            probs = tile_probs(low_ref[start:stop, cols], key, start, first, rows_ref, cols_ref)
            attended = dot(probs.astype(bf16), value, (1, 0))
            out_ref[slot_at(mine_ref, start), cols] = attended.astype(bf16)


def norm_grad(raw, gain, upstream):
    scale = lax.rsqrt(jnp.mean(raw * raw, axis=-1, keepdims=True) + epsilon)
    unit = raw * scale
    inner = upstream * gain
    grad = scale * (inner - unit * jnp.mean(inner * unit, axis=-1, keepdims=True))
    return grad, jnp.sum(upstream * unit, axis=0, keepdims=True)


def backward_kernel(
    mine_ref, raw_ref, low_ref, up_ref, cos_ref, sin_ref, rows_ref, cols_ref, gain_ref, out_ref,
    gain_out_ref, key_sum, value_sum,
):
    length, across = raw_ref.shape
    heads = across // HEAD_DIM - 2
    key_at, value_at = heads * HEAD_DIM, (heads + 1) * HEAD_DIM
    scale = HEAD_DIM**-0.5
    key_sum[...] = jnp.zeros_like(key_sum)
    value_sum[...] = jnp.zeros_like(value_sum)
    query_gain = jnp.zeros((1, HEAD_DIM), f32)
    key_gain = jnp.zeros((1, HEAD_DIM), f32)
    for start, first in tiles(length):
        stop = start + TILE
        at, here = slice(start, stop), slot_at(mine_ref, start)
        key = low_ref[first:stop, key_at:value_at]
        value = low_ref[first:stop, value_at:]
        for head in range(heads):
            cols = slice(head * HEAD_DIM, (head + 1) * HEAD_DIM)
            query = low_ref[at, cols]
            upstream = up_ref[here, cols]
            probs = tile_probs(query, key, start, first, rows_ref, cols_ref)
            grad_probs = dot(upstream, value, (1, 1))
            inner = jnp.sum(probs * grad_probs, axis=-1, keepdims=True)
            grad_scores = (probs * (grad_probs - inner)).astype(bf16)
            value_sum[first:stop, :] += dot(probs.astype(bf16), upstream, (0, 0))
            key_sum[first:stop, :] += dot(grad_scores, query, (0, 0)) * scale
            grad_query = dot(grad_scores, key, (1, 0)) * scale
            grad_query = turn(grad_query, cos_ref[at, :], -sin_ref[at, :])
            grad, gain = norm_grad(raw_ref[here, cols], gain_ref[0:1, :], grad_query)
            out_ref[here, cols] = grad.astype(bf16)
            query_gain += gain
    for start in range(0, length, TILE):
        at, here = slice(start, start + TILE), slot_at(mine_ref, start)
        grad_key = turn(key_sum[at, :], cos_ref[at, :], -sin_ref[at, :])
        grad, gain = norm_grad(raw_ref[here, key_at:value_at], gain_ref[1:2, :], grad_key)
        out_ref[here, key_at:value_at] = grad.astype(bf16)
        key_gain += gain
        grad, _ = norm_grad(raw_ref[here, value_at:], 1.0, value_sum[at, :])
        out_ref[here, value_at:] = grad.astype(bf16)
    gain_out_ref[...] = jnp.concatenate([query_gain, key_gain])


def local_call(kernel, out_shape, inputs, scratch=()):
    vmem = pl.BlockSpec(memory_space=pltpu.VMEM)
    return pl.pallas_call(
        kernel,
        out_shape=out_shape,
        in_specs=[pl.BlockSpec(memory_space=pltpu.SMEM)] + [vmem] * (len(inputs) - 1),
        out_specs=[vmem] * len(out_shape),
        scratch_shapes=list(scratch),
        compiler_params=pltpu.CompilerParams(vmem_limit_bytes=40 * 2**20),
        cost_estimate=light,
    )(*inputs)


def attention(mine, raw, cosine, sine, segments, head_scales):
    length, across = raw.shape
    tables = (cosine, sine, segments[:, None], segments[None, :], head_scales)
    heads = across // HEAD_DIM - 2
    return local_call(
        forward_kernel,
        [
            jax.ShapeDtypeStruct((length, heads * HEAD_DIM), bf16),
            jax.ShapeDtypeStruct((length, across), bf16),
        ],
        (mine, raw, *tables),
    )


def attention_back(mine, raw, low, upstream, cosine, sine, segments, head_scales):
    length, across = raw.shape
    tables = (cosine, sine, segments[:, None], segments[None, :], head_scales)
    return local_call(
        backward_kernel,
        [jax.ShapeDtypeStruct((length, across), bf16), jax.ShapeDtypeStruct((2, HEAD_DIM), f32)],
        (mine, raw, low, upstream, *tables),
        [pltpu.VMEM((length, HEAD_DIM), f32)] * 2,
    )


gelu_scale = math.sqrt(2.0 / math.pi)


def feed_forward_kernel(x_ref, gate_ref, up_ref, gate_pre_ref, up_pre_ref, hidden_ref):
    x = x_ref[...]
    gate_pre = dot(x, gate_ref[...].reshape(-1, TILE), (1, 0))
    up_pre = dot(x, up_ref[...].reshape(-1, TILE), (1, 0))
    gate_pre_ref[...] = gate_pre
    up_pre_ref[...] = up_pre
    bend = jnp.tanh(gelu_scale * (gate_pre + 0.044715 * gate_pre**3))
    hidden_ref[...] = (0.5 * gate_pre * (1.0 + bend) * up_pre).astype(bf16)


def feed_forward_back_kernel(grad_ref, down_ref, gate_ref, up_ref, grad_gate_ref, grad_up_ref):
    grad = dot(grad_ref[...], down_ref[...], (1, 0))
    gate = gate_ref[...]
    bend = jnp.tanh(gelu_scale * (gate + 0.044715 * gate**3))
    slope = gelu_scale * (1.0 + 3.0 * 0.044715 * gate * gate)
    grad_up_ref[...] = (grad * (0.5 * gate * (1.0 + bend))).astype(bf16)
    slope = 0.5 * (1.0 + bend) + 0.5 * gate * (1.0 - bend * bend) * slope
    grad_gate_ref[...] = (grad * up_ref[...] * slope).astype(bf16)


def grad_in_kernel(grad_gate_ref, grad_up_ref, pair_ref, out_ref):
    rows = pair_ref.shape[0] // 2
    out_ref[...] = dot(grad_gate_ref[...], pair_ref[:rows], (1, 1)) + dot(
        grad_up_ref[...], pair_ref[rows:], (1, 1)
    )


def tiled_call(kernel, outs, inputs, specs, out_specs, steps):
    return pl.pallas_call(
        kernel,
        out_shape=outs,
        grid=(steps,),
        in_specs=specs,
        out_specs=out_specs,
        compiler_params=pltpu.CompilerParams(vmem_limit_bytes=48 * 2**20),
        cost_estimate=light,
    )(*inputs)


def column_tile(rows):
    return pl.BlockSpec((rows, TILE), lambda i: (0, i))


def feed_forward(x, pair, part, before=()):
    tokens, width = x.shape
    units = pair.shape[1]
    steps = units // TILE // 2
    size = width // lax.axis_size("dp")
    pair = pair.reshape(-1, 2, size, units)
    wide = jax.ShapeDtypeStruct((tokens, units), f32)

    def weight(which):
        return pl.BlockSpec(
            (width // size, None, size, TILE), lambda i: (0, which, 0, i + part * steps)
        )

    def tile(rows):
        return pl.BlockSpec((rows, TILE), lambda i: (0, i + part * steps))

    def kernel(*refs):
        feed_forward_kernel(*refs[:3], *refs[-3:])

    return pl.pallas_call(
        kernel,
        out_shape=[wide, wide, jax.ShapeDtypeStruct((tokens, units), bf16)],
        grid=(steps,),
        in_specs=[
            pl.BlockSpec((tokens, width), lambda i: (0, 0)),
            weight(0),
            weight(1),
            *[pl.BlockSpec(memory_space=pl.ANY)] * len(before),
        ],
        out_specs=[tile(tokens)] * 3,
        input_output_aliases={3 + i: i for i in range(len(before))},
        compiler_params=pltpu.CompilerParams(vmem_limit_bytes=48 * 2**20),
        cost_estimate=light,
    )(x, pair, pair, *before)


def pair_grad_kernel(left_ref, gate_ref, up_ref, out_ref):
    left = left_ref[...]
    rows = left.shape[1]
    out_ref[:rows] = dot(left, gate_ref[...], (0, 0)).astype(bf16)
    out_ref[rows:] = dot(left, up_ref[...], (0, 0)).astype(bf16)


def pair_grad(left, grad_gate, grad_up):
    tokens, width = left.shape
    units = grad_gate.shape[1]
    size = width // lax.axis_size("dp")
    tile = max(size, 128)
    whole = pl.BlockSpec((tokens, units), lambda i: (0, 0))
    out = tiled_call(
        pair_grad_kernel,
        [jax.ShapeDtypeStruct((2 * width, units), bf16)],
        (left, grad_gate, grad_up),
        [pl.BlockSpec((tokens, tile), lambda i: (0, i)), whole, whole],
        [pl.BlockSpec((2 * tile, units), lambda i: (i, 0))],
        width // tile,
    )[0]
    if tile == size:
        return out
    out = out.reshape(width // tile, 2, tile // size, size, units)
    return out.transpose(0, 2, 1, 3, 4).reshape(2 * width, units)


def pair_share_kernel(members_ref, *refs):
    number = (len(refs) - 2) // 2
    gate_ref, up_ref = refs[number : number + 2]
    for left_ref, out_ref in zip(refs[:number], refs[number + 2 :]):
        left = left_ref[...]
        rows = left.shape[1]
        out_ref[:rows] = dot(left, gate_ref[...], (0, 0)).astype(bf16)
        out_ref[rows:] = dot(left, up_ref[...], (0, 0)).astype(bf16)


def pair_share(ring, left, grad_gate, grad_up, offsets):
    tokens, width = left.shape
    units = grad_gate.shape[1]
    size = width // ring.count
    step = units // 2

    def own(k):
        return pl.BlockSpec((tokens, size), lambda j, at: (0, at[k]))

    grads = pl.BlockSpec((tokens, step), lambda j, at: (0, j))
    number = len(offsets)
    return tuple(
        pl.pallas_call(
            pair_share_kernel,
            out_shape=[jax.ShapeDtypeStruct((2 * size, units), bf16)] * number,
            grid_spec=pltpu.PrefetchScalarGridSpec(
                num_scalar_prefetch=1,
                grid=(2,),
                in_specs=[*map(own, range(number)), grads, grads],
                out_specs=[pl.BlockSpec((2 * size, step), lambda j, at: (0, j))] * number,
            ),
            compiler_params=pltpu.CompilerParams(vmem_limit_bytes=40 * 2**20),
            cost_estimate=light,
        )(
            jnp.stack([ring.member(o) for o in offsets]).astype(jnp.int32),
            *[left] * number,
            grad_gate,
            grad_up,
        )
    )


def feed_forward_back(grad, down_t, gate_pre, up_pre, far, before=()):
    half, width = grad.shape
    units = down_t.shape[1]

    def kernel(*refs):
        feed_forward_back_kernel(*refs[:4], *refs[-2:])

    return pl.pallas_call(
        kernel,
        out_shape=[jax.ShapeDtypeStruct((2 * half, units), bf16)] * 2,
        grid=(units // TILE,),
        in_specs=[
            pl.BlockSpec((half, width), lambda i: (0, 0)),
            column_tile(width),
            *[pl.BlockSpec((half, TILE), lambda i: (far, i))] * 2,
            *[pl.BlockSpec(memory_space=pl.ANY)] * len(before),
        ],
        out_specs=[pl.BlockSpec((half, TILE), lambda i: (far, i))] * 2,
        input_output_aliases={4 + i: i for i in range(len(before))},
        compiler_params=pltpu.CompilerParams(vmem_limit_bytes=48 * 2**20),
        cost_estimate=light,
    )(grad, down_t, gate_pre, up_pre, *before)


def grad_in(grad_gate, grad_up, pair, far):
    tokens, units = grad_gate.shape
    half, width = tokens // 2, pair.shape[0] // 2
    size = width // lax.axis_size("dp")
    tile = max(size, 128)
    if tile > size:
        pair = pair.reshape(width // tile, tile // size, 2, size, units)
        pair = pair.transpose(0, 2, 1, 3, 4).reshape(2 * width, units)
    rows = pl.BlockSpec((half, units), lambda i: (far, 0))
    return tiled_call(
        grad_in_kernel,
        [jax.ShapeDtypeStruct((half, width), f32)],
        (grad_gate, grad_up, pair),
        [rows, rows, pl.BlockSpec((2 * tile, units), lambda i: (i, 0))],
        [pl.BlockSpec((half, tile), lambda i: (0, i))],
        width // tile,
    )[0]


def place_kernel(members_ref, *refs):
    *inputs, out_ref = refs
    place = 0
    for near, far in zip(inputs[::2], inputs[1::2]):
        for start in range(0, near.shape[1], TILE):
            cols = slice(start, start + TILE)
            at = pl.ds(pl.multiple_of(members_ref[place] * TILE, TILE), TILE)
            out_ref[:, at] = near[:, cols] + far[:, cols].astype(f32)
            place += 1


def place(members, sums, rows, width):
    return local_call(
        place_kernel, [jax.ShapeDtypeStruct((rows, width), f32)], (members, *sums)
    )[0]


def shards(
    tokens,
    layer_vectors,
    segment_ids,
    cotangent,
    norm_gains,
    head_gains,
    w_query,
    w_key,
    w_value,
    w_out,
    w_left,
    w_right,
    w_gate,
    w_up,
    w_down,
    w_layer_gate,
    w_layer_proj,
):
    ring = Ring()
    count = ring.count
    mine = lax.axis_index("mp")
    chip, core = mine // 2, mine % 2
    rows, width = tokens.shape
    length = segment_ids.shape[0]
    share = w_key.shape[0]
    rank = w_left.shape[1]
    layer_dim = w_layer_gate.shape[1]

    heads_part = head_gains.shape[0]
    def pick(value, index, axis):
        return lax.dynamic_index_in_dim(value, index, axis, keepdims=False)

    def small_core(value):
        value = value.reshape(count, 2, 2, share, -1)
        mine_too = core_swap(pick(value, 1 - core, 2))
        return (pick(value, core, 2).astype(f32) + mine_too).astype(bf16)

    def small_chip(value):
        other = chip_swap(pick(value, 1 - chip, 1))
        return (pick(value, chip, 1).astype(f32) + other).astype(bf16)

    side = HEAD_DIM
    line = w_query.shape[1]
    fold = 2 * rank * share // line
    extra = jnp.concatenate(
        [norm_gains, jnp.pad(head_gains, (0, norm_gains.shape[1] - heads_part))[None]]
    )
    extra = gather_chip(jnp.pad(extra, ((0, 8 - extra.shape[0]), (0, 0))), 1)
    gain_columns = extra.shape[1]
    extra = extra.reshape(-1, line)
    gain_rows = extra.shape[0]
    parts = [
        w_query,
        w_out.T,
        w_key,
        w_value,
        jnp.concatenate([w_layer_gate, w_layer_proj.T], axis=1),
        jnp.concatenate([w_left, w_right.T], axis=1).reshape(fold, line),
        jnp.pad(extra, ((0, 16 - gain_rows), (0, 0))),
    ]
    first = ring.gather(jnp.concatenate(parts))
    pair_block, down_block = stack(w_gate, w_up), w_down.T
    inputs = tokens.astype(f32)
    vectors = layer_vectors.astype(f32)
    tokens_near = phase([first], core_swap(tokens))
    tables = phase([first], *rotary_tables(segment_ids))
    cosine, sine = tables
    tokens_far, pair_block, down_block = phase([first], chip_swap(tokens), pair_block, down_block)
    tokens_last, pair_block = phase([first], core_swap(tokens_far), pair_block)
    both = ring.gather(pair_block)

    whole = first.whole.reshape(count, -1, line)
    starts = [sum(p.shape[0] for p in parts[:i]) for i in range(len(parts) + 1)]
    query_weight, out_t, key_part, value_part, layer_part, rank_part, extra = (
        whole[:, a:b] for a, b in zip(starts[:-1], starts[1:])
    )
    out_t = out_t.reshape(-1, line)

    def head_columns(value, head):
        return lax.dynamic_slice_in_dim(value, head * side, side, 2)

    def kv_of(head):
        return jnp.concatenate(
            [head_columns(key_part, head), head_columns(value_part, head)], axis=2
        )

    small_part = jnp.concatenate(
        [layer_part, rank_part.reshape(count, share, 2 * rank)], axis=2
    )

    def interleave(own, across):
        both = join(own[:, None], across[:, None], chip == 1, 1)[:, :, None]
        other = core_swap(both)
        return join(both, other, core == 1, 2).reshape(count * 4 * share, -1)

    gains = extra[:, :gain_rows].reshape(count, 8, gain_columns).transpose(1, 0, 2)
    gains = gains.reshape(8, width).astype(f32)
    head_scales = gains[6].reshape(-1, norm_gains.shape[1])[:, :heads_part].reshape(2, HEAD_DIM)
    normed = rms_norm(inputs, gains[0])
    normed_low = normed.astype(bf16)
    normed_all = stack(
        normed_low,
        *(
            rms_norm(t.astype(f32), gains[0]).astype(bf16)
            for t in (tokens_near, tokens_far, tokens_last)
        ),
    )
    kv_weight, small_part = sync((chip_swap(kv_of(1 - chip)), small_part))
    qkv_weight = jnp.concatenate(
        [query_weight.reshape(-1, line), interleave(kv_of(chip), kv_weight)], axis=1
    )
    qkv_raw = product(normed_all, qkv_weight)
    here = mine.reshape(1)
    attended_low, qkv_low = attention(
        here, qkv_raw, cosine, sine, segment_ids, head_scales
    )
    half = length // 2
    attn_far = product_right(attended_low[half:], out_t)
    attn_far, attended_low, normed_low, small_all, down_block = phase(
        [both], attn_far, attended_low, normed_low, chip_swap(small_part), down_block
    )
    attn_far, attended_low = sync((add_core(attn_far).astype(bf16), attended_low))
    attn_near = product_right(attended_low[:half], out_t)
    attn = add_core(attn_near) + chip_swap(attn_far)
    small_all = interleave(small_part, small_all)
    layer_gate_weight, layer_proj_weight, left_weight, right_weight = jnp.split(
        small_all, [layer_dim, 2 * layer_dim, 2 * layer_dim + rank], axis=1
    )
    left_low = product(normed_low, left_weight).astype(bf16)
    laurel_pre = product_right(left_low, right_weight)
    after_attn = inputs + rms_norm(attn, gains[1])
    mixed = (after_attn + normed + rms_norm(laurel_pre, gains[2])) * root_half
    ff_in_low = rms_norm(mixed, gains[3]).astype(bf16)
    ff_in_low, mixed, attn, laurel_pre, down_block = phase(
        [both], ff_in_low, mixed, attn, laurel_pre, down_block
    )
    ff_in_near, ff_in_low, mixed = sync((core_swap(ff_in_low), ff_in_low, mixed))
    ff_in_far, down_block = phase([both], chip_swap(ff_in_low), down_block)
    ff_in_all = stack(ff_in_low, ff_in_near, ff_in_far, core_swap(ff_in_far))
    ff_in_all, down_block = phase([both], ff_in_all, down_block)
    pair = both.whole
    last = ring.gather(down_block)
    forward, ff_in_all = phase([last], feed_forward(ff_in_all, pair, 0), ff_in_all)
    forward, ff_in_all = phase([last], feed_forward(ff_in_all, pair, 1, forward), ff_in_all)
    gate_pre, up_pre, hidden_low = forward
    hidden_near, hidden_far = hidden_low[:half], hidden_low[half:]

    if ring.unrolled:
        early = jnp.concatenate([p for hop in last.came for p in hop])
        early_far, early_near = phase(
            [last], product_right(hidden_far, early), product_right(hidden_near, early)
        )
        early_far, early_near = phase([last], cross(early_far), early_near)
        late = jnp.concatenate([p for hop in last.came[-2:] for p in hop])
        late_far, late_near = sync(
            (cross(product_right(hidden_far, late)), product_right(hidden_near, late))
        )
        offsets = [0]
        for hop in range(1, count // 2):
            offsets += [-hop, hop]
        members = jnp.stack([ring.member(o) for o in [*offsets, count // 2]]).astype(jnp.int32)
        sums = (add_core(early_near), early_far, add_core(late_near), late_far)
        ff_out = place(members, sums, rows, width)
    else:
        late_far = cross(product_right(hidden_far, last.whole))
        ff_out = add_core(product_right(hidden_near, last.whole)) + late_far
    down_t = last.whole
    after_ff = mixed + rms_norm(ff_out, gains[4])
    after_ff_low = after_ff.astype(bf16)
    layer_pre = product(after_ff_low, layer_gate_weight)
    layer_mix_low = geglu(layer_pre, vectors).astype(bf16)
    layer_out = product_right(layer_mix_low, layer_proj_weight)
    result = after_ff + rms_norm(layer_out, gains[5])

    upstream = cotangent.astype(f32)
    grad_layer_out, grad_gain_five = norm_back(layer_out, gains[5], upstream)
    grad_layer_out_low = grad_layer_out.astype(bf16)
    grad_mix = product(grad_layer_out_low, layer_proj_weight)
    _, layer_pull = jax.vjp(geglu, layer_pre, vectors)
    grad_layer_pre, grad_vectors = layer_pull(grad_mix)
    grad_layer_pre_low = grad_layer_pre.astype(bf16)
    grad_after_ff = upstream + product_right(grad_layer_pre_low, layer_gate_weight)
    grad_ff_out, grad_gain_four = norm_back(ff_out, gains[4], grad_after_ff)
    grad_ff_low, layer_mix_low, after_ff_low = sync(
        (grad_ff_out.astype(bf16), layer_mix_low, after_ff_low)
    )
    grad_layer_proj = product_left(grad_layer_out_low, layer_mix_low)
    grad_layer_gate = product_left(after_ff_low, grad_layer_pre_low)
    grad_ff_near = core_swap(grad_ff_low)
    grads_low = feed_forward_back(stack(grad_ff_low, grad_ff_near), down_t, gate_pre, up_pre, 0)
    grad_ff_far, grads_low, grad_ff_near = sync((chip_swap(grad_ff_low), grads_low, grad_ff_near))
    grad_ff_last = core_swap(grad_ff_far)
    grad_ff_all = stack(grad_ff_low, grad_ff_near, grad_ff_far, grad_ff_last)
    block = width // count
    far_columns = lax.dynamic_slice_in_dim(
        grad_ff_all, ring.member(count // 2) * block, block, 1
    )
    far_grad, grad_ff_all = sync(
        (product_left(far_columns, hidden_low).astype(bf16), grad_ff_all)
    )
    down_grad = product_left(grad_ff_all, hidden_low).astype(bf16)
    down_back = Reduce(ring, slices, (down_grad,), lambda: down_grad, far_grad)
    grad_ff_all = phase([down_back], grad_ff_all)
    grads_low = feed_forward_back(grad_ff_all[half:], down_t, gate_pre, up_pre, 1, grads_low)
    ff_in_far, *grads_low = phase([down_back], grad_in(*grads_low, pair, 1), *grads_low)
    both_back = Reduce(
        ring, pair_share, (ff_in_all, *grads_low), lambda: pair_grad(ff_in_all, *grads_low)
    )
    ff_in_far, ff_in_near, both_back.far, both_back.source = phase(
        [down_back],
        cross(ff_in_far),
        grad_in(*grads_low, pair, 0),
        both_back.far,
        both_back.source,
    )
    grad_ff_in = add_core(ff_in_near) + ff_in_far
    grad_mixed_norm, grad_gain_three = norm_back(mixed, gains[3], grad_ff_in)
    grad_branch = (grad_after_ff + grad_mixed_norm) * root_half
    grad_attn, grad_gain_one = norm_back(attn, gains[1], grad_branch)
    grad_attn_low, grad_branch = sync((grad_attn.astype(bf16), grad_branch))
    grad_laurel, grad_gain_two = norm_back(laurel_pre, gains[2], grad_branch)
    grad_laurel_low = grad_laurel.astype(bf16)
    grad_right = product_left(grad_laurel_low, left_low)
    grad_left_low = product(grad_laurel_low, right_weight).astype(bf16)
    grad_left = product_left(normed_low, grad_left_low)
    small_grad = jnp.concatenate(
        [grad_layer_gate, grad_layer_proj, grad_left, grad_right], axis=1
    ).astype(bf16)
    grad_attn_far, grad_attn_near, grad_attn_low, grad_branch, small_grad, grad_left_low = phase(
        [down_back, both_back],
        chip_swap(grad_attn_low),
        core_swap(grad_attn_low),
        grad_attn_low,
        grad_branch,
        small_grad,
        grad_left_low,
    )
    grad_attn_all = stack(grad_attn_low, grad_attn_near, grad_attn_far, core_swap(grad_attn_far))
    grad_attended_low = product(grad_attn_all, out_t).astype(bf16)
    grad_qkv_low, head_grads = attention_back(
        here, qkv_raw, qkv_low, grad_attended_low, cosine, sine, segment_ids, head_scales
    )
    normed_far = product_right(grad_qkv_low[half:], qkv_weight)
    normed_far, grad_qkv_low, grad_attn_all, grad_branch, small_grad = phase(
        [both_back],
        normed_far,
        grad_qkv_low,
        grad_attn_all,
        grad_branch,
        small_core(small_grad),
    )

    normed_far, grad_qkv_low = sync((add_core(normed_far).astype(bf16), grad_qkv_low))
    qkv_grad = product_left(normed_all, grad_qkv_low).astype(bf16)
    out_grad = product_left(grad_attn_all, attended_low).astype(bf16)
    kv_grad = small_core(qkv_grad[:, line:])
    small_grad = small_chip(small_grad)
    second = jnp.concatenate(
        [
            qkv_grad[:, :line].reshape(count, -1, line),
            kv_grad.reshape(count, 2 * share, 2 * side),
            out_grad.reshape(count, -1, line),
            small_grad[:, :, : 2 * layer_dim],
            small_grad[:, :, 2 * layer_dim :].reshape(count, fold, line),
        ],
        axis=1,
    )
    normed_far, second, grad_qkv_low, grad_branch = phase(
        [both_back], normed_far, second, grad_qkv_low, grad_branch
    )
    normed_far = chip_swap(normed_far)
    normed_near = product_right(grad_qkv_low[:half], qkv_weight)
    second = ring.reduce(second.reshape(-1, line))
    grad_normed_heads = add_core(normed_near) + normed_far
    grad_normed = grad_branch + product_right(grad_left_low, left_weight) + grad_normed_heads
    grad_inputs_norm, grad_gain_zero = norm_back(inputs, gains[0], grad_normed)
    grad_inputs = grad_branch + grad_inputs_norm
    head_grads = head_grads.reshape(-1)
    gain_grads = jnp.stack(
        [
            grad_gain_zero,
            grad_gain_one,
            grad_gain_two,
            grad_gain_three,
            grad_gain_four,
            grad_gain_five,
            jnp.pad(head_grads, (0, width - head_grads.shape[0])),
        ]
    )
    gain_grads, grad_inputs = phase(
        [both_back, second], sum_step(sum_chip(gain_grads), 1), grad_inputs
    )
    both_grad, down_grad, gain_grads = phase(
        [second], both_back.total(), down_back.total().T, sum_step(gain_grads, 2)
    )
    gate_grad, up_grad = jnp.split(both_grad, 2)
    gain_grads = phase([second], sum_step(gain_grads, 4))
    step = 8
    while step < count:
        gain_grads = sum_step(gain_grads, step)
        step *= 2
    device = lax.axis_index("dp") * 4 + mine
    part = norm_gains.shape[1]
    grad_norm_gains = lax.dynamic_slice_in_dim(gain_grads[:6], device * part, part, 1)
    grad_head_gains = lax.dynamic_slice_in_dim(gain_grads[6], device * heads_part, heads_part, 0)

    second = second.total()
    out_rows = width // count
    grad_query_weight, kv_sum, grad_out, grad_layer, grad_rank = jnp.split(
        second,
        [out_rows, out_rows + 2 * share, 2 * out_rows + 2 * share, 2 * out_rows + 3 * share],
    )
    grad_out = grad_out.T
    grad_layer_gate_weight = grad_layer[:, :layer_dim]
    grad_layer_proj_weight = grad_layer[:, layer_dim:].T
    grad_rank = grad_rank.reshape(share, 2 * rank)
    grad_left_weight = grad_rank[:, :rank]
    grad_right_weight = grad_rank[:, rank:].T
    kv_sum = kv_sum.reshape(2, share, 2 * side)
    kv_mine = pick(kv_sum, chip, 0)
    kv_other = chip_swap(pick(kv_sum, 1 - chip, 0).astype(bf16)).astype(f32)
    grad_key_weight = join(kv_mine[:, :side], kv_other[:, :side], chip == 1, 1)
    grad_value_weight = join(kv_mine[:, side:], kv_other[:, side:], chip == 1, 1)
    return (
        result.astype(bf16),
        grad_inputs.astype(bf16),
        grad_vectors.astype(bf16),
        grad_norm_gains,
        grad_head_gains,
        grad_query_weight,
        grad_key_weight,
        grad_value_weight,
        grad_out,
        grad_left_weight,
        grad_right_weight,
        gate_grad,
        up_grad,
        down_grad,
        grad_layer_gate_weight,
        grad_layer_proj_weight,
    )


def solution(mesh):
    both = ("dp", "mp")
    in_specs = (
        P(both, None),
        P(both, None),
        P("dp"),
        P(both, None),
        P(None, both),
        P(both),
        P("dp", "mp"),
        P(both, None),
        P(both, None),
        P("mp", "dp"),
        P(both, None),
        P(None, both),
        P("dp", "mp"),
        P("dp", "mp"),
        P("mp", "dp"),
        P(both, None),
        P(None, both),
    )
    out_specs = (
        P(both, None),
        P(both, None),
        P(both, None),
        P(None, both),
        P(both),
        P("dp", "mp"),
        P(both, None),
        P(both, None),
        P("mp", "dp"),
        P(both, None),
        P(None, both),
        P("dp", "mp"),
        P("dp", "mp"),
        P("mp", "dp"),
        P(both, None),
        P(None, both),
    )
    return jax.shard_map(shards, mesh=mesh, in_specs=in_specs, out_specs=out_specs, check_vma=False)
```

```python
import math

import jax
import jax.numpy as jnp
from jax import lax
from jax.experimental import pallas as pl
from jax.experimental.pallas import tpu as pltpu
from jax.sharding import PartitionSpec as P

HEAD_DIM = 256
WINDOW = 512

epsilon = 1e-06
root_half = 1.0 / math.sqrt(2.0)
masked_score = -1e30
bf16 = jnp.bfloat16
f32 = jnp.float32


light = pl.CostEstimate(flops=1, bytes_accessed=1, transcendentals=0)


def rms_norm(values, scales):
    return values * lax.rsqrt(jnp.mean(values * values, axis=-1, keepdims=True) + epsilon) * scales


def norm_back(values, scales, upstream):
    _, pullback = jax.vjp(rms_norm, values, scales)
    return pullback(upstream)


def geglu(gate_pre, other):
    return jax.nn.gelu(gate_pre, approximate=True) * other


def product(left, right):
    return jnp.dot(left, right, preferred_element_type=f32)


def product_left(left, right):
    return lax.dot_general(left, right, (((0,), (0,)), ((), ())), preferred_element_type=f32)


def product_right(left, right):
    return lax.dot_general(left, right, (((1,), (1,)), ((), ())), preferred_element_type=f32)


def rotary_tables(segments):
    length = segments.shape[0]
    half = HEAD_DIM // 2
    places = jnp.arange(length, dtype=jnp.int32)
    starts = jnp.sum((segments[None, :] < segments[:, None]).astype(jnp.int32), axis=1)
    frequency = jnp.exp(jnp.arange(half, dtype=f32) * (-2.0 * math.log(10000.0) / HEAD_DIM))
    angle = (places - starts).astype(f32)[:, None] * frequency[None, :]
    return jnp.cos(angle), jnp.sin(angle)


def sync(value):
    return lax.optimization_barrier(value)


def core_swap(value):
    return lax.ppermute(value, "mp", [(0, 1), (1, 0), (2, 3), (3, 2)])


def chip_swap(value):
    return lax.ppermute(value, "mp", [(0, 2), (2, 0), (1, 3), (3, 1)])


class Ring:
    def __init__(self):
        self.count = count = lax.axis_size("dp")
        order = [*range(0, count, 2), *reversed(range(1, count, 2))]
        self.ahead = [(order[i], order[(i + 1) % count]) for i in range(count)]
        self.behind = [(b, a) for a, b in self.ahead]
        me = lax.axis_index("dp")
        self.place = jnp.where(me % 2 == 0, me // 2, count - 1 - me // 2)
        self.unrolled = count <= 8

    def member(self, offset):
        place = (self.place + offset) % self.count
        return jnp.where(place < self.count // 2, 2 * place, 2 * (self.count - 1 - place) + 1)

    def up(self, value):
        return lax.ppermute(value, "dp", self.ahead)

    def down(self, value):
        return lax.ppermute(value, "dp", self.behind)

    def gather(self, block):
        return Gather(self, block)

    def reduce(self, whole):
        whole = sync(whole)
        return Reduce(self, slices, (whole,), lambda: whole)


class Gather:
    def __init__(self, ring, block):
        self.ring, self.size, self.hop = ring, block.shape[0], 0
        self.left = self.right = block
        self.came, self.source = [(block,)], ()
        self.hops = ring.count // 2 if ring.unrolled else 1
        if ring.unrolled:
            whole = jnp.zeros((self.size * ring.count, block.shape[1]), block.dtype)
            self.whole = self.put(whole, block, 0)

    def put(self, whole, piece, offset, inner=0):
        start = self.ring.member(offset) * self.size + inner
        return lax.dynamic_update_slice(whole, piece, (start, 0))

    def ended(self):
        return self.hop == self.hops

    def step(self):
        if not self.ring.unrolled:
            self.hop += 1
            return lax.all_gather(self.left, "dp", axis=0, tiled=True)
        self.hop += 1
        left, right = self.left, self.right
        if self.hop == self.hops:
            half = self.size // 32 * 16
            left, right = left[:half], right[half:]
        return self.ring.up(left), self.ring.down(right)

    def upcoming(self):
        return ()

    def accept(self, pieces, later=()):
        if not self.ring.unrolled:
            self.whole = pieces
            return
        self.left, self.right = pieces
        self.came.append(pieces)
        inner = self.left.shape[0] if self.hop == self.hops else 0
        self.whole = self.put(self.whole, self.left, -self.hop)
        self.whole = self.put(self.whole, self.right, self.hop, inner)


def hop_kernel(ahead_ref, behind_ref, left_ref, right_ref, up_ref, down_ref):
    size, some = ahead_ref.shape[0], left_ref.shape[0]
    up_ref[:some] = (ahead_ref[:some].astype(f32) + left_ref[...].astype(f32)).astype(bf16)
    if some < size:
        up_ref[some:] = ahead_ref[some:]
    rest = size - right_ref.shape[0]
    down_ref[rest:] = (behind_ref[rest:].astype(f32) + right_ref[...].astype(f32)).astype(bf16)
    if rest:
        down_ref[:rest] = behind_ref[:rest]


def slices(ring, whole, offsets):
    size = whole.shape[0] // ring.count
    return tuple(
        lax.dynamic_slice_in_dim(whole, ring.member(o) * size, size, 0) for o in offsets
    )


class Reduce:
    def __init__(self, ring, share, source, whole=None, far=None):
        self.ring, self.share, self.source = ring, share, source
        self.hop = self.hops = ring.count // 2 if ring.unrolled else 1
        if not ring.unrolled:
            self.whole, self.far = whole(), ()
        elif far is None:
            (self.far,) = share(ring, *source, (self.hops,))
        else:
            self.far = far

    def ended(self):
        return self.hop == 0

    def step(self):
        if not self.ring.unrolled:
            return lax.psum_scatter(self.whole, "dp", scatter_dimension=0, tiled=True)
        if self.hop == self.hops:
            half = self.far.shape[0] // 32 * 16
            left, right = self.far[:half], self.far[half:]
        else:
            size, width = self.next[0].shape
            step = math.gcd(width, 1024)
            inputs = (*self.next, self.left, self.right)
            left, right = tiled_call(
                hop_kernel,
                [jax.ShapeDtypeStruct((size, width), bf16)] * 2,
                inputs,
                [pl.BlockSpec((p.shape[0], step), lambda i: (0, i)) for p in inputs],
                [pl.BlockSpec((size, step), lambda i: (0, i))] * 2,
                width // step,
            )
        return self.ring.up(left), self.ring.down(right)

    def upcoming(self):
        if not self.ring.unrolled:
            return ()
        later = self.hop - 1
        return self.share(self.ring, *self.source, (later, -later) if later else (0,))

    def accept(self, pieces, later=()):
        self.hop -= 1
        self.next = later
        if not self.ring.unrolled:
            self.left = pieces
        else:
            self.left, self.right = pieces

    def total(self):
        while self.hop > 0:
            pieces = self.step()
            self.accept(pieces, self.upcoming())
        if not self.ring.unrolled:
            return self.left.astype(f32)
        return self.next[0].astype(f32) + self.left.astype(f32) + self.right.astype(f32)


def phase(rings, *values):
    rings = [r for r in rings if not r.ended()]
    pieces, later, sources, values = sync(
        ([r.step() for r in rings], [r.upcoming() for r in rings], [r.source for r in rings], values)
    )
    for r, p, n, source in zip(rings, pieces, later, sources):
        r.accept(p, n)
        r.source = source
    return values[0] if len(values) == 1 else values


def join(mine, other, swapped, axis):
    return jnp.where(
        swapped,
        jnp.concatenate([other, mine], axis=axis),
        jnp.concatenate([mine, other], axis=axis),
    )


def gather_chip(piece, axis):
    me = lax.axis_index("mp")
    piece = join(piece, core_swap(piece), me % 2 == 1, axis)
    return join(piece, chip_swap(piece), me // 2 == 1, axis)


def gather_small(piece, axis):
    count = lax.axis_size("dp")
    me = lax.axis_index("dp")
    step = 1
    while step < count:
        other = lax.ppermute(piece, "dp", [(i, i ^ step) for i in range(count)])
        piece = join(piece, other, (me // step) % 2 == 1, axis)
        step *= 2
    return piece


def sum_chip(value):
    value = value + core_swap(value)
    return value + chip_swap(value)


def sum_step(value, step):
    count = lax.axis_size("dp")
    if step >= count:
        return value
    return value + lax.ppermute(value, "dp", [(i, i ^ step) for i in range(count)])


def stack_kernel(*refs):
    *pieces, out_ref = refs
    rows = pieces[0].shape[0]
    for i, piece in enumerate(pieces):
        out_ref[i * rows : (i + 1) * rows] = piece[...]


def stack(*pieces):
    rows, width = pieces[0].shape
    step = width // 2
    return pl.pallas_call(
        stack_kernel,
        out_shape=jax.ShapeDtypeStruct((rows * len(pieces), width), pieces[0].dtype),
        grid=(2,),
        in_specs=[pl.BlockSpec((rows, step), lambda i: (0, i))] * len(pieces),
        out_specs=pl.BlockSpec((rows * len(pieces), step), lambda i: (0, i)),
        compiler_params=pltpu.CompilerParams(vmem_limit_bytes=24 * 2**20),
        cost_estimate=light,
    )(*pieces)


def gather_slots(piece):
    near = core_swap(piece)
    across = chip_swap(piece)
    return stack(piece, near, across, core_swap(across))


def top(value):
    return value[: value.shape[0] // 2]


def bottom(value):
    return value[value.shape[0] // 2 :]


def add_core(value):
    return top(value) + core_swap(bottom(value).astype(bf16))


def cross(far):
    return chip_swap(add_core(far).astype(bf16))


def rows_of(value, i, pieces):
    width = value.shape[0] // pieces
    return value[i * width : (i + 1) * width]


def normalize(raw):
    return raw * lax.rsqrt(jnp.mean(raw * raw, axis=-1, keepdims=True) + epsilon)


def turn(values, cosine, sine):
    half = HEAD_DIM // 2
    first, second = values[:, :half], values[:, half:]
    return jnp.concatenate(
        [first * cosine - second * sine, second * cosine + first * sine], axis=1
    )


def dot(left, right, dims):
    return lax.dot_general(left, right, ((dims[:1], dims[1:]), ((), ())), preferred_element_type=f32)


TILE = 256


def tiles(length):
    return [(i, max(0, i - WINDOW)) for i in range(0, length, TILE)]


def tile_probs(query, key, start, first, rows_ref, cols_ref):
    stop = start + TILE
    scores = dot(query, key, (1, 1)) * HEAD_DIM**-0.5
    row = start + lax.broadcasted_iota(jnp.int32, scores.shape, 0)
    col = first + lax.broadcasted_iota(jnp.int32, scores.shape, 1)
    kept = (col <= row) & (row - col < WINDOW)
    kept &= rows_ref[start:stop, :] == cols_ref[:, first:stop]
    scores = jnp.where(kept, scores, masked_score)
    expo = jnp.exp(scores - jnp.max(scores, axis=-1, keepdims=True))
    return expo / jnp.sum(expo, axis=-1, keepdims=True)


def slot_at(mine_ref, start):
    return pl.ds(pl.multiple_of((mine_ref[0] ^ (start // TILE)) * TILE, TILE), TILE)


def forward_kernel(
    mine_ref, raw_ref, cos_ref, sin_ref, rows_ref, cols_ref, gain_ref, out_ref, low_ref
):
    length, across = raw_ref.shape
    heads = across // HEAD_DIM - 2
    key_at, value_at = heads * HEAD_DIM, (heads + 1) * HEAD_DIM
    for start in range(0, length, TILE):
        at, here = slice(start, start + TILE), slot_at(mine_ref, start)
        for head in range(heads + 1):
            cols = slice(head * HEAD_DIM, (head + 1) * HEAD_DIM)
            gain = gain_ref[int(head == heads) : int(head == heads) + 1, :]
            turned = turn(normalize(raw_ref[here, cols]) * gain, cos_ref[at, :], sin_ref[at, :])
            low_ref[at, cols] = turned.astype(bf16)
        low_ref[at, value_at:] = normalize(raw_ref[here, value_at:]).astype(bf16)
    for start, first in tiles(length):
        stop = start + TILE
        key = low_ref[first:stop, key_at:value_at]
        value = low_ref[first:stop, value_at:]
        for head in range(heads):
            cols = slice(head * HEAD_DIM, (head + 1) * HEAD_DIM)
            probs = tile_probs(low_ref[start:stop, cols], key, start, first, rows_ref, cols_ref)
            attended = dot(probs.astype(bf16), value, (1, 0))
            out_ref[slot_at(mine_ref, start), cols] = attended.astype(bf16)


def norm_grad(raw, gain, upstream):
    scale = lax.rsqrt(jnp.mean(raw * raw, axis=-1, keepdims=True) + epsilon)
    unit = raw * scale
    inner = upstream * gain
    grad = scale * (inner - unit * jnp.mean(inner * unit, axis=-1, keepdims=True))
    return grad, jnp.sum(upstream * unit, axis=0, keepdims=True)


def backward_kernel(
    mine_ref, raw_ref, low_ref, up_ref, cos_ref, sin_ref, rows_ref, cols_ref, gain_ref, out_ref,
    gain_out_ref, key_sum, value_sum,
):
    length, across = raw_ref.shape
    heads = across // HEAD_DIM - 2
    key_at, value_at = heads * HEAD_DIM, (heads + 1) * HEAD_DIM
    scale = HEAD_DIM**-0.5
    key_sum[...] = jnp.zeros_like(key_sum)
    value_sum[...] = jnp.zeros_like(value_sum)
    query_gain = jnp.zeros((1, HEAD_DIM), f32)
    key_gain = jnp.zeros((1, HEAD_DIM), f32)
    for start, first in tiles(length):
        stop = start + TILE
        at, here = slice(start, stop), slot_at(mine_ref, start)
        key = low_ref[first:stop, key_at:value_at]
        value = low_ref[first:stop, value_at:]
        for head in range(heads):
            cols = slice(head * HEAD_DIM, (head + 1) * HEAD_DIM)
            query = low_ref[at, cols]
            upstream = up_ref[here, cols]
            probs = tile_probs(query, key, start, first, rows_ref, cols_ref)
            grad_probs = dot(upstream, value, (1, 1))
            inner = jnp.sum(probs * grad_probs, axis=-1, keepdims=True)
            grad_scores = (probs * (grad_probs - inner)).astype(bf16)
            value_sum[first:stop, :] += dot(probs.astype(bf16), upstream, (0, 0))
            key_sum[first:stop, :] += dot(grad_scores, query, (0, 0)) * scale
            grad_query = dot(grad_scores, key, (1, 0)) * scale
            grad_query = turn(grad_query, cos_ref[at, :], -sin_ref[at, :])
            grad, gain = norm_grad(raw_ref[here, cols], gain_ref[0:1, :], grad_query)
            out_ref[here, cols] = grad.astype(bf16)
            query_gain += gain
    for start in range(0, length, TILE):
        at, here = slice(start, start + TILE), slot_at(mine_ref, start)
        grad_key = turn(key_sum[at, :], cos_ref[at, :], -sin_ref[at, :])
        grad, gain = norm_grad(raw_ref[here, key_at:value_at], gain_ref[1:2, :], grad_key)
        out_ref[here, key_at:value_at] = grad.astype(bf16)
        key_gain += gain
        grad, _ = norm_grad(raw_ref[here, value_at:], 1.0, value_sum[at, :])
        out_ref[here, value_at:] = grad.astype(bf16)
    gain_out_ref[...] = jnp.concatenate([query_gain, key_gain])


def local_call(kernel, out_shape, inputs, scratch=()):
    vmem = pl.BlockSpec(memory_space=pltpu.VMEM)
    return pl.pallas_call(
        kernel,
        out_shape=out_shape,
        in_specs=[pl.BlockSpec(memory_space=pltpu.SMEM)] + [vmem] * (len(inputs) - 1),
        out_specs=[vmem] * len(out_shape),
        scratch_shapes=list(scratch),
        compiler_params=pltpu.CompilerParams(vmem_limit_bytes=40 * 2**20),
        cost_estimate=light,
    )(*inputs)


def attention(mine, raw, cosine, sine, segments, head_scales):
    length, across = raw.shape
    tables = (cosine, sine, segments[:, None], segments[None, :], head_scales)
    heads = across // HEAD_DIM - 2
    return local_call(
        forward_kernel,
        [
            jax.ShapeDtypeStruct((length, heads * HEAD_DIM), bf16),
            jax.ShapeDtypeStruct((length, across), bf16),
        ],
        (mine, raw, *tables),
    )


def attention_back(mine, raw, low, upstream, cosine, sine, segments, head_scales):
    length, across = raw.shape
    tables = (cosine, sine, segments[:, None], segments[None, :], head_scales)
    return local_call(
        backward_kernel,
        [jax.ShapeDtypeStruct((length, across), bf16), jax.ShapeDtypeStruct((2, HEAD_DIM), f32)],
        (mine, raw, low, upstream, *tables),
        [pltpu.VMEM((length, HEAD_DIM), f32)] * 2,
    )


gelu_scale = math.sqrt(2.0 / math.pi)


def feed_forward_kernel(x_ref, gate_ref, up_ref, gate_pre_ref, up_pre_ref, hidden_ref):
    x = x_ref[...]
    gate_pre = dot(x, gate_ref[...].reshape(-1, TILE), (1, 0))
    up_pre = dot(x, up_ref[...].reshape(-1, TILE), (1, 0))
    gate_pre_ref[...] = gate_pre
    up_pre_ref[...] = up_pre
    bend = jnp.tanh(gelu_scale * (gate_pre + 0.044715 * gate_pre**3))
    hidden_ref[...] = (0.5 * gate_pre * (1.0 + bend) * up_pre).astype(bf16)


def feed_forward_back_kernel(grad_ref, down_ref, gate_ref, up_ref, grad_gate_ref, grad_up_ref):
    grad = dot(grad_ref[...], down_ref[...], (1, 0))
    gate = gate_ref[...]
    bend = jnp.tanh(gelu_scale * (gate + 0.044715 * gate**3))
    slope = gelu_scale * (1.0 + 3.0 * 0.044715 * gate * gate)
    grad_up_ref[...] = (grad * (0.5 * gate * (1.0 + bend))).astype(bf16)
    slope = 0.5 * (1.0 + bend) + 0.5 * gate * (1.0 - bend * bend) * slope
    grad_gate_ref[...] = (grad * up_ref[...] * slope).astype(bf16)


def grad_in_kernel(grad_gate_ref, grad_up_ref, pair_ref, out_ref):
    rows = pair_ref.shape[0] // 2
    out_ref[...] = dot(grad_gate_ref[...], pair_ref[:rows], (1, 1)) + dot(
        grad_up_ref[...], pair_ref[rows:], (1, 1)
    )


def tiled_call(kernel, outs, inputs, specs, out_specs, steps):
    return pl.pallas_call(
        kernel,
        out_shape=outs,
        grid=(steps,),
        in_specs=specs,
        out_specs=out_specs,
        compiler_params=pltpu.CompilerParams(vmem_limit_bytes=48 * 2**20),
        cost_estimate=light,
    )(*inputs)


def column_tile(rows):
    return pl.BlockSpec((rows, TILE), lambda i: (0, i))


def feed_forward(x, pair, part, before=()):
    tokens, width = x.shape
    units = pair.shape[1]
    steps = units // TILE // 2
    size = width // lax.axis_size("dp")
    pair = pair.reshape(-1, 2, size, units)
    wide = jax.ShapeDtypeStruct((tokens, units), f32)

    def weight(which):
        return pl.BlockSpec(
            (width // size, None, size, TILE), lambda i: (0, which, 0, i + part * steps)
        )

    def tile(rows):
        return pl.BlockSpec((rows, TILE), lambda i: (0, i + part * steps))

    def kernel(*refs):
        feed_forward_kernel(*refs[:3], *refs[-3:])

    return pl.pallas_call(
        kernel,
        out_shape=[wide, wide, jax.ShapeDtypeStruct((tokens, units), bf16)],
        grid=(steps,),
        in_specs=[
            pl.BlockSpec((tokens, width), lambda i: (0, 0)),
            weight(0),
            weight(1),
            *[pl.BlockSpec(memory_space=pl.ANY)] * len(before),
        ],
        out_specs=[tile(tokens)] * 3,
        input_output_aliases={3 + i: i for i in range(len(before))},
        compiler_params=pltpu.CompilerParams(vmem_limit_bytes=48 * 2**20),
        cost_estimate=light,
    )(x, pair, pair, *before)


def pair_grad_kernel(left_ref, gate_ref, up_ref, out_ref):
    left = left_ref[...]
    rows = left.shape[1]
    out_ref[:rows] = dot(left, gate_ref[...], (0, 0)).astype(bf16)
    out_ref[rows:] = dot(left, up_ref[...], (0, 0)).astype(bf16)


def pair_grad(left, grad_gate, grad_up):
    tokens, width = left.shape
    units = grad_gate.shape[1]
    size = width // lax.axis_size("dp")
    tile = max(size, 128)
    whole = pl.BlockSpec((tokens, units), lambda i: (0, 0))
    out = tiled_call(
        pair_grad_kernel,
        [jax.ShapeDtypeStruct((2 * width, units), bf16)],
        (left, grad_gate, grad_up),
        [pl.BlockSpec((tokens, tile), lambda i: (0, i)), whole, whole],
        [pl.BlockSpec((2 * tile, units), lambda i: (i, 0))],
        width // tile,
    )[0]
    if tile == size:
        return out
    out = out.reshape(width // tile, 2, tile // size, size, units)
    return out.transpose(0, 2, 1, 3, 4).reshape(2 * width, units)


def pair_share_kernel(members_ref, *refs):
    number = (len(refs) - 2) // 2
    gate_ref, up_ref = refs[number : number + 2]
    for left_ref, out_ref in zip(refs[:number], refs[number + 2 :]):
        left = left_ref[...]
        rows = left.shape[1]
        out_ref[:rows] = dot(left, gate_ref[...], (0, 0)).astype(bf16)
        out_ref[rows:] = dot(left, up_ref[...], (0, 0)).astype(bf16)


def pair_share(ring, left, grad_gate, grad_up, offsets):
    tokens, width = left.shape
    units = grad_gate.shape[1]
    size = width // ring.count
    step = units // 2

    def own(k):
        return pl.BlockSpec((tokens, size), lambda j, at: (0, at[k]))

    grads = pl.BlockSpec((tokens, step), lambda j, at: (0, j))
    number = len(offsets)
    return tuple(
        pl.pallas_call(
            pair_share_kernel,
            out_shape=[jax.ShapeDtypeStruct((2 * size, units), bf16)] * number,
            grid_spec=pltpu.PrefetchScalarGridSpec(
                num_scalar_prefetch=1,
                grid=(2,),
                in_specs=[*map(own, range(number)), grads, grads],
                out_specs=[pl.BlockSpec((2 * size, step), lambda j, at: (0, j))] * number,
            ),
            compiler_params=pltpu.CompilerParams(vmem_limit_bytes=40 * 2**20),
            cost_estimate=light,
        )(
            jnp.stack([ring.member(o) for o in offsets]).astype(jnp.int32),
            *[left] * number,
            grad_gate,
            grad_up,
        )
    )


def feed_forward_back(grad, down_t, gate_pre, up_pre, far, before=()):
    half, width = grad.shape
    units = down_t.shape[1]

    def kernel(*refs):
        feed_forward_back_kernel(*refs[:4], *refs[-2:])

    return pl.pallas_call(
        kernel,
        out_shape=[jax.ShapeDtypeStruct((2 * half, units), bf16)] * 2,
        grid=(units // TILE,),
        in_specs=[
            pl.BlockSpec((half, width), lambda i: (0, 0)),
            column_tile(width),
            *[pl.BlockSpec((half, TILE), lambda i: (far, i))] * 2,
            *[pl.BlockSpec(memory_space=pl.ANY)] * len(before),
        ],
        out_specs=[pl.BlockSpec((half, TILE), lambda i: (far, i))] * 2,
        input_output_aliases={4 + i: i for i in range(len(before))},
        compiler_params=pltpu.CompilerParams(vmem_limit_bytes=48 * 2**20),
        cost_estimate=light,
    )(grad, down_t, gate_pre, up_pre, *before)


def grad_in(grad_gate, grad_up, pair, far):
    tokens, units = grad_gate.shape
    half, width = tokens // 2, pair.shape[0] // 2
    size = width // lax.axis_size("dp")
    tile = max(size, 128)
    if tile > size:
        pair = pair.reshape(width // tile, tile // size, 2, size, units)
        pair = pair.transpose(0, 2, 1, 3, 4).reshape(2 * width, units)
    rows = pl.BlockSpec((half, units), lambda i: (far, 0))
    return tiled_call(
        grad_in_kernel,
        [jax.ShapeDtypeStruct((half, width), f32)],
        (grad_gate, grad_up, pair),
        [rows, rows, pl.BlockSpec((2 * tile, units), lambda i: (i, 0))],
        [pl.BlockSpec((half, tile), lambda i: (0, i))],
        width // tile,
    )[0]


def place_kernel(members_ref, *refs):
    *inputs, out_ref = refs
    place = 0
    for near, far in zip(inputs[::2], inputs[1::2]):
        for start in range(0, near.shape[1], TILE):
            cols = slice(start, start + TILE)
            at = pl.ds(pl.multiple_of(members_ref[place] * TILE, TILE), TILE)
            out_ref[:, at] = near[:, cols] + far[:, cols].astype(f32)
            place += 1


def place(members, sums, rows, width):
    return local_call(
        place_kernel, [jax.ShapeDtypeStruct((rows, width), f32)], (members, *sums)
    )[0]


def shards(
    tokens,
    layer_vectors,
    segment_ids,
    cotangent,
    norm_gains,
    head_gains,
    w_query,
    w_key,
    w_value,
    w_out,
    w_left,
    w_right,
    w_gate,
    w_up,
    w_down,
    w_layer_gate,
    w_layer_proj,
):
    ring = Ring()
    count = ring.count
    mine = lax.axis_index("mp")
    chip, core = mine // 2, mine % 2
    rows, width = tokens.shape
    length = segment_ids.shape[0]
    share = w_key.shape[0]
    rank = w_left.shape[1]
    layer_dim = w_layer_gate.shape[1]

    heads_part = head_gains.shape[0]
    def pick(value, index, axis):
        return lax.dynamic_index_in_dim(value, index, axis, keepdims=False)

    def small_core(value):
        value = value.reshape(count, 2, 2, share, -1)
        mine_too = core_swap(pick(value, 1 - core, 2))
        return (pick(value, core, 2).astype(f32) + mine_too).astype(bf16)

    def small_chip(value):
        other = chip_swap(pick(value, 1 - chip, 1))
        return (pick(value, chip, 1).astype(f32) + other).astype(bf16)

    side = HEAD_DIM
    line = w_query.shape[1]
    fold = 2 * rank * share // line
    extra = jnp.concatenate(
        [norm_gains, jnp.pad(head_gains, (0, norm_gains.shape[1] - heads_part))[None]]
    )
    extra = gather_chip(jnp.pad(extra, ((0, 8 - extra.shape[0]), (0, 0))), 1)
    gain_columns = extra.shape[1]
    extra = extra.reshape(-1, line)
    gain_rows = extra.shape[0]
    parts = [
        w_query,
        w_out.T,
        w_key,
        w_value,
        jnp.concatenate([w_layer_gate, w_layer_proj.T], axis=1),
        jnp.concatenate([w_left, w_right.T], axis=1).reshape(fold, line),
        jnp.pad(extra, ((0, 16 - gain_rows), (0, 0))),
    ]
    first = ring.gather(jnp.concatenate(parts))
    pair_block, down_block = stack(w_gate, w_up), w_down.T
    inputs = tokens.astype(f32)
    vectors = layer_vectors.astype(f32)
    tokens_near = phase([first], core_swap(tokens))
    tables = phase([first], *rotary_tables(segment_ids))
    cosine, sine = tables
    tokens_far, pair_block, down_block = phase([first], chip_swap(tokens), pair_block, down_block)
    tokens_last, pair_block = phase([first], core_swap(tokens_far), pair_block)
    both = ring.gather(pair_block)

    whole = first.whole.reshape(count, -1, line)
    starts = [sum(p.shape[0] for p in parts[:i]) for i in range(len(parts) + 1)]
    query_weight, out_t, key_part, value_part, layer_part, rank_part, extra = (
        whole[:, a:b] for a, b in zip(starts[:-1], starts[1:])
    )
    out_t = out_t.reshape(-1, line)

    def head_columns(value, head):
        return lax.dynamic_slice_in_dim(value, head * side, side, 2)

    def kv_of(head):
        return jnp.concatenate(
            [head_columns(key_part, head), head_columns(value_part, head)], axis=2
        )

    small_part = jnp.concatenate(
        [layer_part, rank_part.reshape(count, share, 2 * rank)], axis=2
    )

    def interleave(own, across):
        both = join(own[:, None], across[:, None], chip == 1, 1)[:, :, None]
        other = core_swap(both)
        return join(both, other, core == 1, 2).reshape(count * 4 * share, -1)

    gains = extra[:, :gain_rows].reshape(count, 8, gain_columns).transpose(1, 0, 2)
    gains = gains.reshape(8, width).astype(f32)
    head_scales = gains[6].reshape(-1, norm_gains.shape[1])[:, :heads_part].reshape(2, HEAD_DIM)
    normed = rms_norm(inputs, gains[0])
    normed_low = normed.astype(bf16)
    normed_all = stack(
        normed_low,
        *(
            rms_norm(t.astype(f32), gains[0]).astype(bf16)
            for t in (tokens_near, tokens_far, tokens_last)
        ),
    )
    kv_weight, small_part = sync((chip_swap(kv_of(1 - chip)), small_part))
    qkv_weight = jnp.concatenate(
        [query_weight.reshape(-1, line), interleave(kv_of(chip), kv_weight)], axis=1
    )
    qkv_raw = product(normed_all, qkv_weight)
    here = mine.reshape(1)
    attended_low, qkv_low = attention(
        here, qkv_raw, cosine, sine, segment_ids, head_scales
    )
    half = length // 2
    attn_far = product_right(attended_low[half:], out_t)
    attn_far, attended_low, normed_low, small_all, down_block = phase(
        [both], attn_far, attended_low, normed_low, chip_swap(small_part), down_block
    )
    attn_far, attended_low = sync((add_core(attn_far).astype(bf16), attended_low))
    attn_near = product_right(attended_low[:half], out_t)
    attn = add_core(attn_near) + chip_swap(attn_far)
    small_all = interleave(small_part, small_all)
    layer_gate_weight, layer_proj_weight, left_weight, right_weight = jnp.split(
        small_all, [layer_dim, 2 * layer_dim, 2 * layer_dim + rank], axis=1
    )
    left_low = product(normed_low, left_weight).astype(bf16)
    laurel_pre = product_right(left_low, right_weight)
    after_attn = inputs + rms_norm(attn, gains[1])
    mixed = (after_attn + normed + rms_norm(laurel_pre, gains[2])) * root_half
    ff_in_low = rms_norm(mixed, gains[3]).astype(bf16)
    ff_in_low, mixed, attn, laurel_pre, down_block = phase(
        [both], ff_in_low, mixed, attn, laurel_pre, down_block
    )
    ff_in_near, ff_in_low, mixed = sync((core_swap(ff_in_low), ff_in_low, mixed))
    ff_in_far, down_block = phase([both], chip_swap(ff_in_low), down_block)
    ff_in_all = stack(ff_in_low, ff_in_near, ff_in_far, core_swap(ff_in_far))
    last = ring.gather(down_block)
    ff_in_all = phase([both], ff_in_all)
    pair = both.whole
    forward, ff_in_all = phase([last], feed_forward(ff_in_all, pair, 0), ff_in_all)
    forward, ff_in_all = phase([last], feed_forward(ff_in_all, pair, 1, forward), ff_in_all)
    gate_pre, up_pre, hidden_low = forward
    hidden_near, hidden_far = hidden_low[:half], hidden_low[half:]

    if ring.unrolled:
        early = jnp.concatenate([p for hop in last.came for p in hop])
        early_far, early_near = phase(
            [last], product_right(hidden_far, early), product_right(hidden_near, early)
        )
        early_far, early_near = phase([last], cross(early_far), early_near)
        late = jnp.concatenate([p for hop in last.came[-2:] for p in hop])
        late_far, late_near = sync(
            (cross(product_right(hidden_far, late)), product_right(hidden_near, late))
        )
        offsets = [0]
        for hop in range(1, count // 2):
            offsets += [-hop, hop]
        members = jnp.stack([ring.member(o) for o in [*offsets, count // 2]]).astype(jnp.int32)
        sums = (add_core(early_near), early_far, add_core(late_near), late_far)
        ff_out = place(members, sums, rows, width)
    else:
        late_far = cross(product_right(hidden_far, last.whole))
        ff_out = add_core(product_right(hidden_near, last.whole)) + late_far
    down_t = last.whole
    after_ff = mixed + rms_norm(ff_out, gains[4])
    after_ff_low = after_ff.astype(bf16)
    layer_pre = product(after_ff_low, layer_gate_weight)
    layer_mix_low = geglu(layer_pre, vectors).astype(bf16)
    layer_out = product_right(layer_mix_low, layer_proj_weight)
    result = after_ff + rms_norm(layer_out, gains[5])

    upstream = cotangent.astype(f32)
    grad_layer_out, grad_gain_five = norm_back(layer_out, gains[5], upstream)
    grad_layer_out_low = grad_layer_out.astype(bf16)
    grad_mix = product(grad_layer_out_low, layer_proj_weight)
    _, layer_pull = jax.vjp(geglu, layer_pre, vectors)
    grad_layer_pre, grad_vectors = layer_pull(grad_mix)
    grad_layer_pre_low = grad_layer_pre.astype(bf16)
    grad_after_ff = upstream + product_right(grad_layer_pre_low, layer_gate_weight)
    grad_ff_out, grad_gain_four = norm_back(ff_out, gains[4], grad_after_ff)
    grad_ff_low, layer_mix_low, after_ff_low = sync(
        (grad_ff_out.astype(bf16), layer_mix_low, after_ff_low)
    )
    grad_layer_proj = product_left(grad_layer_out_low, layer_mix_low)
    grad_layer_gate = product_left(after_ff_low, grad_layer_pre_low)
    grad_ff_near = core_swap(grad_ff_low)
    grads_low = feed_forward_back(stack(grad_ff_low, grad_ff_near), down_t, gate_pre, up_pre, 0)
    grad_ff_far, grads_low, grad_ff_near = sync((chip_swap(grad_ff_low), grads_low, grad_ff_near))
    grad_ff_last = core_swap(grad_ff_far)
    grad_ff_all = stack(grad_ff_low, grad_ff_near, grad_ff_far, grad_ff_last)
    block = width // count
    far_columns = lax.dynamic_slice_in_dim(
        grad_ff_all, ring.member(count // 2) * block, block, 1
    )
    far_grad, grad_ff_all = sync(
        (product_left(far_columns, hidden_low).astype(bf16), grad_ff_all)
    )
    down_grad = product_left(grad_ff_all, hidden_low).astype(bf16)
    down_back = Reduce(ring, slices, (down_grad,), lambda: down_grad, far_grad)
    grad_ff_all = phase([down_back], grad_ff_all)
    grads_low = feed_forward_back(grad_ff_all[half:], down_t, gate_pre, up_pre, 1, grads_low)
    ff_in_far, *grads_low = phase([down_back], grad_in(*grads_low, pair, 1), *grads_low)
    both_back = Reduce(
        ring, pair_share, (ff_in_all, *grads_low), lambda: pair_grad(ff_in_all, *grads_low)
    )
    ff_in_far, ff_in_near, both_back.far, both_back.source = phase(
        [down_back],
        cross(ff_in_far),
        grad_in(*grads_low, pair, 0),
        both_back.far,
        both_back.source,
    )
    grad_ff_in = add_core(ff_in_near) + ff_in_far
    grad_mixed_norm, grad_gain_three = norm_back(mixed, gains[3], grad_ff_in)
    grad_branch = (grad_after_ff + grad_mixed_norm) * root_half
    grad_attn, grad_gain_one = norm_back(attn, gains[1], grad_branch)
    grad_attn_low, grad_branch, both_back.source = sync(
        (grad_attn.astype(bf16), grad_branch, both_back.source)
    )
    grad_laurel, grad_gain_two = norm_back(laurel_pre, gains[2], grad_branch)
    grad_laurel_low = grad_laurel.astype(bf16)
    grad_right = product_left(grad_laurel_low, left_low)
    grad_left_low = product(grad_laurel_low, right_weight).astype(bf16)
    grad_left = product_left(normed_low, grad_left_low)
    small_grad = jnp.concatenate(
        [grad_layer_gate, grad_layer_proj, grad_left, grad_right], axis=1
    ).astype(bf16)
    grad_attn_far, grad_attn_near, grad_attn_low, grad_branch, small_grad, grad_left_low = phase(
        [down_back, both_back],
        chip_swap(grad_attn_low),
        core_swap(grad_attn_low),
        grad_attn_low,
        grad_branch,
        small_grad,
        grad_left_low,
    )
    grad_attn_all = stack(grad_attn_low, grad_attn_near, grad_attn_far, core_swap(grad_attn_far))
    grad_attended_low = product(grad_attn_all, out_t).astype(bf16)
    grad_qkv_low, head_grads = attention_back(
        here, qkv_raw, qkv_low, grad_attended_low, cosine, sine, segment_ids, head_scales
    )
    normed_far = product_right(grad_qkv_low[half:], qkv_weight)
    normed_far, grad_qkv_low, grad_attn_all, grad_branch, small_grad = phase(
        [both_back],
        normed_far,
        grad_qkv_low,
        grad_attn_all,
        grad_branch,
        small_core(small_grad),
    )

    normed_far, grad_qkv_low = sync((add_core(normed_far).astype(bf16), grad_qkv_low))
    qkv_grad = product_left(normed_all, grad_qkv_low).astype(bf16)
    out_grad = product_left(grad_attn_all, attended_low).astype(bf16)
    kv_grad = small_core(qkv_grad[:, line:])
    small_grad = small_chip(small_grad)
    second = jnp.concatenate(
        [
            qkv_grad[:, :line].reshape(count, -1, line),
            kv_grad.reshape(count, 2 * share, 2 * side),
            out_grad.reshape(count, -1, line),
            small_grad[:, :, : 2 * layer_dim],
            small_grad[:, :, 2 * layer_dim :].reshape(count, fold, line),
        ],
        axis=1,
    )
    normed_near = product_right(grad_qkv_low[:half], qkv_weight)
    normed_far, normed_near, second, grad_branch = phase(
        [both_back], normed_far, normed_near, second, grad_branch
    )
    normed_far = chip_swap(normed_far)
    second = ring.reduce(second.reshape(-1, line))
    grad_normed_heads = add_core(normed_near) + normed_far
    grad_normed = grad_branch + product_right(grad_left_low, left_weight) + grad_normed_heads
    grad_inputs_norm, grad_gain_zero = norm_back(inputs, gains[0], grad_normed)
    grad_inputs = grad_branch + grad_inputs_norm
    head_grads = head_grads.reshape(-1)
    gain_grads = jnp.stack(
        [
            grad_gain_zero,
            grad_gain_one,
            grad_gain_two,
            grad_gain_three,
            grad_gain_four,
            grad_gain_five,
            jnp.pad(head_grads, (0, width - head_grads.shape[0])),
        ]
    )
    gain_grads, grad_inputs = phase(
        [both_back, second], sum_step(sum_chip(gain_grads), 1), grad_inputs
    )
    both_grad, down_grad, gain_grads = phase(
        [second], both_back.total(), down_back.total().T, sum_step(gain_grads, 2)
    )
    gate_grad, up_grad = jnp.split(both_grad, 2)
    gain_grads = phase([second], sum_step(gain_grads, 4))
    step = 8
    while step < count:
        gain_grads = sum_step(gain_grads, step)
        step *= 2
    device = lax.axis_index("dp") * 4 + mine
    part = norm_gains.shape[1]
    grad_norm_gains = lax.dynamic_slice_in_dim(gain_grads[:6], device * part, part, 1)
    grad_head_gains = lax.dynamic_slice_in_dim(gain_grads[6], device * heads_part, heads_part, 0)

    second = second.total()
    out_rows = width // count
    grad_query_weight, kv_sum, grad_out, grad_layer, grad_rank = jnp.split(
        second,
        [out_rows, out_rows + 2 * share, 2 * out_rows + 2 * share, 2 * out_rows + 3 * share],
    )
    grad_out = grad_out.T
    grad_layer_gate_weight = grad_layer[:, :layer_dim]
    grad_layer_proj_weight = grad_layer[:, layer_dim:].T
    grad_rank = grad_rank.reshape(share, 2 * rank)
    grad_left_weight = grad_rank[:, :rank]
    grad_right_weight = grad_rank[:, rank:].T
    kv_sum = kv_sum.reshape(2, share, 2 * side)
    kv_mine = pick(kv_sum, chip, 0)
    kv_other = chip_swap(pick(kv_sum, 1 - chip, 0).astype(bf16)).astype(f32)
    grad_key_weight = join(kv_mine[:, :side], kv_other[:, :side], chip == 1, 1)
    grad_value_weight = join(kv_mine[:, side:], kv_other[:, side:], chip == 1, 1)
    return (
        result.astype(bf16),
        grad_inputs.astype(bf16),
        grad_vectors.astype(bf16),
        grad_norm_gains,
        grad_head_gains,
        grad_query_weight,
        grad_key_weight,
        grad_value_weight,
        grad_out,
        grad_left_weight,
        grad_right_weight,
        gate_grad,
        up_grad,
        down_grad,
        grad_layer_gate_weight,
        grad_layer_proj_weight,
    )


def solution(mesh):
    both = ("dp", "mp")
    in_specs = (
        P(both, None),
        P(both, None),
        P("dp"),
        P(both, None),
        P(None, both),
        P(both),
        P("dp", "mp"),
        P(both, None),
        P(both, None),
        P("mp", "dp"),
        P(both, None),
        P(None, both),
        P("dp", "mp"),
        P("dp", "mp"),
        P("mp", "dp"),
        P(both, None),
        P(None, both),
    )
    out_specs = (
        P(both, None),
        P(both, None),
        P(both, None),
        P(None, both),
        P(both),
        P("dp", "mp"),
        P(both, None),
        P(both, None),
        P("mp", "dp"),
        P(both, None),
        P(None, both),
        P("dp", "mp"),
        P("dp", "mp"),
        P("mp", "dp"),
        P(both, None),
        P(None, both),
    )
    return jax.shard_map(shards, mesh=mesh, in_specs=in_specs, out_specs=out_specs, check_vma=False)
```

```python
import math

import jax
import jax.numpy as jnp
from jax import lax
from jax.experimental import pallas as pl
from jax.experimental.pallas import tpu as pltpu
from jax.sharding import PartitionSpec as P

HEAD_DIM = 256
WINDOW = 512

epsilon = 1e-06
root_half = 1.0 / math.sqrt(2.0)
masked_score = -1e30
bf16 = jnp.bfloat16
f32 = jnp.float32


light = pl.CostEstimate(flops=1, bytes_accessed=1, transcendentals=0)


def rms_norm(values, scales):
    return values * lax.rsqrt(jnp.mean(values * values, axis=-1, keepdims=True) + epsilon) * scales


def norm_back(values, scales, upstream):
    _, pullback = jax.vjp(rms_norm, values, scales)
    return pullback(upstream)


def geglu(gate_pre, other):
    return jax.nn.gelu(gate_pre, approximate=True) * other


def product(left, right):
    return jnp.dot(left, right, preferred_element_type=f32)


def product_left(left, right):
    return lax.dot_general(left, right, (((0,), (0,)), ((), ())), preferred_element_type=f32)


def product_right(left, right):
    return lax.dot_general(left, right, (((1,), (1,)), ((), ())), preferred_element_type=f32)


def rotary_tables(segments):
    length = segments.shape[0]
    half = HEAD_DIM // 2
    places = jnp.arange(length, dtype=jnp.int32)
    starts = jnp.sum((segments[None, :] < segments[:, None]).astype(jnp.int32), axis=1)
    frequency = jnp.exp(jnp.arange(half, dtype=f32) * (-2.0 * math.log(10000.0) / HEAD_DIM))
    angle = (places - starts).astype(f32)[:, None] * frequency[None, :]
    return jnp.cos(angle), jnp.sin(angle)


def sync(value):
    return lax.optimization_barrier(value)


def core_swap(value):
    return lax.ppermute(value, "mp", [(0, 1), (1, 0), (2, 3), (3, 2)])


def chip_swap(value):
    return lax.ppermute(value, "mp", [(0, 2), (2, 0), (1, 3), (3, 1)])


class Ring:
    def __init__(self):
        self.count = count = lax.axis_size("dp")
        order = [*range(0, count, 2), *reversed(range(1, count, 2))]
        self.ahead = [(order[i], order[(i + 1) % count]) for i in range(count)]
        self.behind = [(b, a) for a, b in self.ahead]
        me = lax.axis_index("dp")
        self.place = jnp.where(me % 2 == 0, me // 2, count - 1 - me // 2)
        self.unrolled = count <= 8

    def member(self, offset):
        place = (self.place + offset) % self.count
        return jnp.where(place < self.count // 2, 2 * place, 2 * (self.count - 1 - place) + 1)

    def up(self, value):
        return lax.ppermute(value, "dp", self.ahead)

    def down(self, value):
        return lax.ppermute(value, "dp", self.behind)

    def gather(self, block):
        return Gather(self, block)

    def reduce(self, whole):
        whole = sync(whole)
        return Reduce(self, slices, (whole,), lambda: whole)


class Gather:
    def __init__(self, ring, block):
        self.ring, self.size, self.hop = ring, block.shape[0], 0
        self.left = self.right = block
        self.came, self.source = [(block,)], ()
        self.hops = ring.count // 2 if ring.unrolled else 1
        if ring.unrolled:
            whole = jnp.zeros((self.size * ring.count, block.shape[1]), block.dtype)
            self.whole = self.put(whole, block, 0)

    def put(self, whole, piece, offset, inner=0):
        start = self.ring.member(offset) * self.size + inner
        return lax.dynamic_update_slice(whole, piece, (start, 0))

    def ended(self):
        return self.hop == self.hops

    def step(self):
        if not self.ring.unrolled:
            self.hop += 1
            return lax.all_gather(self.left, "dp", axis=0, tiled=True)
        self.hop += 1
        left, right = self.left, self.right
        if self.hop == self.hops:
            half = self.size // 32 * 16
            left, right = left[:half], right[half:]
        return self.ring.up(left), self.ring.down(right)

    def upcoming(self):
        return ()

    def accept(self, pieces, later=()):
        if not self.ring.unrolled:
            self.whole = pieces
            return
        self.left, self.right = pieces
        self.came.append(pieces)
        inner = self.left.shape[0] if self.hop == self.hops else 0
        self.whole = self.put(self.whole, self.left, -self.hop)
        self.whole = self.put(self.whole, self.right, self.hop, inner)


def hop_kernel(ahead_ref, behind_ref, left_ref, right_ref, up_ref, down_ref):
    size, some = ahead_ref.shape[0], left_ref.shape[0]
    up_ref[:some] = (ahead_ref[:some].astype(f32) + left_ref[...].astype(f32)).astype(bf16)
    if some < size:
        up_ref[some:] = ahead_ref[some:]
    rest = size - right_ref.shape[0]
    down_ref[rest:] = (behind_ref[rest:].astype(f32) + right_ref[...].astype(f32)).astype(bf16)
    if rest:
        down_ref[:rest] = behind_ref[:rest]


def slices(ring, whole, offsets):
    size = whole.shape[0] // ring.count
    return tuple(
        lax.dynamic_slice_in_dim(whole, ring.member(o) * size, size, 0) for o in offsets
    )


class Reduce:
    def __init__(self, ring, share, source, whole=None, far=None):
        self.ring, self.share, self.source = ring, share, source
        self.hop = self.hops = ring.count // 2 if ring.unrolled else 1
        if not ring.unrolled:
            self.whole, self.far = whole(), ()
        elif far is None:
            (self.far,) = share(ring, *source, (self.hops,))
        else:
            self.far = far

    def ended(self):
        return self.hop == 0

    def step(self):
        if not self.ring.unrolled:
            return lax.psum_scatter(self.whole, "dp", scatter_dimension=0, tiled=True)
        if self.hop == self.hops:
            half = self.far.shape[0] // 32 * 16
            left, right = self.far[:half], self.far[half:]
        else:
            size, width = self.next[0].shape
            step = math.gcd(width, 1024)
            inputs = (*self.next, self.left, self.right)
            left, right = tiled_call(
                hop_kernel,
                [jax.ShapeDtypeStruct((size, width), bf16)] * 2,
                inputs,
                [pl.BlockSpec((p.shape[0], step), lambda i: (0, i)) for p in inputs],
                [pl.BlockSpec((size, step), lambda i: (0, i))] * 2,
                width // step,
            )
        return self.ring.up(left), self.ring.down(right)

    def upcoming(self):
        if not self.ring.unrolled:
            return ()
        later = self.hop - 1
        return self.share(self.ring, *self.source, (later, -later) if later else (0,))

    def accept(self, pieces, later=()):
        self.hop -= 1
        self.next = later
        if not self.ring.unrolled:
            self.left = pieces
        else:
            self.left, self.right = pieces

    def total(self):
        while self.hop > 0:
            pieces = self.step()
            self.accept(pieces, self.upcoming())
        if not self.ring.unrolled:
            return self.left.astype(f32)
        return self.next[0].astype(f32) + self.left.astype(f32) + self.right.astype(f32)


def phase(rings, *values):
    rings = [r for r in rings if not r.ended()]
    pieces, later, sources, values = sync(
        ([r.step() for r in rings], [r.upcoming() for r in rings], [r.source for r in rings], values)
    )
    for r, p, n, source in zip(rings, pieces, later, sources):
        r.accept(p, n)
        r.source = source
    return values[0] if len(values) == 1 else values


def join(mine, other, swapped, axis):
    return jnp.where(
        swapped,
        jnp.concatenate([other, mine], axis=axis),
        jnp.concatenate([mine, other], axis=axis),
    )


def gather_chip(piece, axis):
    me = lax.axis_index("mp")
    piece = join(piece, core_swap(piece), me % 2 == 1, axis)
    return join(piece, chip_swap(piece), me // 2 == 1, axis)


def gather_small(piece, axis):
    count = lax.axis_size("dp")
    me = lax.axis_index("dp")
    step = 1
    while step < count:
        other = lax.ppermute(piece, "dp", [(i, i ^ step) for i in range(count)])
        piece = join(piece, other, (me // step) % 2 == 1, axis)
        step *= 2
    return piece


def sum_chip(value):
    value = value + core_swap(value)
    return value + chip_swap(value)


def sum_step(value, step):
    count = lax.axis_size("dp")
    if step >= count:
        return value
    return value + lax.ppermute(value, "dp", [(i, i ^ step) for i in range(count)])


def stack_kernel(*refs):
    *pieces, out_ref = refs
    rows = pieces[0].shape[0]
    for i, piece in enumerate(pieces):
        out_ref[i * rows : (i + 1) * rows] = piece[...]


def stack(*pieces):
    rows, width = pieces[0].shape
    step = width // 2
    return pl.pallas_call(
        stack_kernel,
        out_shape=jax.ShapeDtypeStruct((rows * len(pieces), width), pieces[0].dtype),
        grid=(2,),
        in_specs=[pl.BlockSpec((rows, step), lambda i: (0, i))] * len(pieces),
        out_specs=pl.BlockSpec((rows * len(pieces), step), lambda i: (0, i)),
        compiler_params=pltpu.CompilerParams(vmem_limit_bytes=24 * 2**20),
        cost_estimate=light,
    )(*pieces)


def gather_slots(piece):
    near = core_swap(piece)
    across = chip_swap(piece)
    return stack(piece, near, across, core_swap(across))


def top(value):
    return value[: value.shape[0] // 2]


def bottom(value):
    return value[value.shape[0] // 2 :]


def add_core(value):
    return top(value) + core_swap(bottom(value).astype(bf16))


def cross(far):
    return chip_swap(add_core(far).astype(bf16))


def rows_of(value, i, pieces):
    width = value.shape[0] // pieces
    return value[i * width : (i + 1) * width]


def normalize(raw):
    return raw * lax.rsqrt(jnp.mean(raw * raw, axis=-1, keepdims=True) + epsilon)


def turn(values, cosine, sine):
    half = HEAD_DIM // 2
    first, second = values[:, :half], values[:, half:]
    return jnp.concatenate(
        [first * cosine - second * sine, second * cosine + first * sine], axis=1
    )


def dot(left, right, dims):
    return lax.dot_general(left, right, ((dims[:1], dims[1:]), ((), ())), preferred_element_type=f32)


TILE = 256


def tiles(length):
    return [(i, max(0, i - WINDOW)) for i in range(0, length, TILE)]


def tile_probs(query, key, start, first, rows_ref, cols_ref):
    stop = start + TILE
    scores = dot(query, key, (1, 1)) * HEAD_DIM**-0.5
    row = start + lax.broadcasted_iota(jnp.int32, scores.shape, 0)
    col = first + lax.broadcasted_iota(jnp.int32, scores.shape, 1)
    kept = (col <= row) & (row - col < WINDOW)
    kept &= rows_ref[start:stop, :] == cols_ref[:, first:stop]
    scores = jnp.where(kept, scores, masked_score)
    expo = jnp.exp(scores - jnp.max(scores, axis=-1, keepdims=True))
    return expo / jnp.sum(expo, axis=-1, keepdims=True)


def slot_at(mine_ref, start):
    return pl.ds(pl.multiple_of((mine_ref[0] ^ (start // TILE)) * TILE, TILE), TILE)


def forward_kernel(
    mine_ref, raw_ref, cos_ref, sin_ref, rows_ref, cols_ref, gain_ref, out_ref, low_ref
):
    length, across = raw_ref.shape
    heads = across // HEAD_DIM - 2
    key_at, value_at = heads * HEAD_DIM, (heads + 1) * HEAD_DIM
    for start in range(0, length, TILE):
        at, here = slice(start, start + TILE), slot_at(mine_ref, start)
        for head in range(heads + 1):
            cols = slice(head * HEAD_DIM, (head + 1) * HEAD_DIM)
            gain = gain_ref[int(head == heads) : int(head == heads) + 1, :]
            turned = turn(normalize(raw_ref[here, cols]) * gain, cos_ref[at, :], sin_ref[at, :])
            low_ref[at, cols] = turned.astype(bf16)
        low_ref[at, value_at:] = normalize(raw_ref[here, value_at:]).astype(bf16)
    for start, first in tiles(length):
        stop = start + TILE
        key = low_ref[first:stop, key_at:value_at]
        value = low_ref[first:stop, value_at:]
        for head in range(heads):
            cols = slice(head * HEAD_DIM, (head + 1) * HEAD_DIM)
            probs = tile_probs(low_ref[start:stop, cols], key, start, first, rows_ref, cols_ref)
            attended = dot(probs.astype(bf16), value, (1, 0))
            out_ref[slot_at(mine_ref, start), cols] = attended.astype(bf16)


def norm_grad(raw, gain, upstream):
    scale = lax.rsqrt(jnp.mean(raw * raw, axis=-1, keepdims=True) + epsilon)
    unit = raw * scale
    inner = upstream * gain
    grad = scale * (inner - unit * jnp.mean(inner * unit, axis=-1, keepdims=True))
    return grad, jnp.sum(upstream * unit, axis=0, keepdims=True)


def backward_kernel(
    mine_ref, raw_ref, low_ref, up_ref, cos_ref, sin_ref, rows_ref, cols_ref, gain_ref, out_ref,
    gain_out_ref, key_sum, value_sum,
):
    length, across = raw_ref.shape
    heads = across // HEAD_DIM - 2
    key_at, value_at = heads * HEAD_DIM, (heads + 1) * HEAD_DIM
    scale = HEAD_DIM**-0.5
    key_sum[...] = jnp.zeros_like(key_sum)
    value_sum[...] = jnp.zeros_like(value_sum)
    query_gain = jnp.zeros((1, HEAD_DIM), f32)
    key_gain = jnp.zeros((1, HEAD_DIM), f32)
    for start, first in tiles(length):
        stop = start + TILE
        at, here = slice(start, stop), slot_at(mine_ref, start)
        key = low_ref[first:stop, key_at:value_at]
        value = low_ref[first:stop, value_at:]
        for head in range(heads):
            cols = slice(head * HEAD_DIM, (head + 1) * HEAD_DIM)
            query = low_ref[at, cols]
            upstream = up_ref[here, cols]
            probs = tile_probs(query, key, start, first, rows_ref, cols_ref)
            grad_probs = dot(upstream, value, (1, 1))
            inner = jnp.sum(probs * grad_probs, axis=-1, keepdims=True)
            grad_scores = (probs * (grad_probs - inner)).astype(bf16)
            value_sum[first:stop, :] += dot(probs.astype(bf16), upstream, (0, 0))
            key_sum[first:stop, :] += dot(grad_scores, query, (0, 0)) * scale
            grad_query = dot(grad_scores, key, (1, 0)) * scale
            grad_query = turn(grad_query, cos_ref[at, :], -sin_ref[at, :])
            grad, gain = norm_grad(raw_ref[here, cols], gain_ref[0:1, :], grad_query)
            out_ref[here, cols] = grad.astype(bf16)
            query_gain += gain
    for start in range(0, length, TILE):
        at, here = slice(start, start + TILE), slot_at(mine_ref, start)
        grad_key = turn(key_sum[at, :], cos_ref[at, :], -sin_ref[at, :])
        grad, gain = norm_grad(raw_ref[here, key_at:value_at], gain_ref[1:2, :], grad_key)
        out_ref[here, key_at:value_at] = grad.astype(bf16)
        key_gain += gain
        grad, _ = norm_grad(raw_ref[here, value_at:], 1.0, value_sum[at, :])
        out_ref[here, value_at:] = grad.astype(bf16)
    gain_out_ref[...] = jnp.concatenate([query_gain, key_gain])


def local_call(kernel, out_shape, inputs, scratch=()):
    vmem = pl.BlockSpec(memory_space=pltpu.VMEM)
    return pl.pallas_call(
        kernel,
        out_shape=out_shape,
        in_specs=[pl.BlockSpec(memory_space=pltpu.SMEM)] + [vmem] * (len(inputs) - 1),
        out_specs=[vmem] * len(out_shape),
        scratch_shapes=list(scratch),
        compiler_params=pltpu.CompilerParams(vmem_limit_bytes=40 * 2**20),
        cost_estimate=light,
    )(*inputs)


def attention(mine, raw, cosine, sine, segments, head_scales):
    length, across = raw.shape
    tables = (cosine, sine, segments[:, None], segments[None, :], head_scales)
    heads = across // HEAD_DIM - 2
    return local_call(
        forward_kernel,
        [
            jax.ShapeDtypeStruct((length, heads * HEAD_DIM), bf16),
            jax.ShapeDtypeStruct((length, across), bf16),
        ],
        (mine, raw, *tables),
    )


def attention_back(mine, raw, low, upstream, cosine, sine, segments, head_scales):
    length, across = raw.shape
    tables = (cosine, sine, segments[:, None], segments[None, :], head_scales)
    return local_call(
        backward_kernel,
        [jax.ShapeDtypeStruct((length, across), bf16), jax.ShapeDtypeStruct((2, HEAD_DIM), f32)],
        (mine, raw, low, upstream, *tables),
        [pltpu.VMEM((length, HEAD_DIM), f32)] * 2,
    )


gelu_scale = math.sqrt(2.0 / math.pi)


def feed_forward_kernel(x_ref, gate_ref, up_ref, gate_pre_ref, up_pre_ref, hidden_ref):
    x = x_ref[...]
    gate_pre = dot(x, gate_ref[...].reshape(-1, TILE), (1, 0))
    up_pre = dot(x, up_ref[...].reshape(-1, TILE), (1, 0))
    gate_pre_ref[...] = gate_pre
    up_pre_ref[...] = up_pre
    bend = jnp.tanh(gelu_scale * (gate_pre + 0.044715 * gate_pre**3))
    hidden_ref[...] = (0.5 * gate_pre * (1.0 + bend) * up_pre).astype(bf16)


def feed_forward_back_kernel(grad_ref, down_ref, gate_ref, up_ref, grad_gate_ref, grad_up_ref):
    grad = dot(grad_ref[...], down_ref[...], (1, 0))
    gate = gate_ref[...]
    bend = jnp.tanh(gelu_scale * (gate + 0.044715 * gate**3))
    slope = gelu_scale * (1.0 + 3.0 * 0.044715 * gate * gate)
    grad_up_ref[...] = (grad * (0.5 * gate * (1.0 + bend))).astype(bf16)
    slope = 0.5 * (1.0 + bend) + 0.5 * gate * (1.0 - bend * bend) * slope
    grad_gate_ref[...] = (grad * up_ref[...] * slope).astype(bf16)


def grad_in_kernel(grad_gate_ref, grad_up_ref, pair_ref, out_ref):
    rows = pair_ref.shape[0] // 2
    out_ref[...] = dot(grad_gate_ref[...], pair_ref[:rows], (1, 1)) + dot(
        grad_up_ref[...], pair_ref[rows:], (1, 1)
    )


def tiled_call(kernel, outs, inputs, specs, out_specs, steps):
    return pl.pallas_call(
        kernel,
        out_shape=outs,
        grid=(steps,),
        in_specs=specs,
        out_specs=out_specs,
        compiler_params=pltpu.CompilerParams(vmem_limit_bytes=48 * 2**20),
        cost_estimate=light,
    )(*inputs)


def column_tile(rows):
    return pl.BlockSpec((rows, TILE), lambda i: (0, i))


def feed_forward(x, pair, part, before=()):
    tokens, width = x.shape
    units = pair.shape[1]
    steps = units // TILE // 2
    size = width // lax.axis_size("dp")
    pair = pair.reshape(-1, 2, size, units)
    wide = jax.ShapeDtypeStruct((tokens, units), f32)

    def weight(which):
        return pl.BlockSpec(
            (width // size, None, size, TILE), lambda i: (0, which, 0, i + part * steps)
        )

    def tile(rows):
        return pl.BlockSpec((rows, TILE), lambda i: (0, i + part * steps))

    def kernel(*refs):
        feed_forward_kernel(*refs[:3], *refs[-3:])

    return pl.pallas_call(
        kernel,
        out_shape=[wide, wide, jax.ShapeDtypeStruct((tokens, units), bf16)],
        grid=(steps,),
        in_specs=[
            pl.BlockSpec((tokens, width), lambda i: (0, 0)),
            weight(0),
            weight(1),
            *[pl.BlockSpec(memory_space=pl.ANY)] * len(before),
        ],
        out_specs=[tile(tokens)] * 3,
        input_output_aliases={3 + i: i for i in range(len(before))},
        compiler_params=pltpu.CompilerParams(vmem_limit_bytes=48 * 2**20),
        cost_estimate=light,
    )(x, pair, pair, *before)


def pair_grad_kernel(left_ref, gate_ref, up_ref, out_ref):
    left = left_ref[...]
    rows = left.shape[1]
    out_ref[:rows] = dot(left, gate_ref[...], (0, 0)).astype(bf16)
    out_ref[rows:] = dot(left, up_ref[...], (0, 0)).astype(bf16)


def pair_grad(left, grad_gate, grad_up):
    tokens, width = left.shape
    units = grad_gate.shape[1]
    size = width // lax.axis_size("dp")
    tile = max(size, 128)
    whole = pl.BlockSpec((tokens, units), lambda i: (0, 0))
    out = tiled_call(
        pair_grad_kernel,
        [jax.ShapeDtypeStruct((2 * width, units), bf16)],
        (left, grad_gate, grad_up),
        [pl.BlockSpec((tokens, tile), lambda i: (0, i)), whole, whole],
        [pl.BlockSpec((2 * tile, units), lambda i: (i, 0))],
        width // tile,
    )[0]
    if tile == size:
        return out
    out = out.reshape(width // tile, 2, tile // size, size, units)
    return out.transpose(0, 2, 1, 3, 4).reshape(2 * width, units)


def pair_share_kernel(members_ref, *refs):
    number = (len(refs) - 2) // 2
    gate_ref, up_ref = refs[number : number + 2]
    for left_ref, out_ref in zip(refs[:number], refs[number + 2 :]):
        left = left_ref[...]
        rows = left.shape[1]
        out_ref[:rows] = dot(left, gate_ref[...], (0, 0)).astype(bf16)
        out_ref[rows:] = dot(left, up_ref[...], (0, 0)).astype(bf16)


def pair_share(ring, left, grad_gate, grad_up, offsets):
    tokens, width = left.shape
    units = grad_gate.shape[1]
    size = width // ring.count
    step = units // 2

    def own(k):
        return pl.BlockSpec((tokens, size), lambda j, at: (0, at[k]))

    grads = pl.BlockSpec((tokens, step), lambda j, at: (0, j))
    number = len(offsets)
    return tuple(
        pl.pallas_call(
            pair_share_kernel,
            out_shape=[jax.ShapeDtypeStruct((2 * size, units), bf16)] * number,
            grid_spec=pltpu.PrefetchScalarGridSpec(
                num_scalar_prefetch=1,
                grid=(2,),
                in_specs=[*map(own, range(number)), grads, grads],
                out_specs=[pl.BlockSpec((2 * size, step), lambda j, at: (0, j))] * number,
            ),
            compiler_params=pltpu.CompilerParams(vmem_limit_bytes=40 * 2**20),
            cost_estimate=light,
        )(
            jnp.stack([ring.member(o) for o in offsets]).astype(jnp.int32),
            *[left] * number,
            grad_gate,
            grad_up,
        )
    )


def feed_forward_back(grad, down_t, gate_pre, up_pre, far, before=()):
    half, width = grad.shape
    units = down_t.shape[1]

    def kernel(*refs):
        feed_forward_back_kernel(*refs[:4], *refs[-2:])

    return pl.pallas_call(
        kernel,
        out_shape=[jax.ShapeDtypeStruct((2 * half, units), bf16)] * 2,
        grid=(units // TILE,),
        in_specs=[
            pl.BlockSpec((half, width), lambda i: (0, 0)),
            column_tile(width),
            *[pl.BlockSpec((half, TILE), lambda i: (far, i))] * 2,
            *[pl.BlockSpec(memory_space=pl.ANY)] * len(before),
        ],
        out_specs=[pl.BlockSpec((half, TILE), lambda i: (far, i))] * 2,
        input_output_aliases={4 + i: i for i in range(len(before))},
        compiler_params=pltpu.CompilerParams(vmem_limit_bytes=48 * 2**20),
        cost_estimate=light,
    )(grad, down_t, gate_pre, up_pre, *before)


def grad_in(grad_gate, grad_up, pair, far):
    tokens, units = grad_gate.shape
    half, width = tokens // 2, pair.shape[0] // 2
    size = width // lax.axis_size("dp")
    tile = max(size, 128)
    if tile > size:
        pair = pair.reshape(width // tile, tile // size, 2, size, units)
        pair = pair.transpose(0, 2, 1, 3, 4).reshape(2 * width, units)
    rows = pl.BlockSpec((half, units), lambda i: (far, 0))
    return tiled_call(
        grad_in_kernel,
        [jax.ShapeDtypeStruct((half, width), f32)],
        (grad_gate, grad_up, pair),
        [rows, rows, pl.BlockSpec((2 * tile, units), lambda i: (i, 0))],
        [pl.BlockSpec((half, tile), lambda i: (0, i))],
        width // tile,
    )[0]


def place_kernel(members_ref, *refs):
    *inputs, out_ref = refs
    place = 0
    for near, far in zip(inputs[::2], inputs[1::2]):
        for start in range(0, near.shape[1], TILE):
            cols = slice(start, start + TILE)
            at = pl.ds(pl.multiple_of(members_ref[place] * TILE, TILE), TILE)
            out_ref[:, at] = near[:, cols] + far[:, cols].astype(f32)
            place += 1


def place(members, sums, rows, width):
    return local_call(
        place_kernel, [jax.ShapeDtypeStruct((rows, width), f32)], (members, *sums)
    )[0]


def shards(
    tokens,
    layer_vectors,
    segment_ids,
    cotangent,
    norm_gains,
    head_gains,
    w_query,
    w_key,
    w_value,
    w_out,
    w_left,
    w_right,
    w_gate,
    w_up,
    w_down,
    w_layer_gate,
    w_layer_proj,
):
    ring = Ring()
    count = ring.count
    mine = lax.axis_index("mp")
    chip, core = mine // 2, mine % 2
    rows, width = tokens.shape
    length = segment_ids.shape[0]
    share = w_key.shape[0]
    rank = w_left.shape[1]
    layer_dim = w_layer_gate.shape[1]

    heads_part = head_gains.shape[0]
    def pick(value, index, axis):
        return lax.dynamic_index_in_dim(value, index, axis, keepdims=False)

    def small_core(value):
        value = value.reshape(count, 2, 2, share, -1)
        mine_too = core_swap(pick(value, 1 - core, 2))
        return (pick(value, core, 2).astype(f32) + mine_too).astype(bf16)

    def small_chip(value):
        other = chip_swap(pick(value, 1 - chip, 1))
        return (pick(value, chip, 1).astype(f32) + other).astype(bf16)

    side = HEAD_DIM
    line = w_query.shape[1]
    fold = 2 * rank * share // line
    extra = jnp.concatenate(
        [norm_gains, jnp.pad(head_gains, (0, norm_gains.shape[1] - heads_part))[None]]
    )
    extra = gather_chip(jnp.pad(extra, ((0, 8 - extra.shape[0]), (0, 0))), 1)
    gain_columns = extra.shape[1]
    extra = extra.reshape(-1, line)
    gain_rows = extra.shape[0]
    parts = [
        w_query,
        w_out.T,
        w_key,
        w_value,
        jnp.concatenate([w_layer_gate, w_layer_proj.T], axis=1),
        jnp.concatenate([w_left, w_right.T], axis=1).reshape(fold, line),
        jnp.pad(extra, ((0, 16 - gain_rows), (0, 0))),
    ]
    first = ring.gather(jnp.concatenate(parts))
    pair_block, down_block = stack(w_gate, w_up), w_down.T
    inputs = tokens.astype(f32)
    vectors = layer_vectors.astype(f32)
    tokens_near = phase([first], core_swap(tokens))
    tables = phase([first], *rotary_tables(segment_ids))
    cosine, sine = tables
    tokens_far, pair_block, down_block = phase([first], chip_swap(tokens), pair_block, down_block)
    tokens_last, pair_block = phase([first], core_swap(tokens_far), pair_block)
    both = ring.gather(pair_block)

    whole = first.whole.reshape(count, -1, line)
    starts = [sum(p.shape[0] for p in parts[:i]) for i in range(len(parts) + 1)]
    query_weight, out_t, key_part, value_part, layer_part, rank_part, extra = (
        whole[:, a:b] for a, b in zip(starts[:-1], starts[1:])
    )
    out_t = out_t.reshape(-1, line)

    def head_columns(value, head):
        return lax.dynamic_slice_in_dim(value, head * side, side, 2)

    def kv_of(head):
        return jnp.concatenate(
            [head_columns(key_part, head), head_columns(value_part, head)], axis=2
        )

    small_part = jnp.concatenate(
        [layer_part, rank_part.reshape(count, share, 2 * rank)], axis=2
    )

    def interleave(own, across):
        both = join(own[:, None], across[:, None], chip == 1, 1)[:, :, None]
        other = core_swap(both)
        return join(both, other, core == 1, 2).reshape(count * 4 * share, -1)

    gains = extra[:, :gain_rows].reshape(count, 8, gain_columns).transpose(1, 0, 2)
    gains = gains.reshape(8, width).astype(f32)
    head_scales = gains[6].reshape(-1, norm_gains.shape[1])[:, :heads_part].reshape(2, HEAD_DIM)
    normed = rms_norm(inputs, gains[0])
    normed_low = normed.astype(bf16)
    normed_all = stack(
        normed_low,
        *(
            rms_norm(t.astype(f32), gains[0]).astype(bf16)
            for t in (tokens_near, tokens_far, tokens_last)
        ),
    )
    kv_weight, small_part = sync((chip_swap(kv_of(1 - chip)), small_part))
    qkv_weight = jnp.concatenate(
        [query_weight.reshape(-1, line), interleave(kv_of(chip), kv_weight)], axis=1
    )
    qkv_raw = product(normed_all, qkv_weight)
    here = mine.reshape(1)
    attended_low, qkv_low = attention(
        here, qkv_raw, cosine, sine, segment_ids, head_scales
    )
    half = length // 2
    attn_far = product_right(attended_low[half:], out_t)
    attn_far, attended_low, normed_low, small_all, down_block = phase(
        [both], attn_far, attended_low, normed_low, chip_swap(small_part), down_block
    )
    attn_far, attended_low = sync((add_core(attn_far).astype(bf16), attended_low))
    attn_near = product_right(attended_low[:half], out_t)
    attn = add_core(attn_near) + chip_swap(attn_far)
    small_all = interleave(small_part, small_all)
    layer_gate_weight, layer_proj_weight, left_weight, right_weight = jnp.split(
        small_all, [layer_dim, 2 * layer_dim, 2 * layer_dim + rank], axis=1
    )
    left_low = product(normed_low, left_weight).astype(bf16)
    laurel_pre = product_right(left_low, right_weight)
    after_attn = inputs + rms_norm(attn, gains[1])
    mixed = (after_attn + normed + rms_norm(laurel_pre, gains[2])) * root_half
    ff_in_low = rms_norm(mixed, gains[3]).astype(bf16)
    ff_in_low, mixed, attn, laurel_pre, down_block = phase(
        [both], ff_in_low, mixed, attn, laurel_pre, down_block
    )
    ff_in_near, ff_in_low, mixed = sync((core_swap(ff_in_low), ff_in_low, mixed))
    ff_in_far, down_block = phase([both], chip_swap(ff_in_low), down_block)
    ff_in_all = stack(ff_in_low, ff_in_near, ff_in_far, core_swap(ff_in_far))
    last = ring.gather(down_block)
    ff_in_all = phase([both], ff_in_all)
    pair = both.whole
    forward, ff_in_all = phase([last], feed_forward(ff_in_all, pair, 0), ff_in_all)
    forward, ff_in_all = phase([last], feed_forward(ff_in_all, pair, 1, forward), ff_in_all)
    gate_pre, up_pre, hidden_low = forward
    hidden_near, hidden_far = hidden_low[:half], hidden_low[half:]

    if ring.unrolled:
        early = jnp.concatenate([p for hop in last.came for p in hop])
        early_far, early_near = phase(
            [last], product_right(hidden_far, early), product_right(hidden_near, early)
        )
        early_far, early_near = phase([last], cross(early_far), early_near)
        late = jnp.concatenate([p for hop in last.came[-2:] for p in hop])
        late_far, late_near = sync(
            (cross(product_right(hidden_far, late)), product_right(hidden_near, late))
        )
        offsets = [0]
        for hop in range(1, count // 2):
            offsets += [-hop, hop]
        members = jnp.stack([ring.member(o) for o in [*offsets, count // 2]]).astype(jnp.int32)
        sums = (add_core(early_near), early_far, add_core(late_near), late_far)
        ff_out = place(members, sums, rows, width)
    else:
        late_far = cross(product_right(hidden_far, last.whole))
        ff_out = add_core(product_right(hidden_near, last.whole)) + late_far
    down_t = last.whole
    after_ff = mixed + rms_norm(ff_out, gains[4])
    after_ff_low = after_ff.astype(bf16)
    layer_pre = product(after_ff_low, layer_gate_weight)
    layer_mix_low = geglu(layer_pre, vectors).astype(bf16)
    layer_out = product_right(layer_mix_low, layer_proj_weight)
    result = after_ff + rms_norm(layer_out, gains[5])

    upstream = cotangent.astype(f32)
    grad_layer_out, grad_gain_five = norm_back(layer_out, gains[5], upstream)
    grad_layer_out_low = grad_layer_out.astype(bf16)
    grad_mix = product(grad_layer_out_low, layer_proj_weight)
    _, layer_pull = jax.vjp(geglu, layer_pre, vectors)
    grad_layer_pre, grad_vectors = layer_pull(grad_mix)
    grad_layer_pre_low = grad_layer_pre.astype(bf16)
    grad_after_ff = upstream + product_right(grad_layer_pre_low, layer_gate_weight)
    grad_ff_out, grad_gain_four = norm_back(ff_out, gains[4], grad_after_ff)
    grad_ff_low, layer_mix_low, after_ff_low = sync(
        (grad_ff_out.astype(bf16), layer_mix_low, after_ff_low)
    )
    grad_layer_proj = product_left(grad_layer_out_low, layer_mix_low)
    grad_layer_gate = product_left(after_ff_low, grad_layer_pre_low)
    grad_ff_near = core_swap(grad_ff_low)
    grads_low = feed_forward_back(stack(grad_ff_low, grad_ff_near), down_t, gate_pre, up_pre, 0)
    grad_ff_far, grads_low, grad_ff_near = sync((chip_swap(grad_ff_low), grads_low, grad_ff_near))
    grad_ff_last = core_swap(grad_ff_far)
    grad_ff_all = stack(grad_ff_low, grad_ff_near, grad_ff_far, grad_ff_last)
    block = width // count
    far_columns = lax.dynamic_slice_in_dim(
        grad_ff_all, ring.member(count // 2) * block, block, 1
    )
    far_grad, grad_ff_all = sync(
        (product_left(far_columns, hidden_low).astype(bf16), grad_ff_all)
    )
    down_grad = product_left(grad_ff_all, hidden_low).astype(bf16)
    down_back = Reduce(ring, slices, (down_grad,), lambda: down_grad, far_grad)
    grad_ff_all = phase([down_back], grad_ff_all)
    grads_low = feed_forward_back(grad_ff_all[half:], down_t, gate_pre, up_pre, 1, grads_low)
    ff_in_far, *grads_low = phase([down_back], grad_in(*grads_low, pair, 1), *grads_low)
    ff_in_far, ff_in_near, *grads_low = phase(
        [down_back], cross(ff_in_far), grad_in(*grads_low, pair, 0), *grads_low
    )
    both_back = Reduce(
        ring, pair_share, (ff_in_all, *grads_low), lambda: pair_grad(ff_in_all, *grads_low)
    )
    grad_ff_in = add_core(ff_in_near) + ff_in_far
    grad_mixed_norm, grad_gain_three = norm_back(mixed, gains[3], grad_ff_in)
    grad_branch = (grad_after_ff + grad_mixed_norm) * root_half
    grad_attn, grad_gain_one = norm_back(attn, gains[1], grad_branch)
    grad_attn_low, grad_branch, both_back.source = sync(
        (grad_attn.astype(bf16), grad_branch, both_back.source)
    )
    grad_laurel, grad_gain_two = norm_back(laurel_pre, gains[2], grad_branch)
    grad_laurel_low = grad_laurel.astype(bf16)
    grad_right = product_left(grad_laurel_low, left_low)
    grad_left_low = product(grad_laurel_low, right_weight).astype(bf16)
    grad_left = product_left(normed_low, grad_left_low)
    small_grad = jnp.concatenate(
        [grad_layer_gate, grad_layer_proj, grad_left, grad_right], axis=1
    ).astype(bf16)
    grad_attn_far, grad_attn_near, grad_attn_low, grad_branch, small_grad, grad_left_low = phase(
        [down_back, both_back],
        chip_swap(grad_attn_low),
        core_swap(grad_attn_low),
        grad_attn_low,
        grad_branch,
        small_grad,
        grad_left_low,
    )
    grad_attn_all = stack(grad_attn_low, grad_attn_near, grad_attn_far, core_swap(grad_attn_far))
    grad_attended_low = product(grad_attn_all, out_t).astype(bf16)
    grad_qkv_low, head_grads = attention_back(
        here, qkv_raw, qkv_low, grad_attended_low, cosine, sine, segment_ids, head_scales
    )
    normed_far = product_right(grad_qkv_low[half:], qkv_weight)
    normed_far, grad_qkv_low, grad_attn_all, grad_branch, small_grad = phase(
        [both_back],
        normed_far,
        grad_qkv_low,
        grad_attn_all,
        grad_branch,
        small_core(small_grad),
    )

    normed_far, grad_qkv_low = sync((add_core(normed_far).astype(bf16), grad_qkv_low))
    qkv_grad = product_left(normed_all, grad_qkv_low).astype(bf16)
    out_grad = product_left(grad_attn_all, attended_low).astype(bf16)
    kv_grad = small_core(qkv_grad[:, line:])
    small_grad = small_chip(small_grad)
    second = jnp.concatenate(
        [
            qkv_grad[:, :line].reshape(count, -1, line),
            kv_grad.reshape(count, 2 * share, 2 * side),
            out_grad.reshape(count, -1, line),
            small_grad[:, :, : 2 * layer_dim],
            small_grad[:, :, 2 * layer_dim :].reshape(count, fold, line),
        ],
        axis=1,
    )
    normed_near = product_right(grad_qkv_low[:half], qkv_weight)
    normed_far, normed_near, second, grad_branch = phase(
        [both_back], normed_far, normed_near, second, grad_branch
    )
    normed_far = chip_swap(normed_far)
    second = ring.reduce(second.reshape(-1, line))
    grad_normed_heads = add_core(normed_near) + normed_far
    grad_normed = grad_branch + product_right(grad_left_low, left_weight) + grad_normed_heads
    grad_inputs_norm, grad_gain_zero = norm_back(inputs, gains[0], grad_normed)
    grad_inputs = grad_branch + grad_inputs_norm
    head_grads = head_grads.reshape(-1)
    gain_grads = jnp.stack(
        [
            grad_gain_zero,
            grad_gain_one,
            grad_gain_two,
            grad_gain_three,
            grad_gain_four,
            grad_gain_five,
            jnp.pad(head_grads, (0, width - head_grads.shape[0])),
        ]
    )
    gain_grads, grad_inputs = phase(
        [both_back, second], sum_step(sum_chip(gain_grads), 1), grad_inputs
    )
    both_grad, down_grad, gain_grads = phase(
        [second], both_back.total(), down_back.total().T, sum_step(gain_grads, 2)
    )
    gate_grad, up_grad = jnp.split(both_grad, 2)
    gain_grads = phase([second], sum_step(gain_grads, 4))
    step = 8
    while step < count:
        gain_grads = sum_step(gain_grads, step)
        step *= 2
    device = lax.axis_index("dp") * 4 + mine
    part = norm_gains.shape[1]
    grad_norm_gains = lax.dynamic_slice_in_dim(gain_grads[:6], device * part, part, 1)
    grad_head_gains = lax.dynamic_slice_in_dim(gain_grads[6], device * heads_part, heads_part, 0)

    second = second.total()
    out_rows = width // count
    grad_query_weight, kv_sum, grad_out, grad_layer, grad_rank = jnp.split(
        second,
        [out_rows, out_rows + 2 * share, 2 * out_rows + 2 * share, 2 * out_rows + 3 * share],
    )
    grad_out = grad_out.T
    grad_layer_gate_weight = grad_layer[:, :layer_dim]
    grad_layer_proj_weight = grad_layer[:, layer_dim:].T
    grad_rank = grad_rank.reshape(share, 2 * rank)
    grad_left_weight = grad_rank[:, :rank]
    grad_right_weight = grad_rank[:, rank:].T
    kv_sum = kv_sum.reshape(2, share, 2 * side)
    kv_mine = pick(kv_sum, chip, 0)
    kv_other = chip_swap(pick(kv_sum, 1 - chip, 0).astype(bf16)).astype(f32)
    grad_key_weight = join(kv_mine[:, :side], kv_other[:, :side], chip == 1, 1)
    grad_value_weight = join(kv_mine[:, side:], kv_other[:, side:], chip == 1, 1)
    return (
        result.astype(bf16),
        grad_inputs.astype(bf16),
        grad_vectors.astype(bf16),
        grad_norm_gains,
        grad_head_gains,
        grad_query_weight,
        grad_key_weight,
        grad_value_weight,
        grad_out,
        grad_left_weight,
        grad_right_weight,
        gate_grad,
        up_grad,
        down_grad,
        grad_layer_gate_weight,
        grad_layer_proj_weight,
    )


def solution(mesh):
    both = ("dp", "mp")
    in_specs = (
        P(both, None),
        P(both, None),
        P("dp"),
        P(both, None),
        P(None, both),
        P(both),
        P("dp", "mp"),
        P(both, None),
        P(both, None),
        P("mp", "dp"),
        P(both, None),
        P(None, both),
        P("dp", "mp"),
        P("dp", "mp"),
        P("mp", "dp"),
        P(both, None),
        P(None, both),
    )
    out_specs = (
        P(both, None),
        P(both, None),
        P(both, None),
        P(None, both),
        P(both),
        P("dp", "mp"),
        P(both, None),
        P(both, None),
        P("mp", "dp"),
        P(both, None),
        P(None, both),
        P("dp", "mp"),
        P("dp", "mp"),
        P("mp", "dp"),
        P(both, None),
        P(None, both),
    )
    return jax.shard_map(shards, mesh=mesh, in_specs=in_specs, out_specs=out_specs, check_vma=False)
```
